512 devices in a mesh: slab: 64 (over y, x, core), panel: 8 (over z).
Axes of the slice: x: 4, y: 8, z: 8, core: 2. Of those that a mesh axis runs over, the one named last changes fastest.
Arguments:
- vectors: float32 [65536, 1024], P('slab', 'panel'), may hold values from -6 to 6
- hop_table: bfloat16 [8, 256, 256], replicated, may hold values from -0.375 to 0.375
- block_kind: int32 [256, 2], P('slab'), may hold values from 0 to 8
- block_phase: int32 [256], P('slab'), may hold values from 0 to 15
- phase_angles: float32 [16, 256], replicated, may hold values from -3.140625 to 3.140625
- centre: float32 [1], replicated, may hold values from -1 to 1
- half_width: float32 [1], replicated, may hold values from 1.5 to 3
Outputs:
- filtered: float32 [65536, 1024], P('slab', 'panel')
The draws below stay inside these ranges and needn't reach their ends.
Inputs may be any that keep to these rules, and one draw needn't show every extreme that they name: `block_kind`: the value 8 marks a missing block.
All inputs are finite; a program needn't handle non-finite values.
Results may differ from the reference program's by a relative error of at most 0.0059.
Values may be sent and summed in bfloat16 or wider, within the bound.
No kernel may reach another device: no remote copies, remote signals or barrier semaphores. Data moves between devices by JAX's collectives and lax.ppermute only.
A program may use at most 64 MiB of HBM per device.

```python
import jax
import jax.numpy as jnp
from jax import lax

BLK = 256
VEC_DEV = 64
KINDS = 8
PHASES = 16
DEGREE = 2
GS_STEPS = 2
NBLOCKS = 256
SITES = 65536
NVEC = 512
N_PANEL = 8


def plant(result, key, low, largest):
    shape = result.shape
    spot = [jax.random.randint(jax.random.fold_in(key, axis), (), 0, shape[axis]) for axis in range(len(shape))]
    result = result.at[tuple(spot)].set(low)
    longest = shape.index(max(shape))
    spot[longest] = (spot[longest] + 1) % shape[longest]
    return result.at[tuple(spot)].set(largest)


def block_scale(stream_key, dims, split, least, largest):
    level = 1.0
    for axis_at, parts in split:
        draws = jax.random.uniform(jax.random.fold_in(jax.random.fold_in(stream_key, 6), axis_at), (parts,), jnp.float32, least / len(split), largest / len(split))
        level = level * jnp.repeat(jnp.exp(draws), dims[axis_at] // parts).reshape((-1,) + (1,) * (len(dims) - 1 - axis_at))
    return level


def centred(stream_key, extent, deviation, most, cuts=(), kind=jnp.bfloat16):
    values = deviation * jax.random.normal(stream_key, extent, jnp.float32)
    if cuts:
        values = values * block_scale(stream_key, extent, cuts, -0.22, 0.18)
    return jnp.clip(values, -most, most).astype(kind)


def setup_inputs(seed: int = 0) -> dict:
    streams_of = jax.random.split(jax.random.key(seed), 8)
    vectors = centred(streams_of[0], (SITES, 2 * NVEC), 1.0, 6.0, ((0, 64), (1, 8)), jnp.float32)
    hop_table = centred(streams_of[1], (KINDS, BLK, BLK), BLK ** -0.5, 0.375)
    block_kind = plant(jax.random.randint(streams_of[2], (NBLOCKS, 2), 0, KINDS + 1), jax.random.fold_in(streams_of[2], 1), 0, KINDS).astype(jnp.int32)
    block_phase = plant(jax.random.randint(streams_of[3], (NBLOCKS,), 0, PHASES), jax.random.fold_in(streams_of[3], 1), 0, PHASES - 1).astype(jnp.int32)
    phase_angles = jnp.clip(jax.random.uniform(streams_of[4], (PHASES, BLK), jnp.float32, -3.140625, 3.140625), -3.140625, 3.140625)
    centre = jnp.clip(jax.random.uniform(streams_of[5], (1,), jnp.float32, -1.0, 1.0), -1.0, 1.0)
    half_width = jnp.clip(jax.random.uniform(streams_of[6], (1,), jnp.float32, 1.5, 3.0), 1.5, 3.0)
    return dict(vectors=vectors, hop_table=hop_table, block_kind=block_kind, block_phase=block_phase, phase_angles=phase_angles, centre=centre, half_width=half_width)


HIGHEST = lax.Precision.HIGHEST

def complex_inner(left_side, right_side):
    product = jnp.einsum('sa,sb->ab', left_side, right_side, precision=HIGHEST)
    split_at = left_side.shape[1] // 2
    real_part = product[:split_at, :split_at] + product[split_at:, split_at:]
    imag_part = product[:split_at, split_at:] - product[split_at:, :split_at]
    return (real_part, imag_part)

def times_embedded(field_data, real_part, imag_part):
    upper_half = jnp.concatenate([real_part, imag_part], axis=1)
    lower_half = jnp.concatenate([-imag_part, real_part], axis=1)
    return jnp.dot(field_data, jnp.concatenate([upper_half, lower_half], axis=0), precision=HIGHEST)

def cholesky_inverse(gram_real, gram_imag):
    order_size = gram_real.shape[0]
    embedded = jnp.stack([jnp.stack([gram_real, -gram_imag], -1), jnp.stack([gram_imag, gram_real], -1)], 1)
    embedded = embedded.reshape(2 * order_size, 2 * order_size)
    factor = jnp.linalg.cholesky(embedded)
    identity = jnp.eye(2 * order_size, dtype=jnp.float32)
    inverse = jax.scipy.linalg.solve_triangular(factor, identity, lower=True)
    pieces = inverse.reshape(order_size, 2, order_size, 2)
    return (pieces[:, 0, :, 0], pieces[:, 1, :, 0])

def reference(vectors, hop_table, block_kind, block_phase, phase_angles, centre, half_width):
    site_total = vectors.shape[0]
    width_all = 2 * VEC_DEV
    panels = vectors.reshape(site_total, N_PANEL, width_all).transpose(1, 0, 2)
    table_wide = hop_table.astype(jnp.float32)
    sym_table = ((table_wide + jnp.transpose(table_wide, (0, 2, 1))) * 0.5).astype(jnp.bfloat16)
    sym_table = lax.optimization_barrier(sym_table).astype(jnp.float32)
    sym_lookup = jnp.concatenate([sym_table, jnp.zeros((1, BLK, BLK), jnp.float32)], axis=0)
    hop_lookup = jnp.concatenate([table_wide, jnp.zeros((1, BLK, BLK), jnp.float32)], axis=0)
    own_blocks = sym_lookup[block_kind[:, 0]]
    next_blocks = hop_lookup[block_kind[:, 1]]
    angles = phase_angles[block_phase]
    fwd_real = (jnp.cos(angles)[:, :, None] * next_blocks).astype(jnp.bfloat16)
    fwd_imag = (jnp.sin(angles)[:, :, None] * next_blocks).astype(jnp.bfloat16)
    fwd_real, fwd_imag = lax.optimization_barrier((fwd_real, fwd_imag))
    fwd_real = fwd_real.astype(jnp.float32)
    fwd_imag = fwd_imag.astype(jnp.float32)
    zero_block = jnp.zeros((1, BLK, BLK), jnp.float32)
    back_real = jnp.concatenate([zero_block, fwd_real[:-1]], axis=0)
    back_imag = jnp.concatenate([zero_block, fwd_imag[:-1]], axis=0)

    def hop_apply(field_data):
        rounded = lax.optimization_barrier(field_data.astype(jnp.bfloat16)).astype(jnp.float32)
        padded = jnp.pad(rounded, ((BLK, BLK), (0, 0))).reshape(NBLOCKS + 2, BLK, width_all)
        own_part = jnp.einsum('rij,rjc->ric', own_blocks, padded[1:NBLOCKS + 1], precision=HIGHEST)
        ahead = padded[2:]
        behind = padded[:NBLOCKS]
        ahead_a = jnp.einsum('rij,rjc->ric', fwd_real, ahead, precision=HIGHEST)
        ahead_b = jnp.einsum('rij,rjc->ric', fwd_imag, ahead, precision=HIGHEST)
        behind_a = jnp.einsum('rji,rjc->ric', back_real, behind, precision=HIGHEST)
        behind_b = jnp.einsum('rji,rjc->ric', back_imag, behind, precision=HIGHEST)
        real_out = ahead_a[:, :, :VEC_DEV] - ahead_b[:, :, VEC_DEV:] + behind_a[:, :, :VEC_DEV] + behind_b[:, :, VEC_DEV:]
        imag_out = ahead_a[:, :, VEC_DEV:] + ahead_b[:, :, :VEC_DEV] + behind_a[:, :, VEC_DEV:] - behind_b[:, :, :VEC_DEV]
        summed = own_part + jnp.concatenate([real_out, imag_out], axis=2)
        return summed.reshape(site_total, width_all)

    def chebyshev(field_data):
        previous = field_data
        current = (hop_apply(field_data) - centre[0] * field_data) / half_width[0]
        for degree in range(1, DEGREE):
            following = 2.0 * (hop_apply(current) - centre[0] * current) / half_width[0] - previous
            previous, current = (current, following)
        return current
    panels = lax.map(chebyshev, panels)
    panel_ids = jnp.arange(N_PANEL)
    for section_index in range(GS_STEPS):
        source = panels[section_index]
        gram_real, gram_imag = complex_inner(source, source)
        inv_real, inv_imag = cholesky_inverse(gram_real, gram_imag)
        basis = times_embedded(source, inv_real.T, -inv_imag.T)

        def project(panel_data):
            coef_real, coef_imag = complex_inner(basis, panel_data)
            return panel_data - times_embedded(basis, coef_real, coef_imag)
        projected = lax.map(project, panels)
        is_root = panel_ids == section_index
        is_done = panel_ids < section_index
        panels = jnp.where(is_root[:, None, None], basis[None], jnp.where(is_done[:, None, None], panels, projected))
    return panels.transpose(1, 0, 2).reshape(site_total, N_PANEL * width_all)
```

```python
import jax
import jax.numpy as jnp
import numpy as np
from jax import lax
from jax.experimental import pallas as pl
from jax.experimental.pallas import tpu as pltpu
from jax.sharding import Mesh, PartitionSpec as P

HIGHEST = lax.Precision.HIGHEST
F32 = jnp.float32
BF16 = jnp.bfloat16
BLK = 256
WIDE = 128
HALF = 64
META = 16
VM = pltpu.VMEM
SM = pltpu.SMEM


def lane_sign(first):
    lane = lax.broadcasted_iota(jnp.int32, (1, WIDE), 1)
    return jnp.where(lane < HALF, first, -first).astype(F32)


def times_i(packed):
    return lane_sign(-1.0) * pltpu.roll(packed, HALF, 1)


def dot(a, b, **kw):
    return lax.dot_general(a, b, (((1,), (0,)), ((), ())), preferred_element_type=F32, **kw)


def dot_t(a, b, **kw):
    return lax.dot_general(a, b, (((0,), (0,)), ((), ())), preferred_element_type=F32, **kw)


def split(x):
    hi = x.astype(BF16)
    return hi, (x - hi.astype(F32)).astype(BF16)


def filter_kernel(meta, nums, v, left, right, hop, hop_t, sym, cos_t, sin_t, w, w_hi, cosb, sinb, z, y1, y1b):
    centre, inv_h, has_left, has_right = nums[0], nums[1], nums[2], nums[3]
    pick = lax.broadcasted_iota(jnp.int32, (cos_t.shape[1], WIDE), 0) % 16

    def own_kind(r):
        return meta[3 * (r + 2)]

    def next_kind(r):
        return meta[3 * (r + 2) + 1]

    def flag(kind):
        return jnp.where(kind < 8, 1.0, 0.0).astype(F32)

    for r in range(-2, 5):
        hot = jnp.where(pick == meta[3 * (r + 2) + 2], 1.0, 0.0).astype(BF16)
        cosb[r + 2] = dot(cos_t[...], hot)
        sinb[r + 2] = dot(sin_t[...], hot)

    def v_row(r):
        if r < 0:
            return left[(r + 2) * BLK : (r + 3) * BLK, :]
        if r > 3:
            return right[(r - 4) * BLK : (r - 3) * BLK, :]
        return v[r * BLK : (r + 1) * BLK, :].astype(BF16)

    def y_row(r):
        return y1b[r + 1]

    def back_phase(x, r):
        x = x.astype(F32)
        return (cosb[r + 2] * x - sinb[r + 2] * times_i(x)).astype(BF16)

    def hop_row(r, row):
        ko, kn, kb = own_kind(r), next_kind(r), next_kind(r - 1)
        total = flag(ko) * dot(sym[jnp.minimum(ko, 7)], row(r))
        ahead = flag(kn) * dot(hop[jnp.minimum(kn, 7)], row(r + 1))
        total += cosb[r + 2] * ahead + sinb[r + 2] * times_i(ahead)
        return total + flag(kb) * dot(hop_t[jnp.minimum(kb, 7)], z[r + 1])

    for r in range(-2, 4):
        z[r + 2] = back_phase(v_row(r), r)
    for r in range(-1, 5):
        vr = v[r * BLK : (r + 1) * BLK, :] if 0 <= r < 4 else v_row(r).astype(F32)
        y = (hop_row(r, v_row) - centre * vr) * inv_h
        if r == -1:
            y = y * has_left
        if r == 4:
            y = y * has_right
        if 0 <= r < 4:
            y1[r] = y
        y1b[r + 1] = y.astype(BF16)
    for r in range(-1, 4):
        z[r + 2] = back_phase(y_row(r), r)
    for r in range(4):
        y = (2.0 * inv_h) * (hop_row(r, y_row) - centre * y1[r]) - v[r * BLK : (r + 1) * BLK, :]
        w[r * BLK : (r + 1) * BLK, :] = y
        w_hi[r * BLK : (r + 1) * BLK, :] = y.astype(BF16)


def chebyshev(meta, nums, v, left, right, hop, hop_t, sym, cos_t, sin_t):
    spec = pl.BlockSpec(memory_space=VM)
    smem = pl.BlockSpec(memory_space=SM)
    return pl.pallas_call(
        filter_kernel,
        out_shape=(jax.ShapeDtypeStruct(v.shape, F32), jax.ShapeDtypeStruct(v.shape, BF16)),
        in_specs=[smem, smem] + [spec] * 8,
        out_specs=(spec, spec),
        scratch_shapes=[
            VM((7, BLK, WIDE), F32),
            VM((7, BLK, WIDE), F32),
            VM((6, BLK, WIDE), BF16),
            VM((4, BLK, WIDE), F32),
            VM((6, BLK, WIDE), BF16),
        ],
        compiler_params=pltpu.CompilerParams(vmem_limit_bytes=40 << 20),
        name="chebyshev",
    )(meta, nums, v, left, right, hop, hop_t, sym, cos_t, sin_t)


def gram_kernel(w, pq, out):
    rows = w.shape[0]
    p0 = pq[:, 0].reshape(rows, WIDE)
    p1 = pq[:, 1].reshape(rows, WIDE)
    w_hi, w_lo = split(w[...])
    prod = dot_t(jnp.concatenate([p0, p1], 1), jnp.concatenate([p0, p1, w_hi, w_lo], 1))

    def inner(a, b):
        d = prod[a * WIDE : (a + 1) * WIDE, b * WIDE : (b + 1) * WIDE]
        return d[:HALF] + lane_sign(1.0) * pltpu.roll(d[HALF:], HALF, 1)

    out[0:HALF, :] = inner(0, 0)
    out[HALF : 2 * HALF, :] = inner(0, 1)
    out[2 * HALF : 3 * HALF, :] = inner(1, 1)
    out[3 * HALF : 4 * HALF, :] = inner(0, 2) + inner(0, 3)
    out[4 * HALF : 5 * HALF, :] = inner(1, 2) + inner(1, 3)


def gram(w, pq):
    spec = pl.BlockSpec(memory_space=VM)
    return pl.pallas_call(
        gram_kernel,
        out_shape=jax.ShapeDtypeStruct((5 * HALF, WIDE), F32),
        in_specs=[spec, spec],
        out_specs=spec,
        compiler_params=pltpu.CompilerParams(vmem_limit_bytes=32 << 20),
        name="gram",
    )(w, pq)


def inverse_factor(tr, ti):
    tiles = WIDE // 8
    re = [tr[8 * t : 8 * t + 8] for t in range(tiles)]
    im = [ti[8 * t : 8 * t + 8] for t in range(tiles)]
    lane = lax.broadcasted_iota(jnp.int32, (8, WIDE), 1)
    sub = lax.broadcasted_iota(jnp.int32, (8, WIDE), 0)
    for k in range(WIDE):
        g, j = divmod(k, 8)
        at_k = lane == k
        row_r = re[g][j : j + 1]
        row_i = im[g][j : j + 1]
        inv = 1.0 / jnp.broadcast_to(row_r[:, k : k + 1], (1, WIDE))
        row_r = jnp.where(at_k[:1], 1.0, row_r) * inv
        row_i = jnp.where(at_k[:1], 0.0, row_i) * inv
        row_r = jnp.broadcast_to(row_r, (8, WIDE))
        row_i = jnp.broadcast_to(row_i, (8, WIDE))
        for t in range(g, tiles):
            if t == g and j == 7:
                continue
            cr = jnp.broadcast_to(re[t][:, k : k + 1], (8, WIDE))
            ci = jnp.broadcast_to(im[t][:, k : k + 1], (8, WIDE))
            keep_r = jnp.where(at_k, 0.0, re[t])
            keep_i = jnp.where(at_k, 0.0, im[t])
            new_r = keep_r - (cr * row_r - ci * row_i)
            new_i = keep_i - (cr * row_i + ci * row_r)
            if t == g:
                new_r = jnp.where(sub > j, new_r, re[t])
                new_i = jnp.where(sub > j, new_i, im[t])
            re[t], im[t] = new_r, new_i
    out_r, out_i = [], []
    for t in range(tiles):
        diag = lane == sub + 8 * t
        below = lane < sub + 8 * t
        pivot = jnp.sum(jnp.where(diag, re[t], 0.0), axis=1, keepdims=True)
        scale = lax.rsqrt(pivot)
        out_r.append(jnp.where(diag, 1.0, jnp.where(below, re[t], 0.0)) * scale)
        out_i.append(jnp.where(below, im[t], 0.0) * scale)
    return jnp.concatenate(out_r, 0), jnp.concatenate(out_i, 0)


def embed(block):
    return jnp.concatenate([block, times_i(block)], 0)


def finish_kernel(pos, g, w, pq, out):
    rows = w.shape[0]
    lane = lax.broadcasted_iota(jnp.int32, (HALF, WIDE), 1)
    left = lane < HALF
    g00, g01, g11 = g[0:HALF, :], g[HALF : 2 * HALF, :], g[2 * HALF : 3 * HALF, :]
    zero = jnp.zeros((HALF, WIDE), F32)

    up_r = jnp.concatenate(
        [jnp.where(left, g00, pltpu.roll(g01, HALF, 1)), jnp.where(left, 0.0, pltpu.roll(g11, HALF, 1))], 0
    )
    up_i = jnp.concatenate([jnp.where(left, pltpu.roll(g00, HALF, 1), g01), jnp.where(left, 0.0, g11)], 0)
    low = jnp.concatenate([zero, jnp.where(left, 1.0, 0.0)], 0)
    tr = up_r + low * jnp.transpose(up_r)
    ti = up_i - low * jnp.transpose(up_i)
    rr, ri = inverse_factor(tr, ti)
    which = pos[0]

    @pl.when(which >= 2)
    def _():
        m = g[3 * HALF : 5 * HALF, :]
        n = dot(rr, m, precision=HIGHEST) + dot(ri, times_i(m), precision=HIGHEST)
        k = dot_t(rr, n, precision=HIGHEST) - dot_t(ri, times_i(n), precision=HIGHEST)
        e_hi, e_lo = split(jnp.concatenate([embed(k[:HALF]), embed(k[HALF:])], 0))
        p01 = jnp.concatenate([pq[:, 0].reshape(rows, WIDE), pq[:, 1].reshape(rows, WIDE)], 1)
        out[...] = w[...] - (dot(p01, e_hi) + dot(p01, e_lo))

    @pl.when(which < 2)
    def _():
        rt, it = jnp.transpose(rr), jnp.transpose(ri)
        full = lax.broadcasted_iota(jnp.int32, (WIDE, WIDE), 1) < HALF
        first = jnp.where(full, rt, -pltpu.roll(it, HALF, 1))
        second = jnp.where(full, pltpu.roll(rt, HALF, 1), -it)
        is_first = which == 0
        own = jnp.where(is_first, first[:HALF], second[HALF:])
        other = jnp.where(is_first, 0.0, second[:HALF])
        o_hi, o_lo = split(embed(other))
        p0 = pq[:, 0].reshape(rows, WIDE)
        out[...] = dot(w[...], embed(own), precision=HIGHEST) + dot(p0, o_hi) + dot(p0, o_lo)


def finish(pos, g, w, pq):
    spec = pl.BlockSpec(memory_space=VM)
    return pl.pallas_call(
        finish_kernel,
        out_shape=jax.ShapeDtypeStruct(w.shape, F32),
        in_specs=[pl.BlockSpec(memory_space=SM), spec, spec, spec],
        out_specs=spec,
        compiler_params=pltpu.CompilerParams(vmem_limit_bytes=40 << 20),
        name="finish",
    )(pos, g, w, pq)


def swap(x, axes):
    return lax.all_to_all(x, axes, 0, 0, tiled=True)


def copies(x, count):
    return jnp.broadcast_to(x[None], (count,) + x.shape).reshape((count * x.shape[0],) + x.shape[1:])


def sum_pieces(x, count):
    return jnp.sum(x.reshape((count, -1) + x.shape[1:]), axis=0)


def slab_sum(x, inner, outer):
    near, far = lax.axis_size(inner), lax.axis_size(outer)
    piece = sum_pieces(swap(x, inner), near)
    piece = sum_pieces(swap(copies(piece, far), outer), far)
    return swap(copies(piece, near), inner)


def thirds(x):
    a = lax.reduce_precision(x, 8, 7)
    b = lax.reduce_precision(x - a, 8, 7)
    return jnp.concatenate([a, b, x - a - b], axis=0).astype(BF16).T


def body(vectors, hop_table, block_kind, block_phase, phase_angles, centre, half_width):
    slab = ("y", "x", "core")
    count = lax.axis_size(slab)
    me = lax.axis_index(slab)
    rows = vectors.shape[0]
    table = jnp.concatenate([block_kind - 8, block_phase[:, None]], axis=1)

    def packet(part, info):
        extra = jnp.zeros((META, WIDE), F32).at[:2, :3].set(info.astype(F32))
        return jnp.concatenate([part.astype(BF16), extra.astype(BF16)], axis=0)

    up = packet(vectors[rows // 2 :], table[2:])
    down = packet(vectors[: rows // 2], table[:2])
    left = lax.ppermute(up, slab, [(i, i + 1) for i in range(count - 1)])
    right = lax.ppermute(down, slab, [(i + 1, i) for i in range(count - 1)])
    wide = hop_table.astype(F32)
    turned = jnp.transpose(hop_table, (0, 2, 1))
    sym = ((wide + turned.astype(F32)) * 0.5).astype(BF16)
    cos_t = thirds(jnp.cos(phase_angles))
    sin_t = thirds(jnp.sin(phase_angles))

    def info(packed):
        return packed[rows // 2 : rows // 2 + 2, :3].astype(jnp.int32)

    meta = jnp.concatenate([info(left), table, info(right)], axis=0) + jnp.array([8, 8, 0], jnp.int32)
    nums = jnp.stack(
        [centre[0], 1.0 / half_width[0], (me > 0).astype(F32), (me < count - 1).astype(F32)]
    )
    w, w_hi = chebyshev(meta.reshape(-1), nums, vectors, left, right, hop_table, turned, sym, cos_t, sin_t)

    panels = lax.axis_size("panel")
    chunk = rows // panels
    mine = swap(w_hi, "panel")[: 2 * chunk]
    pq = swap(copies(mine, panels), "panel").reshape(panels, 2, chunk, WIDE)
    g = slab_sum(gram(w, pq), ("x", "core"), "y")
    pos = lax.axis_index("panel").astype(jnp.int32).reshape(1)
    return finish(pos, g, w, pq)


def solution(mesh):
    panels = mesh.shape["panel"]
    devices = np.asarray(mesh.devices).reshape(8, 4, 2, panels)
    fine = Mesh(devices, ("y", "x", "core", "panel"))
    slab = ("y", "x", "core")
    in_specs = (P(slab, "panel"), P(), P(slab, None), P(slab), P(), P(), P())
    return jax.shard_map(body, mesh=fine, in_specs=in_specs, out_specs=P(slab, "panel"), check_vma=False)
```

```python
import functools

import jax
import jax.numpy as jnp
import numpy as np
from jax import lax
from jax.experimental import pallas as pl
from jax.experimental.pallas import tpu as pltpu
from jax.sharding import Mesh, PartitionSpec as P

HIGHEST = lax.Precision.HIGHEST
F32 = jnp.float32
BF16 = jnp.bfloat16
BLK = 256
WIDE = 128
HALF = 64
META = 16
STEPS = (
    [(0, 1), (4, 5), (1, 2), (5, 6)],
    [(0, 7), (4, 3), (1, 0), (5, 4)],
    [(0, 6), (4, 2), (1, 3), (5, 7)],
)
HELD = ((0, 1, 3, 2, 0, 1, 3, 2), (2, 0, 1, 3, 2, 0, 1, 3))
VM = pltpu.VMEM
SM = pltpu.SMEM


def lane_sign(first):
    lane = lax.broadcasted_iota(jnp.int32, (1, WIDE), 1)
    return jnp.where(lane < HALF, first, -first).astype(F32)


def times_i(packed):
    return lane_sign(-1.0) * pltpu.roll(packed, HALF, 1)


def dot(a, b, **kw):
    return lax.dot_general(a, b, (((1,), (0,)), ((), ())), preferred_element_type=F32, **kw)


def dot_t(a, b, **kw):
    return lax.dot_general(a, b, (((0,), (0,)), ((), ())), preferred_element_type=F32, **kw)


def split(x):
    hi = x.astype(BF16)
    return hi, (x - hi.astype(F32)).astype(BF16)


def filter_kernel(meta, nums, v, left, right, hop, hop_t, sym, cos_t, sin_t, w, w_hi, cosb, sinb, z, y1, y1b):
    centre, inv_h, has_left, has_right = nums[0], nums[1], nums[2], nums[3]
    pick = lax.broadcasted_iota(jnp.int32, (cos_t.shape[1], WIDE), 0) % 16

    def own_kind(r):
        return meta[3 * (r + 2)]

    def next_kind(r):
        return meta[3 * (r + 2) + 1]

    def flag(kind):
        return jnp.where(kind < 8, 1.0, 0.0).astype(F32)

    for r in range(-2, 5):
        hot = jnp.where(pick == meta[3 * (r + 2) + 2], 1.0, 0.0).astype(BF16)
        cosb[r + 2] = dot(cos_t[...], hot)
        sinb[r + 2] = dot(sin_t[...], hot)

    def v_row(r):
        if r < 0:
            return left[(r + 2) * BLK : (r + 3) * BLK, :]
        if r > 3:
            return right[(r - 4) * BLK : (r - 3) * BLK, :]
        return v[r * BLK : (r + 1) * BLK, :].astype(BF16)

    def y_row(r):
        return y1b[r + 1]

    def back_phase(x, r):
        x = x.astype(F32)
        return (cosb[r + 2] * x - sinb[r + 2] * times_i(x)).astype(BF16)

    def hop_row(r, row):
        ko, kn, kb = own_kind(r), next_kind(r), next_kind(r - 1)
        total = flag(ko) * dot(sym[jnp.minimum(ko, 7)], row(r))
        ahead = flag(kn) * dot(hop[jnp.minimum(kn, 7)], row(r + 1))
        total += cosb[r + 2] * ahead + sinb[r + 2] * times_i(ahead)
        return total + flag(kb) * dot(hop_t[jnp.minimum(kb, 7)], z[r + 1])

    for r in range(-2, 4):
        z[r + 2] = back_phase(v_row(r), r)
    for r in range(-1, 5):
        vr = v[r * BLK : (r + 1) * BLK, :] if 0 <= r < 4 else v_row(r).astype(F32)
        y = (hop_row(r, v_row) - centre * vr) * inv_h
        if r == -1:
            y = y * has_left
        if r == 4:
            y = y * has_right
        if 0 <= r < 4:
            y1[r] = y
        y1b[r + 1] = y.astype(BF16)
    for r in range(-1, 4):
        z[r + 2] = back_phase(y_row(r), r)
    for r in range(4):
        y = (2.0 * inv_h) * (hop_row(r, y_row) - centre * y1[r]) - v[r * BLK : (r + 1) * BLK, :]
        w[r * BLK : (r + 1) * BLK, :] = y
        w_hi[r * BLK : (r + 1) * BLK, :] = y.astype(BF16)


def chebyshev(meta, nums, v, left, right, hop, hop_t, sym, cos_t, sin_t):
    spec = pl.BlockSpec(memory_space=VM)
    smem = pl.BlockSpec(memory_space=SM)
    return pl.pallas_call(
        filter_kernel,
        out_shape=(jax.ShapeDtypeStruct(v.shape, F32), jax.ShapeDtypeStruct(v.shape, BF16)),
        in_specs=[smem, smem] + [spec] * 8,
        out_specs=(spec, spec),
        scratch_shapes=[
            VM((7, BLK, WIDE), F32),
            VM((7, BLK, WIDE), F32),
            VM((6, BLK, WIDE), BF16),
            VM((4, BLK, WIDE), F32),
            VM((6, BLK, WIDE), BF16),
        ],
        compiler_params=pltpu.CompilerParams(vmem_limit_bytes=40 << 20),
        name="chebyshev",
    )(meta, nums, v, left, right, hop, hop_t, sym, cos_t, sin_t)


def gram_kernel(pos, w, own, first, second, third, p01, out):
    which = pos[0]
    for src, ref in enumerate((own, first, second, third)):
        for panel in range(2):
            here = [z for z in range(8) if HELD[panel][z] == src]
            hit = functools.reduce(jnp.logical_or, [which == z for z in here])

            @pl.when(hit)
            def _(ref=ref, panel=panel):
                p01[:, panel * WIDE : (panel + 1) * WIDE] = ref[...]

    both = p01[...]
    w_hi, w_lo = split(w[...])
    prod = dot_t(both, jnp.concatenate([both, w_hi, w_lo], 1))

    def inner(a, b):
        d = prod[a * WIDE : (a + 1) * WIDE, b * WIDE : (b + 1) * WIDE]
        return d[:HALF] + lane_sign(1.0) * pltpu.roll(d[HALF:], HALF, 1)

    row = lax.broadcasted_iota(jnp.int32, (HALF, WIDE), 0)
    lane = lax.broadcasted_iota(jnp.int32, (HALF, WIDE), 1)
    col = jnp.where(lane < HALF, lane, lane - HALF)
    g00, g11 = inner(0, 0), inner(1, 1)
    diag = jnp.where(lane < HALF, g00, pltpu.roll(g11, HALF, 1))
    out[0:HALF, :] = jnp.where(col > row, g00, jnp.where(col < row, g11, diag))
    out[HALF : 2 * HALF, :] = inner(0, 1)
    out[2 * HALF : 3 * HALF, :] = inner(0, 2) + inner(0, 3)
    out[3 * HALF : 4 * HALF, :] = inner(1, 2) + inner(1, 3)


def gram(pos, w, parts):
    spec = pl.BlockSpec(memory_space=VM)
    return pl.pallas_call(
        gram_kernel,
        out_shape=(
            jax.ShapeDtypeStruct((w.shape[0], 2 * WIDE), BF16),
            jax.ShapeDtypeStruct((4 * HALF, WIDE), F32),
        ),
        in_specs=[pl.BlockSpec(memory_space=SM)] + [spec] * 5,
        out_specs=(spec, spec),
        compiler_params=pltpu.CompilerParams(vmem_limit_bytes=32 << 20),
        name="gram",
    )(pos, w, *parts)


def inverse_factor(tr, ti):
    tiles = WIDE // 8
    re = [tr[8 * t : 8 * t + 8] for t in range(tiles)]
    im = [ti[8 * t : 8 * t + 8] for t in range(tiles)]
    lane = lax.broadcasted_iota(jnp.int32, (8, WIDE), 1)
    sub = lax.broadcasted_iota(jnp.int32, (8, WIDE), 0)
    for k in range(WIDE):
        g, j = divmod(k, 8)
        at_k = lane == k
        row_r = re[g][j : j + 1]
        row_i = im[g][j : j + 1]
        inv = 1.0 / jnp.broadcast_to(row_r[:, k : k + 1], (1, WIDE))
        row_r = jnp.where(at_k[:1], 1.0, row_r) * inv
        row_i = jnp.where(at_k[:1], 0.0, row_i) * inv
        row_r = jnp.broadcast_to(row_r, (8, WIDE))
        row_i = jnp.broadcast_to(row_i, (8, WIDE))
        for t in range(g, tiles):
            if t == g and j == 7:
                continue
            cr = jnp.broadcast_to(re[t][:, k : k + 1], (8, WIDE))
            ci = jnp.broadcast_to(im[t][:, k : k + 1], (8, WIDE))
            keep_r = jnp.where(at_k, 0.0, re[t])
            keep_i = jnp.where(at_k, 0.0, im[t])
            new_r = keep_r - (cr * row_r - ci * row_i)
            new_i = keep_i - (cr * row_i + ci * row_r)
            if t == g:
                new_r = jnp.where(sub > j, new_r, re[t])
                new_i = jnp.where(sub > j, new_i, im[t])
            re[t], im[t] = new_r, new_i
    out_r, out_i = [], []
    for t in range(tiles):
        diag = lane == sub + 8 * t
        below = lane < sub + 8 * t
        pivot = jnp.sum(jnp.where(diag, re[t], 0.0), axis=1, keepdims=True)
        scale = lax.rsqrt(pivot)
        out_r.append(jnp.where(diag, 1.0, jnp.where(below, re[t], 0.0)) * scale)
        out_i.append(jnp.where(below, im[t], 0.0) * scale)
    return jnp.concatenate(out_r, 0), jnp.concatenate(out_i, 0)


def embed(block):
    return jnp.concatenate([block, times_i(block)], 0)


def finish_kernel(pos, g, w, p01, out):
    row = lax.broadcasted_iota(jnp.int32, (HALF, WIDE), 0)
    lane = lax.broadcasted_iota(jnp.int32, (HALF, WIDE), 1)
    left = lane < HALF
    col = jnp.where(left, lane, lane - HALF)
    c, g01 = g[0:HALF, :], g[HALF : 2 * HALF, :]
    c_turn, g01_turn = pltpu.roll(c, HALF, 1), pltpu.roll(g01, HALF, 1)
    above, below, diag = col > row, col < row, col == row

    def stack(top_left, top_right, low_right):
        return jnp.concatenate([jnp.where(left, top_left, top_right), jnp.where(left, 0.0, low_right)], 0)

    once_r = stack(jnp.where(above, c, 0.0), g01_turn, jnp.where(below, c_turn, 0.0))
    once_i = stack(jnp.where(above, c_turn, 0.0), g01, jnp.where(below, c, 0.0))
    pivots = jnp.where(diag, c, 0.0)
    tr = once_r + jnp.transpose(once_r) + stack(pivots, 0.0, pivots)
    ti = once_i - jnp.transpose(once_i)
    rr, ri = inverse_factor(tr, ti)
    which = pos[0]

    @pl.when(which >= 2)
    def _():
        m = g[2 * HALF : 4 * HALF, :]
        n = dot(rr, m, precision=HIGHEST) + dot(ri, times_i(m), precision=HIGHEST)
        k = dot_t(rr, n, precision=HIGHEST) - dot_t(ri, times_i(n), precision=HIGHEST)
        e_hi, e_lo = split(jnp.concatenate([embed(k[:HALF]), embed(k[HALF:])], 0))
        out[...] = w[...] - (dot(p01[...], e_hi) + dot(p01[...], e_lo))

    @pl.when(which < 2)
    def _():
        rt, it = jnp.transpose(rr), jnp.transpose(ri)
        full = lax.broadcasted_iota(jnp.int32, (WIDE, WIDE), 1) < HALF
        first = jnp.where(full, rt, -pltpu.roll(it, HALF, 1))
        second = jnp.where(full, pltpu.roll(rt, HALF, 1), -it)
        is_first = which == 0
        own = jnp.where(is_first, first[:HALF], second[HALF:])
        other = jnp.where(is_first, 0.0, second[:HALF])
        o_hi, o_lo = split(embed(other))
        p0 = p01[:, :WIDE]
        out[...] = dot(w[...], embed(own), precision=HIGHEST) + dot(p0, o_hi) + dot(p0, o_lo)


def finish(pos, g, w, p01):
    spec = pl.BlockSpec(memory_space=VM)
    return pl.pallas_call(
        finish_kernel,
        out_shape=jax.ShapeDtypeStruct(w.shape, F32),
        in_specs=[pl.BlockSpec(memory_space=SM), spec, spec, spec],
        out_specs=spec,
        compiler_params=pltpu.CompilerParams(vmem_limit_bytes=40 << 20),
        name="finish",
    )(pos, g, w, p01)


def swap(x, axes):
    return lax.all_to_all(x, axes, 0, 0, tiled=True)


def copies(x, count):
    return jnp.broadcast_to(x[None], (count,) + x.shape).reshape((count * x.shape[0],) + x.shape[1:])


def sum_pieces(x, count):
    return jnp.sum(x.reshape((count, -1) + x.shape[1:]), axis=0)


def slab_sum(x, axes):
    count = lax.axis_size(axes)
    return swap(copies(sum_pieces(swap(x, axes), count), count), axes)


def spread(w_hi, pos):
    far = lax.ppermute(w_hi, "panel", [(0, 4), (1, 5)])
    own = jnp.where(pos >= 4, far, w_hi)
    return (own,) + tuple(lax.ppermute(own, "panel", pairs) for pairs in STEPS)


def thirds(x):
    a = lax.reduce_precision(x, 8, 7)
    b = lax.reduce_precision(x - a, 8, 7)
    return jnp.concatenate([a, b, x - a - b], axis=0).astype(BF16).T


def body(vectors, hop_table, block_kind, block_phase, phase_angles, centre, half_width):
    slab = ("y", "x", "core")
    count = lax.axis_size(slab)
    me = lax.axis_index(slab)
    rows = vectors.shape[0]
    table = jnp.concatenate([block_kind - 8, block_phase[:, None]], axis=1)

    def packet(part, info):
        extra = jnp.zeros((META, WIDE), F32).at[:2, :3].set(info.astype(F32))
        return jnp.concatenate([part.astype(BF16), extra.astype(BF16)], axis=0)

    up = packet(vectors[rows // 2 :], table[2:])
    down = packet(vectors[: rows // 2], table[:2])
    left = lax.ppermute(up, slab, [(i, i + 1) for i in range(count - 1)])
    right = lax.ppermute(down, slab, [(i + 1, i) for i in range(count - 1)])
    wide = hop_table.astype(F32)
    turned = jnp.transpose(hop_table, (0, 2, 1))
    sym = ((wide + turned.astype(F32)) * 0.5).astype(BF16)
    cos_t = thirds(jnp.cos(phase_angles))
    sin_t = thirds(jnp.sin(phase_angles))

    def info(packed):
        return packed[rows // 2 : rows // 2 + 2, :3].astype(jnp.int32)

    meta = jnp.concatenate([info(left), table, info(right)], axis=0) + jnp.array([8, 8, 0], jnp.int32)
    nums = jnp.stack(
        [centre[0], 1.0 / half_width[0], (me > 0).astype(F32), (me < count - 1).astype(F32)]
    )
    w, w_hi = chebyshev(meta.reshape(-1), nums, vectors, left, right, hop_table, turned, sym, cos_t, sin_t)

    pos = lax.axis_index("panel").astype(jnp.int32)
    spot = pos.reshape(1)
    p01, part = gram(spot, w, spread(w_hi, pos))
    return finish(spot, slab_sum(part, slab), w, p01)


def solution(mesh):
    panels = mesh.shape["panel"]
    devices = np.asarray(mesh.devices).reshape(8, 4, 2, panels)
    fine = Mesh(devices, ("y", "x", "core", "panel"))
    slab = ("y", "x", "core")
    in_specs = (P(slab, "panel"), P(), P(slab, None), P(slab), P(), P(), P())
    return jax.shard_map(body, mesh=fine, in_specs=in_specs, out_specs=P(slab, "panel"), check_vma=False)
```

```python
import functools

import jax
import jax.numpy as jnp
import numpy as np
from jax import lax
from jax.experimental import pallas as pl
from jax.experimental.pallas import tpu as pltpu
from jax.sharding import Mesh, PartitionSpec as P

HIGHEST = lax.Precision.HIGHEST
F32 = jnp.float32
BF16 = jnp.bfloat16
BLK = 256
WIDE = 128
HALF = 64
META = 16
MISSING = 8
STEPS = (
    [(0, 1), (3, 4), (1, 2), (6, 7)],
    [(0, 7), (3, 2), (1, 0), (6, 5)],
    [(0, 6), (3, 5), (1, 3), (6, 4)],
)
HELD = ((0, 1, 2, 0, 1, 3, 3, 2), (2, 0, 1, 3, 3, 2, 0, 1))
VM = pltpu.VMEM
SM = pltpu.SMEM


def lane_sign(first):
    lane = lax.broadcasted_iota(jnp.int32, (1, WIDE), 1)
    return jnp.where(lane < HALF, first, -first).astype(F32)


def times_i(packed):
    return lane_sign(-1.0) * pltpu.roll(packed, HALF, 1)


def dot(a, b, **kw):
    return lax.dot_general(a, b, (((1,), (0,)), ((), ())), preferred_element_type=F32, **kw)


def dot_t(a, b, **kw):
    return lax.dot_general(a, b, (((0,), (0,)), ((), ())), preferred_element_type=F32, **kw)


def split(x):
    hi = x.astype(BF16)
    return hi, (x - hi.astype(F32)).astype(BF16)


def pack_kernel(v, kinds, phase, up, down, tile):
    half = v.shape[0] // 2
    down[:half, :] = v[:half, :].astype(BF16)
    up[:half, :] = v[half:, :].astype(BF16)
    tile[...] = jnp.zeros(tile.shape, F32)
    tile[0:2, 0:4] = (kinds[...] - MISSING).astype(F32)
    tile[2:3, 0:4] = phase[...].astype(F32)
    tile[3:4, :] = jnp.ones((1, WIDE), F32)
    info = tile[...].astype(BF16)
    down[half:, :] = info
    up[half:, :] = info


def pack(v, kinds, phase):
    spec = pl.BlockSpec(memory_space=VM)
    shape = jax.ShapeDtypeStruct((v.shape[0] // 2 + META, WIDE), BF16)
    return pl.pallas_call(
        pack_kernel,
        out_shape=(shape, shape),
        in_specs=[spec] * 3,
        out_specs=(spec, spec),
        scratch_shapes=[VM((META, WIDE), F32)],
        compiler_params=pltpu.CompilerParams(vmem_limit_bytes=16 << 20),
        name="pack",
    )(v, kinds, phase)


def filter_kernel(
    kinds, phase, shift, width, v, sides, hop, hop_t, sym, cos_t, sin_t,
    w, w_hi, cosb, sinb, z, y1, y1b,
):
    half = v.shape[0] // 2
    left, right = sides.at[0 : half + META], sides.at[half + META :]
    centre = shift[0]
    inv_h = 1.0 / jnp.broadcast_to(width[0], (1, WIDE))
    pick = lax.broadcasted_iota(jnp.int32, (cos_t.shape[1], WIDE), 0) % 16
    tile_l = left[half : half + META, :].astype(F32)
    tile_r = right[half : half + META, :].astype(F32)
    row = lax.broadcasted_iota(jnp.int32, (META, WIDE), 0)
    lane = lax.broadcasted_iota(jnp.int32, (META, WIDE), 1)

    def item(tile, i, j):
        return jnp.sum(jnp.where((row == i) & (lane == j), tile, 0.0)).astype(jnp.int32)

    own = {-1: item(tile_l, 0, 3) + MISSING, 4: item(tile_r, 0, 0) + MISSING}
    ahead_of = {r: item(tile_l, 1, 4 + r) + MISSING for r in (-2, -1)}
    ahead_of[4] = item(tile_r, 1, 0) + MISSING
    own.update({r: kinds[0, r] for r in range(4)})
    ahead_of.update({r: kinds[1, r] for r in range(4)})
    pattern = {r: tile_l[2:3, 4 + r : 5 + r].astype(jnp.int32) for r in (-2, -1)}
    pattern[4] = tile_r[2:3, 0:1].astype(jnp.int32)
    pattern.update({r: phase[0, r] for r in range(4)})
    has_left, has_right = tile_l[3:4, :], tile_r[3:4, :]

    def own_kind(r):
        return own[r]

    def next_kind(r):
        return ahead_of[r]

    def flag(kind):
        return jnp.where(kind < MISSING, 1.0, 0.0).astype(F32)

    for r in range(-2, 5):
        hot = jnp.where(pick == pattern[r], 1.0, 0.0).astype(BF16)
        cosb[r + 2] = dot(cos_t[...], hot)
        sinb[r + 2] = dot(sin_t[...], hot)

    def v_row(r):
        if r < 0:
            return left[(r + 2) * BLK : (r + 3) * BLK, :]
        if r > 3:
            return right[(r - 4) * BLK : (r - 3) * BLK, :]
        return v[r * BLK : (r + 1) * BLK, :].astype(BF16)

    def y_row(r):
        return y1b[r + 1]

    def back_phase(x, r):
        x = x.astype(F32)
        return (cosb[r + 2] * x - sinb[r + 2] * times_i(x)).astype(BF16)

    def hop_row(r, row):
        ko, kn, kb = own_kind(r), next_kind(r), next_kind(r - 1)
        total = flag(ko) * dot(sym[jnp.minimum(ko, 7)], row(r))
        ahead = flag(kn) * dot(hop[jnp.minimum(kn, 7)], row(r + 1))
        total += cosb[r + 2] * ahead + sinb[r + 2] * times_i(ahead)
        return total + flag(kb) * dot(hop_t[jnp.minimum(kb, 7)], z[r + 1])

    for r in range(-2, 4):
        z[r + 2] = back_phase(v_row(r), r)
    for r in range(-1, 5):
        vr = v[r * BLK : (r + 1) * BLK, :] if 0 <= r < 4 else v_row(r).astype(F32)
        y = (hop_row(r, v_row) - centre * vr) * inv_h
        if r == -1:
            y = y * has_left
        if r == 4:
            y = y * has_right
        if 0 <= r < 4:
            y1[r] = y
        y1b[r + 1] = y.astype(BF16)
    for r in range(-1, 4):
        z[r + 2] = back_phase(y_row(r), r)
    for r in range(4):
        y = (2.0 * inv_h) * (hop_row(r, y_row) - centre * y1[r]) - v[r * BLK : (r + 1) * BLK, :]
        w[r * BLK : (r + 1) * BLK, :] = y
        w_hi[r * BLK : (r + 1) * BLK, :] = y.astype(BF16)


def chebyshev(*args):
    spec = pl.BlockSpec(memory_space=VM)
    smem = pl.BlockSpec(memory_space=SM)
    return pl.pallas_call(
        filter_kernel,
        out_shape=(jax.ShapeDtypeStruct(args[4].shape, F32), jax.ShapeDtypeStruct(args[4].shape, BF16)),
        in_specs=[smem] * 4 + [spec] * 7,
        out_specs=(spec, spec),
        scratch_shapes=[
            VM((7, BLK, WIDE), F32),
            VM((7, BLK, WIDE), F32),
            VM((6, BLK, WIDE), BF16),
            VM((4, BLK, WIDE), F32),
            VM((6, BLK, WIDE), BF16),
        ],
        compiler_params=pltpu.CompilerParams(vmem_limit_bytes=16 << 20),
        name="chebyshev",
    )(*args)


def gram_kernel(pos, w, own, first, second, third, p01, out):
    which = pos[0]
    for src, ref in enumerate((own, first, second, third)):
        for panel in range(2):
            here = [z for z in range(8) if HELD[panel][z] == src]
            hit = functools.reduce(jnp.logical_or, [which == z for z in here])

            @pl.when(hit)
            def _(ref=ref, panel=panel):
                p01[:, panel * WIDE : (panel + 1) * WIDE] = ref[...]

    both = p01[...]
    w_hi, w_lo = split(w[...])
    prod = dot_t(both, jnp.concatenate([both, w_hi, w_lo], 1))

    def inner(a, b):
        d = prod[a * WIDE : (a + 1) * WIDE, b * WIDE : (b + 1) * WIDE]
        return d[:HALF] + lane_sign(1.0) * pltpu.roll(d[HALF:], HALF, 1)

    row = lax.broadcasted_iota(jnp.int32, (HALF, WIDE), 0)
    lane = lax.broadcasted_iota(jnp.int32, (HALF, WIDE), 1)
    col = jnp.where(lane < HALF, lane, lane - HALF)
    g00, g11 = inner(0, 0), inner(1, 1)
    diag = jnp.where(lane < HALF, g00, pltpu.roll(g11, HALF, 1))
    out[0:HALF, :] = jnp.where(col > row, g00, jnp.where(col < row, g11, diag))
    out[HALF : 2 * HALF, :] = inner(0, 1)
    out[2 * HALF : 3 * HALF, :] = inner(0, 2) + inner(0, 3)
    out[3 * HALF : 4 * HALF, :] = inner(1, 2) + inner(1, 3)


def gram(pos, w, parts):
    spec = pl.BlockSpec(memory_space=VM)
    return pl.pallas_call(
        gram_kernel,
        out_shape=(
            jax.ShapeDtypeStruct((w.shape[0], 2 * WIDE), BF16),
            jax.ShapeDtypeStruct((4 * HALF, WIDE), F32),
        ),
        in_specs=[pl.BlockSpec(memory_space=SM)] + [spec] * 5,
        out_specs=(spec, spec),
        compiler_params=pltpu.CompilerParams(vmem_limit_bytes=16 << 20),
        name="gram",
    )(pos, w, *parts)


def inverse_factor(tr, ti):
    tiles = WIDE // 8
    re = [tr[8 * t : 8 * t + 8] for t in range(tiles)]
    im = [ti[8 * t : 8 * t + 8] for t in range(tiles)]
    lane = lax.broadcasted_iota(jnp.int32, (8, WIDE), 1)
    sub = lax.broadcasted_iota(jnp.int32, (8, WIDE), 0)
    for k in range(WIDE):
        g, j = divmod(k, 8)
        at_k = lane == k
        row_r = re[g][j : j + 1]
        row_i = im[g][j : j + 1]
        inv = 1.0 / jnp.broadcast_to(row_r[:, k : k + 1], (1, WIDE))
        row_r = jnp.where(at_k[:1], 1.0, row_r) * inv
        row_i = jnp.where(at_k[:1], 0.0, row_i) * inv
        row_r = jnp.broadcast_to(row_r, (8, WIDE))
        row_i = jnp.broadcast_to(row_i, (8, WIDE))
        for t in range(g, tiles):
            if t == g and j == 7:
                continue
            cr = jnp.broadcast_to(re[t][:, k : k + 1], (8, WIDE))
            ci = jnp.broadcast_to(im[t][:, k : k + 1], (8, WIDE))
            keep_r = jnp.where(at_k, 0.0, re[t])
            keep_i = jnp.where(at_k, 0.0, im[t])
            new_r = keep_r - (cr * row_r - ci * row_i)
            new_i = keep_i - (cr * row_i + ci * row_r)
            if t == g:
                new_r = jnp.where(sub > j, new_r, re[t])
                new_i = jnp.where(sub > j, new_i, im[t])
            re[t], im[t] = new_r, new_i
    out_r, out_i = [], []
    for t in range(tiles):
        diag = lane == sub + 8 * t
        below = lane < sub + 8 * t
        pivot = jnp.sum(jnp.where(diag, re[t], 0.0), axis=1, keepdims=True)
        scale = lax.rsqrt(pivot)
        out_r.append(jnp.where(diag, 1.0, jnp.where(below, re[t], 0.0)) * scale)
        out_i.append(jnp.where(below, im[t], 0.0) * scale)
    return jnp.concatenate(out_r, 0), jnp.concatenate(out_i, 0)


def embed(block):
    return jnp.concatenate([block, times_i(block)], 0)


def finish_kernel(pos, g, w, p01, out):
    row = lax.broadcasted_iota(jnp.int32, (HALF, WIDE), 0)
    lane = lax.broadcasted_iota(jnp.int32, (HALF, WIDE), 1)
    left = lane < HALF
    col = jnp.where(left, lane, lane - HALF)
    c, g01 = g[0:HALF, :], g[HALF : 2 * HALF, :]
    c_turn, g01_turn = pltpu.roll(c, HALF, 1), pltpu.roll(g01, HALF, 1)
    above, below, diag = col > row, col < row, col == row

    def stack(top_left, top_right, low_right):
        return jnp.concatenate([jnp.where(left, top_left, top_right), jnp.where(left, 0.0, low_right)], 0)

    once_r = stack(jnp.where(above, c, 0.0), g01_turn, jnp.where(below, c_turn, 0.0))
    once_i = stack(jnp.where(above, c_turn, 0.0), g01, jnp.where(below, c, 0.0))
    pivots = jnp.where(diag, c, 0.0)
    tr = once_r + jnp.transpose(once_r) + stack(pivots, 0.0, pivots)
    ti = once_i - jnp.transpose(once_i)
    rr, ri = inverse_factor(tr, ti)
    which = pos[0]

    @pl.when(which >= 2)
    def _():
        m = g[2 * HALF : 4 * HALF, :]
        n = dot(rr, m, precision=HIGHEST) + dot(ri, times_i(m), precision=HIGHEST)
        k = dot_t(rr, n, precision=HIGHEST) - dot_t(ri, times_i(n), precision=HIGHEST)
        e_hi, e_lo = split(jnp.concatenate([embed(k[:HALF]), embed(k[HALF:])], 0))
        out[...] = w[...] - (dot(p01[...], e_hi) + dot(p01[...], e_lo))

    @pl.when(which < 2)
    def _():
        rt, it = jnp.transpose(rr), jnp.transpose(ri)
        full = lax.broadcasted_iota(jnp.int32, (WIDE, WIDE), 1) < HALF
        first = jnp.where(full, rt, -pltpu.roll(it, HALF, 1))
        second = jnp.where(full, pltpu.roll(rt, HALF, 1), -it)
        is_first = which == 0
        own = jnp.where(is_first, first[:HALF], second[HALF:])
        other = jnp.where(is_first, 0.0, second[:HALF])
        o_hi, o_lo = split(embed(other))
        p0 = p01[:, :WIDE]
        out[...] = dot(w[...], embed(own), precision=HIGHEST) + dot(p0, o_hi) + dot(p0, o_lo)


def finish(pos, g, w, p01):
    spec = pl.BlockSpec(memory_space=VM)
    return pl.pallas_call(
        finish_kernel,
        out_shape=jax.ShapeDtypeStruct(w.shape, F32),
        in_specs=[pl.BlockSpec(memory_space=SM), spec, spec, spec],
        out_specs=spec,
        compiler_params=pltpu.CompilerParams(vmem_limit_bytes=16 << 20),
        name="finish",
    )(pos, g, w, p01)


def swap(x, axes):
    return lax.all_to_all(x, axes, 0, 0, tiled=True)


def copies(x, count):
    return jnp.broadcast_to(x[None], (count,) + x.shape).reshape((count * x.shape[0],) + x.shape[1:])


def sum_pieces(x, count):
    return jnp.sum(x.reshape((count, -1) + x.shape[1:]), axis=0)


def slab_sum(x, axes):
    count = lax.axis_size(axes)
    return swap(copies(sum_pieces(swap(x, axes), count), count), axes)


def spread(w_hi, pos):
    far = lax.ppermute(w_hi, "panel", [(0, 3), (1, 6)])
    own = jnp.where((pos == 3) | (pos == 6), far, w_hi)
    return (own,) + tuple(lax.ppermute(own, "panel", pairs) for pairs in STEPS)


def thirds(x):
    a = lax.reduce_precision(x, 8, 7)
    b = lax.reduce_precision(x - a, 8, 7)
    return jnp.concatenate([a, b, x - a - b], axis=0).astype(BF16).T


def body(vectors, hop_table, block_kind, block_phase, phase_angles, centre, half_width):
    slab = ("y", "x", "core")
    count = lax.axis_size(slab)
    kinds, phase = block_kind.T, block_phase[None, :]
    up, down = pack(vectors, kinds, phase)
    left = lax.ppermute(up, slab, [(i, i + 1) for i in range(count - 1)])
    right = lax.ppermute(down, slab, [(i + 1, i) for i in range(count - 1)])
    sides = jnp.concatenate([left, right], axis=0)
    wide = hop_table.astype(F32)
    turned = jnp.transpose(hop_table, (0, 2, 1))
    sym = ((wide + turned.astype(F32)) * 0.5).astype(BF16)
    cos_t = thirds(jnp.cos(phase_angles))
    sin_t = thirds(jnp.sin(phase_angles))
    w, w_hi = chebyshev(
        kinds, phase, centre, half_width, vectors, sides, hop_table, turned, sym, cos_t, sin_t
    )
    pos = lax.axis_index("panel").astype(jnp.int32)
    spot = pos.reshape(1)
    p01, part = gram(spot, w, spread(w_hi, pos))
    return finish(spot, slab_sum(part, slab), w, p01)


def solution(mesh):
    panels = mesh.shape["panel"]
    devices = np.asarray(mesh.devices).reshape(8, 4, 2, panels)
    fine = Mesh(devices, ("y", "x", "core", "panel"))
    slab = ("y", "x", "core")
    in_specs = (P(slab, "panel"), P(), P(slab, None), P(slab), P(), P(), P())
    return jax.shard_map(body, mesh=fine, in_specs=in_specs, out_specs=P(slab, "panel"), check_vma=False)
```

```python
import functools

import jax
import jax.numpy as jnp
import numpy as np
from jax import lax
from jax.experimental import pallas as pl
from jax.experimental.pallas import tpu as pltpu
from jax.sharding import Mesh, PartitionSpec as P

HIGHEST = lax.Precision.HIGHEST
F32 = jnp.float32
BF16 = jnp.bfloat16
BLK = 256
WIDE = 128
HALF = 64
META = 16
MISSING = 8
STEPS = (
    [(0, 1), (3, 4), (1, 2), (6, 7)],
    [(0, 7), (3, 2), (1, 0), (6, 5)],
    [(0, 6), (3, 5), (1, 3), (6, 4)],
)
HELD = ((0, 1, 2, 0, 1, 3, 3, 2), (2, 0, 1, 3, 3, 2, 0, 1))
VM = pltpu.VMEM
SM = pltpu.SMEM


def lane_sign(first):
    lane = lax.broadcasted_iota(jnp.int32, (1, WIDE), 1)
    return jnp.where(lane < HALF, first, -first).astype(F32)


def times_i(packed):
    return lane_sign(-1.0) * pltpu.roll(packed, HALF, 1)


def dot(a, b, **kw):
    return lax.dot_general(a, b, (((1,), (0,)), ((), ())), preferred_element_type=F32, **kw)


def dot_t(a, b, **kw):
    return lax.dot_general(a, b, (((0,), (0,)), ((), ())), preferred_element_type=F32, **kw)


def split(x):
    hi = x.astype(BF16)
    return hi, (x - hi.astype(F32)).astype(BF16)


def pack_kernel(v, kinds, phase, up, down, tile):
    half = v.shape[0] // 2
    down[:half, :] = v[:half, :].astype(BF16)
    up[:half, :] = v[half:, :].astype(BF16)
    tile[...] = jnp.zeros(tile.shape, F32)
    tile[0:2, 0:4] = (kinds[...] - MISSING).astype(F32)
    tile[2:3, 0:4] = phase[...].astype(F32)
    tile[3:4, :] = jnp.ones((1, WIDE), F32)
    info = tile[...].astype(BF16)
    down[half:, :] = info
    up[half:, :] = info


def pack(v, kinds, phase):
    spec = pl.BlockSpec(memory_space=VM)
    shape = jax.ShapeDtypeStruct((v.shape[0] // 2 + META, WIDE), BF16)
    return pl.pallas_call(
        pack_kernel,
        out_shape=(shape, shape),
        in_specs=[spec] * 3,
        out_specs=(spec, spec),
        scratch_shapes=[VM((META, WIDE), F32)],
        compiler_params=pltpu.CompilerParams(vmem_limit_bytes=16 << 20),
        name="pack",
    )(v, kinds, phase)


def filter_kernel(
    kinds, phase, shift, width, v, sides, hop, hop_t, sym, cos_t, sin_t,
    w, w_hi, cosb, sinb, z, y1, y1b,
):
    half = v.shape[0] // 2
    left, right = sides.at[0 : half + META], sides.at[half + META :]
    centre = shift[0]
    inv_h = 1.0 / jnp.broadcast_to(width[0], (1, WIDE))
    pick = lax.broadcasted_iota(jnp.int32, (cos_t.shape[1], WIDE), 0) % 16
    tile_l = left[half : half + META, :].astype(F32)
    tile_r = right[half : half + META, :].astype(F32)
    row = lax.broadcasted_iota(jnp.int32, (META, WIDE), 0)
    lane = lax.broadcasted_iota(jnp.int32, (META, WIDE), 1)

    def item(tile, i, j):
        return jnp.sum(jnp.where((row == i) & (lane == j), tile, 0.0)).astype(jnp.int32)

    own = {-1: item(tile_l, 0, 3) + MISSING, 4: item(tile_r, 0, 0) + MISSING}
    ahead_of = {r: item(tile_l, 1, 4 + r) + MISSING for r in (-2, -1)}
    ahead_of[4] = item(tile_r, 1, 0) + MISSING
    own.update({r: kinds[0, r] for r in range(4)})
    ahead_of.update({r: kinds[1, r] for r in range(4)})
    pattern = {r: tile_l[2:3, 4 + r : 5 + r].astype(jnp.int32) for r in (-2, -1)}
    pattern[4] = tile_r[2:3, 0:1].astype(jnp.int32)
    pattern.update({r: phase[0, r] for r in range(4)})
    has_left, has_right = tile_l[3:4, :], tile_r[3:4, :]

    def own_kind(r):
        return own[r]

    def next_kind(r):
        return ahead_of[r]

    def flag(kind):
        return jnp.where(kind < MISSING, 1.0, 0.0).astype(F32)

    for r in range(-2, 5):
        hot = jnp.where(pick == pattern[r], 1.0, 0.0).astype(BF16)
        cosb[r + 2] = dot(cos_t[...], hot)
        sinb[r + 2] = dot(sin_t[...], hot)

    def v_row(r):
        if r < 0:
            return left[(r + 2) * BLK : (r + 3) * BLK, :]
        if r > 3:
            return right[(r - 4) * BLK : (r - 3) * BLK, :]
        return v[r * BLK : (r + 1) * BLK, :].astype(BF16)

    def y_row(r):
        return y1b[r + 1]

    def back_phase(x, r):
        x = x.astype(F32)
        return (cosb[r + 2] * x - sinb[r + 2] * times_i(x)).astype(BF16)

    def hop_row(r, row):
        ko, kn, kb = own_kind(r), next_kind(r), next_kind(r - 1)
        total = flag(ko) * dot(sym[jnp.minimum(ko, 7)], row(r))
        ahead = flag(kn) * dot(hop[jnp.minimum(kn, 7)], row(r + 1))
        total += cosb[r + 2] * ahead + sinb[r + 2] * times_i(ahead)
        return total + flag(kb) * dot(hop_t[jnp.minimum(kb, 7)], z[r + 1])

    for r in range(-2, 4):
        z[r + 2] = back_phase(v_row(r), r)
    for r in range(-1, 5):
        vr = v[r * BLK : (r + 1) * BLK, :] if 0 <= r < 4 else v_row(r).astype(F32)
        y = (hop_row(r, v_row) - centre * vr) * inv_h
        if r == -1:
            y = y * has_left
        if r == 4:
            y = y * has_right
        if 0 <= r < 4:
            y1[r] = y
        y1b[r + 1] = y.astype(BF16)
    for r in range(-1, 4):
        z[r + 2] = back_phase(y_row(r), r)
    for r in range(4):
        y = (2.0 * inv_h) * (hop_row(r, y_row) - centre * y1[r]) - v[r * BLK : (r + 1) * BLK, :]
        w[r * BLK : (r + 1) * BLK, :] = y
        w_hi[r * BLK : (r + 1) * BLK, :] = y.astype(BF16)


def chebyshev(*args):
    spec = pl.BlockSpec(memory_space=VM)
    smem = pl.BlockSpec(memory_space=SM)
    return pl.pallas_call(
        filter_kernel,
        out_shape=(jax.ShapeDtypeStruct(args[4].shape, F32), jax.ShapeDtypeStruct(args[4].shape, BF16)),
        in_specs=[smem] * 4 + [spec] * 7,
        out_specs=(spec, spec),
        scratch_shapes=[
            VM((7, BLK, WIDE), F32),
            VM((7, BLK, WIDE), F32),
            VM((6, BLK, WIDE), BF16),
            VM((4, BLK, WIDE), F32),
            VM((6, BLK, WIDE), BF16),
        ],
        compiler_params=pltpu.CompilerParams(vmem_limit_bytes=16 << 20),
        name="chebyshev",
    )(*args)


def gram_kernel(pos, w, own, first, second, third, p01, out):
    which = pos[0]
    for src, ref in enumerate((own, first, second, third)):
        for panel in range(2):
            here = [z for z in range(8) if HELD[panel][z] == src]
            hit = functools.reduce(jnp.logical_or, [which == z for z in here])

            @pl.when(hit)
            def _(ref=ref, panel=panel):
                p01[:, panel * WIDE : (panel + 1) * WIDE] = ref[...]

    both = p01[...]
    w_hi, w_lo = split(w[...])
    prod = dot_t(both, jnp.concatenate([both, w_hi, w_lo], 1))

    def inner(a, b):
        d = prod[a * WIDE : (a + 1) * WIDE, b * WIDE : (b + 1) * WIDE]
        return d[:HALF] + lane_sign(1.0) * pltpu.roll(d[HALF:], HALF, 1)

    row = lax.broadcasted_iota(jnp.int32, (HALF, WIDE), 0)
    lane = lax.broadcasted_iota(jnp.int32, (HALF, WIDE), 1)
    col = jnp.where(lane < HALF, lane, lane - HALF)
    g00, g11 = inner(0, 0), inner(1, 1)
    diag = jnp.where(lane < HALF, g00, pltpu.roll(g11, HALF, 1))
    out[0:HALF, :] = jnp.where(col > row, g00, jnp.where(col < row, g11, diag))
    out[HALF : 2 * HALF, :] = inner(0, 1)
    out[2 * HALF : 3 * HALF, :] = inner(0, 2) + inner(0, 3)
    out[3 * HALF : 4 * HALF, :] = inner(1, 2) + inner(1, 3)


def gram(pos, w, parts):
    spec = pl.BlockSpec(memory_space=VM)
    return pl.pallas_call(
        gram_kernel,
        out_shape=(
            jax.ShapeDtypeStruct((w.shape[0], 2 * WIDE), BF16),
            jax.ShapeDtypeStruct((4 * HALF, WIDE), F32),
        ),
        in_specs=[pl.BlockSpec(memory_space=SM)] + [spec] * 5,
        out_specs=(spec, spec),
        compiler_params=pltpu.CompilerParams(vmem_limit_bytes=16 << 20),
        name="gram",
    )(pos, w, *parts)


def inverse_factor(tr, ti):
    tiles = WIDE // 8
    re = [tr[8 * t : 8 * t + 8] for t in range(tiles)]
    im = [ti[8 * t : 8 * t + 8] for t in range(tiles)]
    lane = lax.broadcasted_iota(jnp.int32, (8, WIDE), 1)
    sub = lax.broadcasted_iota(jnp.int32, (8, WIDE), 0)
    for k in range(WIDE):
        g, j = divmod(k, 8)
        at_k = lane == k
        row_r = re[g][j : j + 1]
        row_i = im[g][j : j + 1]
        inv = 1.0 / jnp.broadcast_to(row_r[:, k : k + 1], (1, WIDE))
        row_r = jnp.where(at_k[:1], 1.0, row_r) * inv
        row_i = jnp.where(at_k[:1], 0.0, row_i) * inv
        row_r = jnp.broadcast_to(row_r, (8, WIDE))
        row_i = jnp.broadcast_to(row_i, (8, WIDE))
        for t in range(g, tiles):
            if t == g and j == 7:
                continue
            cr = jnp.broadcast_to(re[t][:, k : k + 1], (8, WIDE))
            ci = jnp.broadcast_to(im[t][:, k : k + 1], (8, WIDE))
            keep_r = jnp.where(at_k, 0.0, re[t])
            keep_i = jnp.where(at_k, 0.0, im[t])
            new_r = keep_r - (cr * row_r - ci * row_i)
            new_i = keep_i - (cr * row_i + ci * row_r)
            if t == g:
                new_r = jnp.where(sub > j, new_r, re[t])
                new_i = jnp.where(sub > j, new_i, im[t])
            re[t], im[t] = new_r, new_i
    out_r, out_i = [], []
    for t in range(tiles):
        diag = lane == sub + 8 * t
        below = lane < sub + 8 * t
        pivot = jnp.sum(jnp.where(diag, re[t], 0.0), axis=1, keepdims=True)
        scale = lax.rsqrt(pivot)
        out_r.append(jnp.where(diag, 1.0, jnp.where(below, re[t], 0.0)) * scale)
        out_i.append(jnp.where(below, im[t], 0.0) * scale)
    return jnp.concatenate(out_r, 0), jnp.concatenate(out_i, 0)


def wide_dot(x, y):
    xh, xl = split(x)
    yh, yl = split(y)
    return dot(xh, yh) + (dot(xh, yl) + dot(xl, yh))


def pair(re, im):
    return jnp.concatenate([jnp.concatenate([re, im], 1), jnp.concatenate([-im, re], 1)], 0)


def refine(tr, ti, root):
    row = lax.broadcasted_iota(jnp.int32, (WIDE, WIDE), 0)
    col = lax.broadcasted_iota(jnp.int32, (WIDE, WIDE), 1)
    one = jnp.where(row == col, 1.0, 0.0)
    weight = jnp.where(col < row, 1.0, 0.5 * one)
    down = lax.rsqrt(jnp.sum(one * tr, axis=1, keepdims=True))
    across = lax.rsqrt(jnp.sum(one * tr, axis=0, keepdims=True))
    ar, ai = tr * down * across, ti * down * across
    unit = pair(ar, ai)
    root[:, :WIDE] = one - jnp.where(col < row, ar, 0.0)
    root[:, WIDE:] = -jnp.where(col < row, ai, 0.0)

    def cond(carry):
        step, size = carry
        return (step < 8) & (size > 1e-6) & (size < 1.0)

    def step(carry):
        count, _ = carry
        r = root[...]
        half = wide_dot(r, unit)
        rt, it = jnp.transpose(r[:, :WIDE]), jnp.transpose(r[:, WIDE:])
        e = wide_dot(half, pair(rt, -it))
        er, ei = e[:, :WIDE] - one, e[:, WIDE:]
        size = jnp.sum(er * er + ei * ei)
        fix = jnp.concatenate([weight * er, weight * ei], 1)
        root[...] = r - wide_dot(fix, pair(r[:, :WIDE], r[:, WIDE:]))
        return count + 1, size

    count, size = lax.while_loop(cond, step, (jnp.int32(0), jnp.float32(0.5)))
    good = size <= 1e-6

    @pl.when(good)
    def _():
        root[:, :WIDE] = root[:, :WIDE] * across
        root[:, WIDE:] = root[:, WIDE:] * across

    @pl.when(jnp.logical_not(good))
    def _():
        re, im = inverse_factor(tr, ti)
        root[:, :WIDE] = re
        root[:, WIDE:] = im


def embed(block):
    return jnp.concatenate([block, times_i(block)], 0)


def finish_kernel(pos, g, w, p01, out, root):
    row = lax.broadcasted_iota(jnp.int32, (HALF, WIDE), 0)
    lane = lax.broadcasted_iota(jnp.int32, (HALF, WIDE), 1)
    left = lane < HALF
    col = jnp.where(left, lane, lane - HALF)
    c, g01 = g[0:HALF, :], g[HALF : 2 * HALF, :]
    c_turn, g01_turn = pltpu.roll(c, HALF, 1), pltpu.roll(g01, HALF, 1)
    above, below, diag = col > row, col < row, col == row

    def stack(top_left, top_right, low_right):
        return jnp.concatenate([jnp.where(left, top_left, top_right), jnp.where(left, 0.0, low_right)], 0)

    once_r = stack(jnp.where(above, c, 0.0), g01_turn, jnp.where(below, c_turn, 0.0))
    once_i = stack(jnp.where(above, c_turn, 0.0), g01, jnp.where(below, c, 0.0))
    pivots = jnp.where(diag, c, 0.0)
    tr = once_r + jnp.transpose(once_r) + stack(pivots, 0.0, pivots)
    ti = once_i - jnp.transpose(once_i)
    refine(tr, ti, root)
    rr, ri = root[:, :WIDE], root[:, WIDE:]
    which = pos[0]

    @pl.when(which >= 2)
    def _():
        m = g[2 * HALF : 4 * HALF, :]
        n = dot(rr, m, precision=HIGHEST) + dot(ri, times_i(m), precision=HIGHEST)
        k = dot_t(rr, n, precision=HIGHEST) - dot_t(ri, times_i(n), precision=HIGHEST)
        e_hi, e_lo = split(jnp.concatenate([embed(k[:HALF]), embed(k[HALF:])], 0))
        out[...] = w[...] - (dot(p01[...], e_hi) + dot(p01[...], e_lo))

    @pl.when(which < 2)
    def _():
        rt, it = jnp.transpose(rr), jnp.transpose(ri)
        full = lax.broadcasted_iota(jnp.int32, (WIDE, WIDE), 1) < HALF
        first = jnp.where(full, rt, -pltpu.roll(it, HALF, 1))
        second = jnp.where(full, pltpu.roll(rt, HALF, 1), -it)
        is_first = which == 0
        own = jnp.where(is_first, first[:HALF], second[HALF:])
        other = jnp.where(is_first, 0.0, second[:HALF])
        o_hi, o_lo = split(embed(other))
        p0 = p01[:, :WIDE]
        out[...] = dot(w[...], embed(own), precision=HIGHEST) + dot(p0, o_hi) + dot(p0, o_lo)


def finish(pos, g, w, p01):
    spec = pl.BlockSpec(memory_space=VM)
    return pl.pallas_call(
        finish_kernel,
        out_shape=jax.ShapeDtypeStruct(w.shape, F32),
        in_specs=[pl.BlockSpec(memory_space=SM), spec, spec, spec],
        out_specs=spec,
        scratch_shapes=[VM((WIDE, 2 * WIDE), F32)],
        compiler_params=pltpu.CompilerParams(vmem_limit_bytes=16 << 20),
        name="finish",
    )(pos, g, w, p01)


def swap(x, axes):
    return lax.all_to_all(x, axes, 0, 0, tiled=True)


def copies(x, count):
    return jnp.broadcast_to(x[None], (count,) + x.shape).reshape((count * x.shape[0],) + x.shape[1:])


def sum_pieces(x, count):
    return jnp.sum(x.reshape((count, -1) + x.shape[1:]), axis=0)


def slab_sum(x, axes):
    count = lax.axis_size(axes)
    return swap(copies(sum_pieces(swap(x, axes), count), count), axes)


def spread(w_hi, pos):
    far = lax.ppermute(w_hi, "panel", [(0, 3), (1, 6)])
    own = jnp.where((pos == 3) | (pos == 6), far, w_hi)
    return (own,) + tuple(lax.ppermute(own, "panel", pairs) for pairs in STEPS)


def thirds(x):
    a = lax.reduce_precision(x, 8, 7)
    b = lax.reduce_precision(x - a, 8, 7)
    return jnp.concatenate([a, b, x - a - b], axis=0).astype(BF16).T


def body(vectors, hop_table, block_kind, block_phase, phase_angles, centre, half_width):
    slab = ("y", "x", "core")
    count = lax.axis_size(slab)
    kinds, phase = block_kind.T, block_phase[None, :]
    up, down = pack(vectors, kinds, phase)
    left = lax.ppermute(up, slab, [(i, i + 1) for i in range(count - 1)])
    right = lax.ppermute(down, slab, [(i + 1, i) for i in range(count - 1)])
    sides = jnp.concatenate([left, right], axis=0)
    wide = hop_table.astype(F32)
    turned = jnp.transpose(hop_table, (0, 2, 1))
    sym = ((wide + turned.astype(F32)) * 0.5).astype(BF16)
    cos_t = thirds(jnp.cos(phase_angles))
    sin_t = thirds(jnp.sin(phase_angles))
    w, w_hi = chebyshev(
        kinds, phase, centre, half_width, vectors, sides, hop_table, turned, sym, cos_t, sin_t
    )
    pos = lax.axis_index("panel").astype(jnp.int32)
    spot = pos.reshape(1)
    p01, part = gram(spot, w, spread(w_hi, pos))
    return finish(spot, slab_sum(part, slab), w, p01)


def solution(mesh):
    panels = mesh.shape["panel"]
    devices = np.asarray(mesh.devices).reshape(8, 4, 2, panels)
    fine = Mesh(devices, ("y", "x", "core", "panel"))
    slab = ("y", "x", "core")
    in_specs = (P(slab, "panel"), P(), P(slab, None), P(slab), P(), P(), P())
    return jax.shard_map(body, mesh=fine, in_specs=in_specs, out_specs=P(slab, "panel"), check_vma=False)
```

```python
import functools

import jax
import jax.numpy as jnp
import numpy as np
from jax import lax
from jax.experimental import pallas as pl
from jax.experimental.pallas import tpu as pltpu
from jax.sharding import Mesh, PartitionSpec as P

HIGHEST = lax.Precision.HIGHEST
F32 = jnp.float32
BF16 = jnp.bfloat16
BLK = 256
WIDE = 128
HALF = 64
META = 16
MISSING = 8
STEPS = (
    [(0, 1), (3, 4), (1, 2), (6, 7)],
    [(0, 7), (3, 2), (1, 0), (6, 5)],
    [(0, 6), (3, 5), (1, 3), (6, 4)],
)
HELD = ((0, 1, 2, 0, 1, 3, 3, 2), (2, 0, 1, 3, 3, 2, 0, 1))
VM = pltpu.VMEM
SM = pltpu.SMEM


def lane_sign(first):
    lane = lax.broadcasted_iota(jnp.int32, (1, WIDE), 1)
    return jnp.where(lane < HALF, first, -first).astype(F32)


def times_i(packed):
    return lane_sign(-1.0) * pltpu.roll(packed, HALF, 1)


def dot(a, b, **kw):
    return lax.dot_general(a, b, (((1,), (0,)), ((), ())), preferred_element_type=F32, **kw)


def dot_t(a, b, **kw):
    return lax.dot_general(a, b, (((0,), (0,)), ((), ())), preferred_element_type=F32, **kw)


def split(x):
    hi = x.astype(BF16)
    return hi, (x - hi.astype(F32)).astype(BF16)


def pack_kernel(v, kinds, phase, up, down, tile):
    half = v.shape[0] // 2
    down[:half, :] = v[:half, :].astype(BF16)
    up[:half, :] = v[half:, :].astype(BF16)
    tile[...] = jnp.zeros(tile.shape, F32)
    tile[0:2, 0:4] = (kinds[...] - MISSING).astype(F32)
    tile[2:3, 0:4] = phase[...].astype(F32)
    tile[3:4, :] = jnp.ones((1, WIDE), F32)
    info = tile[...].astype(BF16)
    down[half:, :] = info
    up[half:, :] = info


def pack(v, kinds, phase):
    spec = pl.BlockSpec(memory_space=VM)
    shape = jax.ShapeDtypeStruct((v.shape[0] // 2 + META, WIDE), BF16)
    return pl.pallas_call(
        pack_kernel,
        out_shape=(shape, shape),
        in_specs=[spec] * 3,
        out_specs=(spec, spec),
        scratch_shapes=[VM((META, WIDE), F32)],
        name="pack",
    )(v, kinds, phase)


def filter_kernel(
    kinds, phase, shift, width, base, sides, hop, hop_t, sym, cos_t, sin_t,
    w, w_hi, vb, cosb, sinb, z, y1, y1b,
):
    half = base.shape[0] // 2
    left, right = sides.at[0 : half + META], sides.at[half + META :]
    centre = shift[0]
    h = jnp.broadcast_to(width[0], (1, WIDE))
    inv_h = 1.0 / h
    pick = lax.broadcasted_iota(jnp.int32, (cos_t.shape[1], WIDE), 0) % 16
    tile_l = left[half : half + META, :].astype(F32)
    tile_r = right[half : half + META, :].astype(F32)
    row = lax.broadcasted_iota(jnp.int32, (META, WIDE), 0)
    lane = lax.broadcasted_iota(jnp.int32, (META, WIDE), 1)

    def item(tile, i, j):
        return jnp.sum(jnp.where((row == i) & (lane == j), tile, 0.0)).astype(jnp.int32)

    own = {-1: item(tile_l, 0, 3) + MISSING, 4: item(tile_r, 0, 0) + MISSING}
    ahead_of = {r: item(tile_l, 1, 4 + r) + MISSING for r in (-2, -1)}
    ahead_of[4] = item(tile_r, 1, 0) + MISSING
    own.update({r: kinds[0, r] for r in range(4)})
    ahead_of.update({r: kinds[1, r] for r in range(4)})
    pattern = {r: tile_l[2:3, 4 + r : 5 + r].astype(jnp.int32) for r in (-2, -1)}
    pattern[4] = tile_r[2:3, 0:1].astype(jnp.int32)
    pattern.update({r: phase[0, r] for r in range(4)})
    has_left, has_right = tile_l[3:4, :], tile_r[3:4, :]

    def own_kind(r):
        return own[r]

    def next_kind(r):
        return ahead_of[r]

    def flag(kind):
        return jnp.where(kind < MISSING, 1.0, 0.0).astype(F32)

    for r in range(-2, 5):
        hot = jnp.where(pick == pattern[r], 1.0, 0.0).astype(BF16)
        cosb[r + 2] = dot(cos_t[...], hot)
        sinb[r + 2] = dot(sin_t[...], hot)

    def v_row(r):
        if r < 0:
            return left[(r + 2) * BLK : (r + 3) * BLK, :]
        if r > 3:
            return right[(r - 4) * BLK : (r - 3) * BLK, :]
        return vb[r * BLK : (r + 1) * BLK, :]

    def y_row(r):
        return y1b[r + 1]

    def back_phase(x, r):
        x = x.astype(F32)
        return (cosb[r + 2] * x - sinb[r + 2] * times_i(x)).astype(BF16)

    def hop_row(r, row):
        ko, kn, kb = own_kind(r), next_kind(r), next_kind(r - 1)
        total = flag(ko) * dot(sym[jnp.minimum(ko, 7)], row(r))
        ahead = flag(kn) * dot(hop[jnp.minimum(kn, 7)], row(r + 1))
        total += cosb[r + 2] * ahead + sinb[r + 2] * times_i(ahead)
        return total + flag(kb) * dot(hop_t[jnp.minimum(kb, 7)], z[r + 1])

    vb[...] = (h * base[...]).astype(BF16)
    for r in range(-2, 4):
        z[r + 2] = back_phase(v_row(r), r)
    for r in range(-1, 5):
        scaled = base[r * BLK : (r + 1) * BLK, :] if 0 <= r < 4 else v_row(r).astype(F32) * inv_h
        y = hop_row(r, v_row) * inv_h - centre * scaled
        if r == -1:
            y = y * has_left
        if r == 4:
            y = y * has_right
        if 0 <= r < 4:
            y1[r] = y
        y1b[r + 1] = y.astype(BF16)
    for r in range(-1, 4):
        z[r + 2] = back_phase(y_row(r), r)
    for r in range(4):
        y = (2.0 * inv_h) * (hop_row(r, y_row) - centre * y1[r]) - h * base[r * BLK : (r + 1) * BLK, :]
        w[r * BLK : (r + 1) * BLK, :] = y
        w_hi[r * BLK : (r + 1) * BLK, :] = y.astype(BF16)


def chebyshev(*args):
    spec = pl.BlockSpec(memory_space=VM)
    smem = pl.BlockSpec(memory_space=SM)
    return pl.pallas_call(
        filter_kernel,
        out_shape=(jax.ShapeDtypeStruct(args[4].shape, F32), jax.ShapeDtypeStruct(args[4].shape, BF16)),
        in_specs=[smem] * 4 + [spec] * 7,
        out_specs=(spec, spec),
        scratch_shapes=[
            VM(args[4].shape, BF16),
            VM((7, BLK, WIDE), F32),
            VM((7, BLK, WIDE), F32),
            VM((6, BLK, WIDE), BF16),
            VM((4, BLK, WIDE), F32),
            VM((6, BLK, WIDE), BF16),
        ],
        compiler_params=pltpu.CompilerParams(vmem_limit_bytes=16 << 20),
        name="chebyshev",
    )(*args)


def gram_kernel(pos, w, own, first, second, third, p01, out):
    which = pos[0]
    for src, ref in enumerate((own, first, second, third)):
        for panel in range(2):
            here = [z for z in range(8) if HELD[panel][z] == src]
            hit = functools.reduce(jnp.logical_or, [which == z for z in here])

            @pl.when(hit)
            def _(ref=ref, panel=panel):
                p01[:, panel * WIDE : (panel + 1) * WIDE] = ref[...]

    both = p01[...]
    w_hi, w_lo = split(w[...])
    prod = dot_t(both, jnp.concatenate([both, w_hi, w_lo], 1))

    def inner(a, b):
        d = prod[a * WIDE : (a + 1) * WIDE, b * WIDE : (b + 1) * WIDE]
        return d[:HALF] + lane_sign(1.0) * pltpu.roll(d[HALF:], HALF, 1)

    row = lax.broadcasted_iota(jnp.int32, (HALF, WIDE), 0)
    lane = lax.broadcasted_iota(jnp.int32, (HALF, WIDE), 1)
    col = jnp.where(lane < HALF, lane, lane - HALF)
    g00, g11 = inner(0, 0), inner(1, 1)
    diag = jnp.where(lane < HALF, g00, pltpu.roll(g11, HALF, 1))
    out[0:HALF, :] = jnp.where(col > row, g00, jnp.where(col < row, g11, diag))
    out[HALF : 2 * HALF, :] = inner(0, 1)
    out[2 * HALF : 3 * HALF, :] = inner(0, 2) + inner(0, 3)
    out[3 * HALF : 4 * HALF, :] = inner(1, 2) + inner(1, 3)


def gram(pos, w, parts):
    spec = pl.BlockSpec(memory_space=VM)
    return pl.pallas_call(
        gram_kernel,
        out_shape=(
            jax.ShapeDtypeStruct((w.shape[0], 2 * WIDE), BF16),
            jax.ShapeDtypeStruct((4 * HALF, WIDE), F32),
        ),
        in_specs=[pl.BlockSpec(memory_space=SM)] + [spec] * 5,
        out_specs=(spec, spec),
        compiler_params=pltpu.CompilerParams(vmem_limit_bytes=16 << 20),
        name="gram",
    )(pos, w, *parts)


def inverse_factor(tr, ti):
    tiles = WIDE // 8
    re = [tr[8 * t : 8 * t + 8] for t in range(tiles)]
    im = [ti[8 * t : 8 * t + 8] for t in range(tiles)]
    lane = lax.broadcasted_iota(jnp.int32, (8, WIDE), 1)
    sub = lax.broadcasted_iota(jnp.int32, (8, WIDE), 0)
    for k in range(WIDE):
        g, j = divmod(k, 8)
        at_k = lane == k
        row_r = re[g][j : j + 1]
        row_i = im[g][j : j + 1]
        inv = 1.0 / jnp.broadcast_to(row_r[:, k : k + 1], (1, WIDE))
        row_r = jnp.where(at_k[:1], 1.0, row_r) * inv
        row_i = jnp.where(at_k[:1], 0.0, row_i) * inv
        row_r = jnp.broadcast_to(row_r, (8, WIDE))
        row_i = jnp.broadcast_to(row_i, (8, WIDE))
        for t in range(g, tiles):
            if t == g and j == 7:
                continue
            cr = jnp.broadcast_to(re[t][:, k : k + 1], (8, WIDE))
            ci = jnp.broadcast_to(im[t][:, k : k + 1], (8, WIDE))
            keep_r = jnp.where(at_k, 0.0, re[t])
            keep_i = jnp.where(at_k, 0.0, im[t])
            new_r = keep_r - (cr * row_r - ci * row_i)
            new_i = keep_i - (cr * row_i + ci * row_r)
            if t == g:
                new_r = jnp.where(sub > j, new_r, re[t])
                new_i = jnp.where(sub > j, new_i, im[t])
            re[t], im[t] = new_r, new_i
    out_r, out_i = [], []
    for t in range(tiles):
        diag = lane == sub + 8 * t
        below = lane < sub + 8 * t
        pivot = jnp.sum(jnp.where(diag, re[t], 0.0), axis=1, keepdims=True)
        scale = lax.rsqrt(pivot)
        out_r.append(jnp.where(diag, 1.0, jnp.where(below, re[t], 0.0)) * scale)
        out_i.append(jnp.where(below, im[t], 0.0) * scale)
    return jnp.concatenate(out_r, 0), jnp.concatenate(out_i, 0)


def wide_dot(x, y):
    xh, xl = split(x)
    yh, yl = split(y)
    return dot(xh, yh) + (dot(xh, yl) + dot(xl, yh))


def pair(re, im):
    return jnp.concatenate([jnp.concatenate([re, im], 1), jnp.concatenate([-im, re], 1)], 0)


def refine(tr, ti, root):
    row = lax.broadcasted_iota(jnp.int32, (WIDE, WIDE), 0)
    col = lax.broadcasted_iota(jnp.int32, (WIDE, WIDE), 1)
    one = jnp.where(row == col, 1.0, 0.0)
    weight = jnp.where(col < row, 1.0, 0.5 * one)
    down = lax.rsqrt(jnp.sum(one * tr, axis=1, keepdims=True))
    across = lax.rsqrt(jnp.sum(one * tr, axis=0, keepdims=True))
    ar, ai = tr * down * across, ti * down * across
    unit = pair(ar, ai)
    root[:, :WIDE] = one - jnp.where(col < row, ar, 0.0)
    root[:, WIDE:] = -jnp.where(col < row, ai, 0.0)

    def cond(carry):
        step, size = carry
        return (step < 8) & (size > 1e-6) & (size < 1.0)

    def step(carry):
        count, _ = carry
        r = root[...]
        half = wide_dot(r, unit)
        rt, it = jnp.transpose(r[:, :WIDE]), jnp.transpose(r[:, WIDE:])
        e = wide_dot(half, pair(rt, -it))
        er, ei = e[:, :WIDE] - one, e[:, WIDE:]
        size = jnp.sum(er * er + ei * ei)
        fix = jnp.concatenate([weight * er, weight * ei], 1)
        root[...] = r - wide_dot(fix, pair(r[:, :WIDE], r[:, WIDE:]))
        return count + 1, size

    count, size = lax.while_loop(cond, step, (jnp.int32(0), jnp.float32(0.5)))
    good = size <= 1e-6

    @pl.when(good)
    def _():
        root[:, :WIDE] = root[:, :WIDE] * across
        root[:, WIDE:] = root[:, WIDE:] * across

    @pl.when(jnp.logical_not(good))
    def _():
        re, im = inverse_factor(tr, ti)
        root[:, :WIDE] = re
        root[:, WIDE:] = im


def embed(block):
    return jnp.concatenate([block, times_i(block)], 0)


def finish_kernel(pos, g, w, p01, out, root):
    row = lax.broadcasted_iota(jnp.int32, (HALF, WIDE), 0)
    lane = lax.broadcasted_iota(jnp.int32, (HALF, WIDE), 1)
    left = lane < HALF
    col = jnp.where(left, lane, lane - HALF)
    c, g01 = g[0:HALF, :], g[HALF : 2 * HALF, :]
    c_turn, g01_turn = pltpu.roll(c, HALF, 1), pltpu.roll(g01, HALF, 1)
    above, below, diag = col > row, col < row, col == row

    def stack(top_left, top_right, low_right):
        return jnp.concatenate([jnp.where(left, top_left, top_right), jnp.where(left, 0.0, low_right)], 0)

    once_r = stack(jnp.where(above, c, 0.0), g01_turn, jnp.where(below, c_turn, 0.0))
    once_i = stack(jnp.where(above, c_turn, 0.0), g01, jnp.where(below, c, 0.0))
    pivots = jnp.where(diag, c, 0.0)
    tr = once_r + jnp.transpose(once_r) + stack(pivots, 0.0, pivots)
    ti = once_i - jnp.transpose(once_i)
    refine(tr, ti, root)
    rr, ri = root[:, :WIDE], root[:, WIDE:]
    which = pos[0]

    @pl.when(which >= 2)
    def _():
        m = g[2 * HALF : 4 * HALF, :]
        n = dot(rr, m, precision=HIGHEST) + dot(ri, times_i(m), precision=HIGHEST)
        k = dot_t(rr, n, precision=HIGHEST) - dot_t(ri, times_i(n), precision=HIGHEST)
        e_hi, e_lo = split(jnp.concatenate([embed(k[:HALF]), embed(k[HALF:])], 0))
        out[...] = w[...] - (dot(p01[...], e_hi) + dot(p01[...], e_lo))

    @pl.when(which < 2)
    def _():
        rt, it = jnp.transpose(rr), jnp.transpose(ri)
        full = lax.broadcasted_iota(jnp.int32, (WIDE, WIDE), 1) < HALF
        first = jnp.where(full, rt, -pltpu.roll(it, HALF, 1))
        second = jnp.where(full, pltpu.roll(rt, HALF, 1), -it)
        is_first = which == 0
        own = jnp.where(is_first, first[:HALF], second[HALF:])
        other = jnp.where(is_first, 0.0, second[:HALF])
        o_hi, o_lo = split(embed(other))
        p0 = p01[:, :WIDE]
        out[...] = dot(w[...], embed(own), precision=HIGHEST) + dot(p0, o_hi) + dot(p0, o_lo)


def finish(pos, g, w, p01):
    spec = pl.BlockSpec(memory_space=VM)
    return pl.pallas_call(
        finish_kernel,
        out_shape=jax.ShapeDtypeStruct(w.shape, F32),
        in_specs=[pl.BlockSpec(memory_space=SM), spec, spec, spec],
        out_specs=spec,
        scratch_shapes=[VM((WIDE, 2 * WIDE), F32)],
        compiler_params=pltpu.CompilerParams(vmem_limit_bytes=16 << 20),
        name="finish",
    )(pos, g, w, p01)


def swap(x, axes):
    return lax.all_to_all(x, axes, 0, 0, tiled=True)


def copies(x, count):
    return jnp.broadcast_to(x[None], (count,) + x.shape).reshape((count * x.shape[0],) + x.shape[1:])


def sum_pieces(x, count):
    return jnp.sum(x.reshape((count, -1) + x.shape[1:]), axis=0)


def slab_sum(x, axes):
    count = lax.axis_size(axes)
    return swap(copies(sum_pieces(swap(x, axes), count), count), axes)


def spread(w_hi, pos):
    far = lax.ppermute(w_hi, "panel", [(0, 3), (1, 6)])
    own = jnp.where((pos == 3) | (pos == 6), far, w_hi)
    return (own,) + tuple(lax.ppermute(own, "panel", pairs) for pairs in STEPS)


def thirds(x):
    a = lax.reduce_precision(x, 8, 7)
    b = lax.reduce_precision(x - a, 8, 7)
    return jnp.concatenate([a, b, x - a - b], axis=0).astype(BF16).T


def body(vectors, hop_table, block_kind, block_phase, phase_angles, centre, half_width):
    slab = ("y", "x", "core")
    count = lax.axis_size(slab)
    kinds, phase = block_kind.T, block_phase[None, :]
    up, down = pack(vectors, kinds, phase)
    left = lax.ppermute(up, slab, [(i, i + 1) for i in range(count - 1)])
    right = lax.ppermute(down, slab, [(i + 1, i) for i in range(count - 1)])
    base = vectors / half_width[0]
    sides = jnp.concatenate([left, right], axis=0)
    wide = hop_table.astype(F32)
    turned = jnp.transpose(hop_table, (0, 2, 1))
    sym = ((wide + turned.astype(F32)) * 0.5).astype(BF16)
    cos_t = thirds(jnp.cos(phase_angles))
    sin_t = thirds(jnp.sin(phase_angles))
    w, w_hi = chebyshev(
        kinds, phase, centre, half_width, base, sides, hop_table, turned, sym, cos_t, sin_t
    )
    pos = lax.axis_index("panel").astype(jnp.int32)
    spot = pos.reshape(1)
    p01, part = gram(spot, w, spread(w_hi, pos))
    return finish(spot, slab_sum(part, slab), w, p01)


def solution(mesh):
    panels = mesh.shape["panel"]
    devices = np.asarray(mesh.devices).reshape(8, 4, 2, panels)
    fine = Mesh(devices, ("y", "x", "core", "panel"))
    slab = ("y", "x", "core")
    in_specs = (P(slab, "panel"), P(), P(slab, None), P(slab), P(), P(), P())
    return jax.shard_map(body, mesh=fine, in_specs=in_specs, out_specs=P(slab, "panel"), check_vma=False)
```

```python
import functools

import jax
import jax.numpy as jnp
import numpy as np
from jax import lax
from jax.experimental import pallas as pl
from jax.experimental.pallas import tpu as pltpu
from jax.sharding import Mesh, PartitionSpec as P

HIGHEST = lax.Precision.HIGHEST
F32 = jnp.float32
BF16 = jnp.bfloat16
BLK = 256
WIDE = 128
HALF = 64
META = 16
MISSING = 8
STEPS = (
    [(0, 1), (3, 4), (1, 2), (6, 7)],
    [(0, 7), (3, 2), (1, 0), (6, 5)],
    [(0, 6), (3, 5), (1, 3), (6, 4)],
)
HELD = ((0, 1, 2, 0, 1, 3, 3, 2), (2, 0, 1, 3, 3, 2, 0, 1))
VM = pltpu.VMEM
SM = pltpu.SMEM


def lane_sign(first):
    lane = lax.broadcasted_iota(jnp.int32, (1, WIDE), 1)
    return jnp.where(lane < HALF, first, -first).astype(F32)


def times_i(packed):
    return lane_sign(-1.0) * pltpu.roll(packed, HALF, 1)


def dot(a, b, **kw):
    return lax.dot_general(a, b, (((1,), (0,)), ((), ())), preferred_element_type=F32, **kw)


def dot_t(a, b, **kw):
    return lax.dot_general(a, b, (((0,), (0,)), ((), ())), preferred_element_type=F32, **kw)


def split(x):
    hi = x.astype(BF16)
    return hi, (x - hi.astype(F32)).astype(BF16)


def pack_kernel(v, kinds, phase, up, down, tile):
    half = v.shape[0] // 2
    down[:half, :] = v[:half, :].astype(BF16)
    up[:half, :] = v[half:, :].astype(BF16)
    tile[...] = jnp.zeros(tile.shape, F32)
    tile[0:2, 0:4] = (kinds[...] - MISSING).astype(F32)
    tile[2:3, 0:4] = phase[...].astype(F32)
    tile[3:4, :] = jnp.ones((1, WIDE), F32)
    info = tile[...].astype(BF16)
    down[half:, :] = info
    up[half:, :] = info


def pack(v, kinds, phase):
    spec = pl.BlockSpec(memory_space=VM)
    shape = jax.ShapeDtypeStruct((v.shape[0] // 2 + META, WIDE), BF16)
    return pl.pallas_call(
        pack_kernel,
        out_shape=(shape, shape),
        in_specs=[spec] * 3,
        out_specs=(spec, spec),
        scratch_shapes=[VM((META, WIDE), F32)],
        name="pack",
    )(v, kinds, phase)


def filter_kernel(
    kinds, phase, shift, width, base, sides, hop, hop_t, sym, cos_t, sin_t,
    w, w_hi, vb, cosb, sinb, z, y1, y1b,
):
    half = base.shape[0] // 2
    left, right = sides.at[0 : half + META], sides.at[half + META :]
    centre = shift[0]
    h = jnp.broadcast_to(width[0], (1, WIDE))
    inv_h = 1.0 / h
    pick = lax.broadcasted_iota(jnp.int32, (cos_t.shape[1], WIDE), 0) % 16
    tile_l = left[half : half + META, :].astype(F32)
    tile_r = right[half : half + META, :].astype(F32)
    row = lax.broadcasted_iota(jnp.int32, (META, WIDE), 0)
    lane = lax.broadcasted_iota(jnp.int32, (META, WIDE), 1)

    def item(tile, i, j):
        return jnp.sum(jnp.where((row == i) & (lane == j), tile, 0.0)).astype(jnp.int32)

    own = {-1: item(tile_l, 0, 3) + MISSING, 4: item(tile_r, 0, 0) + MISSING}
    ahead_of = {r: item(tile_l, 1, 4 + r) + MISSING for r in (-2, -1)}
    ahead_of[4] = item(tile_r, 1, 0) + MISSING
    own.update({r: kinds[0, r] for r in range(4)})
    ahead_of.update({r: kinds[1, r] for r in range(4)})
    pattern = {r: tile_l[2:3, 4 + r : 5 + r].astype(jnp.int32) for r in (-2, -1)}
    pattern[4] = tile_r[2:3, 0:1].astype(jnp.int32)
    pattern.update({r: phase[0, r] for r in range(4)})
    has_left, has_right = tile_l[3:4, :], tile_r[3:4, :]

    def own_kind(r):
        return own[r]

    def next_kind(r):
        return ahead_of[r]

    def flag(kind):
        return jnp.where(kind < MISSING, 1.0, 0.0).astype(F32)

    for r in range(-2, 5):
        hot = jnp.where(pick == pattern[r], 1.0, 0.0).astype(BF16)
        cosb[r + 2] = dot(cos_t[...], hot)
        sinb[r + 2] = dot(sin_t[...], hot)

    def v_row(r):
        if r < 0:
            return left[(r + 2) * BLK : (r + 3) * BLK, :]
        if r > 3:
            return right[(r - 4) * BLK : (r - 3) * BLK, :]
        return vb[r * BLK : (r + 1) * BLK, :]

    def y_row(r):
        return y1b[r + 1]

    def back_phase(x, r):
        x = x.astype(F32)
        return (cosb[r + 2] * x - sinb[r + 2] * times_i(x)).astype(BF16)

    def hop_row(r, row):
        ko, kn, kb = own_kind(r), next_kind(r), next_kind(r - 1)
        total = flag(ko) * dot(sym[jnp.minimum(ko, 7)], row(r))
        ahead = flag(kn) * dot(hop[jnp.minimum(kn, 7)], row(r + 1))
        total += cosb[r + 2] * ahead + sinb[r + 2] * times_i(ahead)
        return total + flag(kb) * dot(hop_t[jnp.minimum(kb, 7)], z[r + 1])

    vb[...] = (h * base[...]).astype(BF16)
    for r in range(-2, 4):
        z[r + 2] = back_phase(v_row(r), r)
    for r in range(-1, 5):
        scaled = base[r * BLK : (r + 1) * BLK, :] if 0 <= r < 4 else v_row(r).astype(F32) * inv_h
        y = hop_row(r, v_row) * inv_h - centre * scaled
        if r == -1:
            y = y * has_left
        if r == 4:
            y = y * has_right
        if 0 <= r < 4:
            y1[r] = y
        y1b[r + 1] = y.astype(BF16)
    for r in range(-1, 4):
        z[r + 2] = back_phase(y_row(r), r)
    for r in range(4):
        y = (2.0 * inv_h) * (hop_row(r, y_row) - centre * y1[r]) - h * base[r * BLK : (r + 1) * BLK, :]
        w[r * BLK : (r + 1) * BLK, :] = y
        w_hi[r * BLK : (r + 1) * BLK, :] = y.astype(BF16)


def chebyshev(*args):
    spec = pl.BlockSpec(memory_space=VM)
    smem = pl.BlockSpec(memory_space=SM)
    return pl.pallas_call(
        filter_kernel,
        out_shape=(jax.ShapeDtypeStruct(args[4].shape, F32), jax.ShapeDtypeStruct(args[4].shape, BF16)),
        in_specs=[smem] * 4 + [spec] * 7,
        out_specs=(spec, spec),
        scratch_shapes=[
            VM(args[4].shape, BF16),
            VM((7, BLK, WIDE), F32),
            VM((7, BLK, WIDE), F32),
            VM((6, BLK, WIDE), BF16),
            VM((4, BLK, WIDE), F32),
            VM((6, BLK, WIDE), BF16),
        ],
        compiler_params=pltpu.CompilerParams(vmem_limit_bytes=16 << 20),
        name="chebyshev",
    )(*args)


def gram_kernel(pos, w, own, first, second, third, p01, out):
    which = pos[0]
    for src, ref in enumerate((own, first, second, third)):
        for panel in range(2):
            here = [z for z in range(8) if HELD[panel][z] == src]
            hit = functools.reduce(jnp.logical_or, [which == z for z in here])

            @pl.when(hit)
            def _(ref=ref, panel=panel):
                p01[:, panel * WIDE : (panel + 1) * WIDE] = ref[...]

    both = p01[...]
    w_hi, w_lo = split(w[...])
    prod = dot_t(both, jnp.concatenate([both, w_hi, w_lo], 1))

    def inner(a, b):
        d = prod[a * WIDE : (a + 1) * WIDE, b * WIDE : (b + 1) * WIDE]
        return d[:HALF] + lane_sign(1.0) * pltpu.roll(d[HALF:], HALF, 1)

    row = lax.broadcasted_iota(jnp.int32, (HALF, WIDE), 0)
    lane = lax.broadcasted_iota(jnp.int32, (HALF, WIDE), 1)
    col = jnp.where(lane < HALF, lane, lane - HALF)
    g00, g11 = inner(0, 0), inner(1, 1)
    diag = jnp.where(lane < HALF, g00, pltpu.roll(g11, HALF, 1))
    out[0:HALF, :] = jnp.where(col > row, g00, jnp.where(col < row, g11, diag))
    out[HALF : 2 * HALF, :] = inner(0, 1)
    out[2 * HALF : 3 * HALF, :] = inner(0, 2) + inner(0, 3)
    out[3 * HALF : 4 * HALF, :] = inner(1, 2) + inner(1, 3)


def gram(pos, w, parts):
    spec = pl.BlockSpec(memory_space=VM)
    return pl.pallas_call(
        gram_kernel,
        out_shape=(
            jax.ShapeDtypeStruct((w.shape[0], 2 * WIDE), BF16),
            jax.ShapeDtypeStruct((4 * HALF, WIDE), F32),
        ),
        in_specs=[pl.BlockSpec(memory_space=SM)] + [spec] * 5,
        out_specs=(spec, spec),
        compiler_params=pltpu.CompilerParams(vmem_limit_bytes=16 << 20),
        name="gram",
    )(pos, w, *parts)


def inverse_factor(tr, ti):
    tiles = WIDE // 8
    re = [tr[8 * t : 8 * t + 8] for t in range(tiles)]
    im = [ti[8 * t : 8 * t + 8] for t in range(tiles)]
    lane = lax.broadcasted_iota(jnp.int32, (8, WIDE), 1)
    sub = lax.broadcasted_iota(jnp.int32, (8, WIDE), 0)
    for k in range(WIDE):
        g, j = divmod(k, 8)
        at_k = lane == k
        row_r = re[g][j : j + 1]
        row_i = im[g][j : j + 1]
        inv = 1.0 / jnp.broadcast_to(row_r[:, k : k + 1], (1, WIDE))
        row_r = jnp.where(at_k[:1], 1.0, row_r) * inv
        row_i = jnp.where(at_k[:1], 0.0, row_i) * inv
        row_r = jnp.broadcast_to(row_r, (8, WIDE))
        row_i = jnp.broadcast_to(row_i, (8, WIDE))
        for t in range(g, tiles):
            if t == g and j == 7:
                continue
            cr = jnp.broadcast_to(re[t][:, k : k + 1], (8, WIDE))
            ci = jnp.broadcast_to(im[t][:, k : k + 1], (8, WIDE))
            keep_r = jnp.where(at_k, 0.0, re[t])
            keep_i = jnp.where(at_k, 0.0, im[t])
            new_r = keep_r - (cr * row_r - ci * row_i)
            new_i = keep_i - (cr * row_i + ci * row_r)
            if t == g:
                new_r = jnp.where(sub > j, new_r, re[t])
                new_i = jnp.where(sub > j, new_i, im[t])
            re[t], im[t] = new_r, new_i
    out_r, out_i = [], []
    for t in range(tiles):
        diag = lane == sub + 8 * t
        below = lane < sub + 8 * t
        pivot = jnp.sum(jnp.where(diag, re[t], 0.0), axis=1, keepdims=True)
        scale = lax.rsqrt(pivot)
        out_r.append(jnp.where(diag, 1.0, jnp.where(below, re[t], 0.0)) * scale)
        out_i.append(jnp.where(below, im[t], 0.0) * scale)
    return jnp.concatenate(out_r, 0), jnp.concatenate(out_i, 0)


def wide_dot(x, y):
    return split_dot(split(x), split(y))


def split_dot(x, y):
    (xh, xl), (yh, yl) = x, y
    return dot(xh, yh) + (dot(xh, yl) + dot(xl, yh))


def pair(re, im):
    return jnp.concatenate([jnp.concatenate([re, im], 1), jnp.concatenate([-im, re], 1)], 0)


def refine(tr, ti, root):
    row = lax.broadcasted_iota(jnp.int32, (WIDE, WIDE), 0)
    col = lax.broadcasted_iota(jnp.int32, (WIDE, WIDE), 1)
    one = jnp.where(row == col, 1.0, 0.0)
    weight = jnp.where(col < row, 1.0, 0.5 * one)
    down = lax.rsqrt(jnp.sum(one * tr, axis=1, keepdims=True))
    across = lax.rsqrt(jnp.sum(one * tr, axis=0, keepdims=True))
    ar, ai = tr * down * across, ti * down * across
    unit = split(pair(ar, ai))
    root[:, :WIDE] = one - jnp.where(col < row, ar, 0.0)
    root[:, WIDE:] = -jnp.where(col < row, ai, 0.0)

    def cond(carry):
        step, size = carry
        return (step < 8) & (size > 1e-5) & (size < 1.0)

    def step(carry):
        count, _ = carry
        r = root[...]
        half = split_dot(split(r), unit)
        rt, it = jnp.transpose(r[:, :WIDE]), jnp.transpose(r[:, WIDE:])
        e = wide_dot(half, pair(rt, -it))
        er, ei = e[:, :WIDE] - one, e[:, WIDE:]
        size = jnp.sum(er * er + ei * ei)
        fix = jnp.concatenate([weight * er, weight * ei], 1)
        root[...] = r - wide_dot(fix, pair(r[:, :WIDE], r[:, WIDE:]))
        return count + 1, size

    count, size = lax.while_loop(cond, step, (jnp.int32(0), jnp.float32(0.5)))
    good = size <= 1e-5

    @pl.when(good)
    def _():
        root[:, :WIDE] = root[:, :WIDE] * across
        root[:, WIDE:] = root[:, WIDE:] * across

    @pl.when(jnp.logical_not(good))
    def _():
        re, im = inverse_factor(tr, ti)
        root[:, :WIDE] = re
        root[:, WIDE:] = im


def embed(block):
    return jnp.concatenate([block, times_i(block)], 0)


def finish_kernel(pos, g, w, p01, out, root):
    row = lax.broadcasted_iota(jnp.int32, (HALF, WIDE), 0)
    lane = lax.broadcasted_iota(jnp.int32, (HALF, WIDE), 1)
    left = lane < HALF
    col = jnp.where(left, lane, lane - HALF)
    c, g01 = g[0:HALF, :], g[HALF : 2 * HALF, :]
    c_turn, g01_turn = pltpu.roll(c, HALF, 1), pltpu.roll(g01, HALF, 1)
    above, below, diag = col > row, col < row, col == row

    def stack(top_left, top_right, low_right):
        return jnp.concatenate([jnp.where(left, top_left, top_right), jnp.where(left, 0.0, low_right)], 0)

    once_r = stack(jnp.where(above, c, 0.0), g01_turn, jnp.where(below, c_turn, 0.0))
    once_i = stack(jnp.where(above, c_turn, 0.0), g01, jnp.where(below, c, 0.0))
    pivots = jnp.where(diag, c, 0.0)
    tr = once_r + jnp.transpose(once_r) + stack(pivots, 0.0, pivots)
    ti = once_i - jnp.transpose(once_i)
    refine(tr, ti, root)
    rr, ri = root[:, :WIDE], root[:, WIDE:]
    which = pos[0]

    @pl.when(which >= 2)
    def _():
        m = g[2 * HALF : 4 * HALF, :]
        n = wide_dot(root[...], embed(m))
        k = wide_dot(jnp.concatenate([jnp.transpose(rr), -jnp.transpose(ri)], 1), embed(n))
        e_hi, e_lo = split(jnp.concatenate([embed(k[:HALF]), embed(k[HALF:])], 0))
        out[...] = w[...] - (dot(p01[...], e_hi) + dot(p01[...], e_lo))

    @pl.when(which < 2)
    def _():
        rt, it = jnp.transpose(rr), jnp.transpose(ri)
        full = lax.broadcasted_iota(jnp.int32, (WIDE, WIDE), 1) < HALF
        first = jnp.where(full, rt, -pltpu.roll(it, HALF, 1))
        second = jnp.where(full, pltpu.roll(rt, HALF, 1), -it)
        is_first = which == 0
        own = jnp.where(is_first, first[:HALF], second[HALF:])
        other = jnp.where(is_first, 0.0, second[:HALF])
        o_hi, o_lo = split(embed(other))
        p0 = p01[:, :WIDE]
        out[...] = dot(w[...], embed(own), precision=HIGHEST) + dot(p0, o_hi) + dot(p0, o_lo)


def finish(pos, g, w, p01):
    spec = pl.BlockSpec(memory_space=VM)
    return pl.pallas_call(
        finish_kernel,
        out_shape=jax.ShapeDtypeStruct(w.shape, F32),
        in_specs=[pl.BlockSpec(memory_space=SM), spec, spec, spec],
        out_specs=spec,
        scratch_shapes=[VM((WIDE, 2 * WIDE), F32)],
        compiler_params=pltpu.CompilerParams(vmem_limit_bytes=16 << 20),
        name="finish",
    )(pos, g, w, p01)


def swap(x, axes):
    return lax.all_to_all(x, axes, 0, 0, tiled=True)


def copies(x, count):
    return jnp.broadcast_to(x[None], (count,) + x.shape).reshape((count * x.shape[0],) + x.shape[1:])


def sum_pieces(x, count):
    return jnp.sum(x.reshape((count, -1) + x.shape[1:]), axis=0)


def slab_sum(x, inner, outer):
    near, far = lax.axis_size(inner), lax.axis_size(outer)
    piece = sum_pieces(swap(x, inner), near)
    piece = sum_pieces(swap(copies(piece, far), outer), far)
    return swap(copies(piece, near), inner)


def spread(w_hi, pos):
    far = lax.ppermute(w_hi, "panel", [(0, 3), (1, 6)])
    own = jnp.where((pos == 3) | (pos == 6), far, w_hi)
    return (own,) + tuple(lax.ppermute(own, "panel", pairs) for pairs in STEPS)


def thirds(x):
    a = lax.reduce_precision(x, 8, 7)
    b = lax.reduce_precision(x - a, 8, 7)
    return jnp.concatenate([a, b, x - a - b], axis=0).astype(BF16).T


def body(vectors, hop_table, block_kind, block_phase, phase_angles, centre, half_width):
    slab = ("y", "x", "core")
    count = lax.axis_size(slab)
    kinds, phase = block_kind.T, block_phase[None, :]
    up, down = pack(vectors, kinds, phase)
    left = lax.ppermute(up, slab, [(i, i + 1) for i in range(count - 1)])
    right = lax.ppermute(down, slab, [(i + 1, i) for i in range(count - 1)])
    base = vectors / half_width[0]
    sides = jnp.concatenate([left, right], axis=0)
    wide = hop_table.astype(F32)
    turned = jnp.transpose(hop_table, (0, 2, 1))
    sym = ((wide + turned.astype(F32)) * 0.5).astype(BF16)
    cos_t = thirds(jnp.cos(phase_angles))
    sin_t = thirds(jnp.sin(phase_angles))
    w, w_hi = chebyshev(
        kinds, phase, centre, half_width, base, sides, hop_table, turned, sym, cos_t, sin_t
    )
    pos = lax.axis_index("panel").astype(jnp.int32)
    spot = pos.reshape(1)
    p01, part = gram(spot, w, spread(w_hi, pos))
    return finish(spot, slab_sum(part, ("x", "core"), "y"), w, p01)


def solution(mesh):
    panels = mesh.shape["panel"]
    devices = np.asarray(mesh.devices).reshape(8, 4, 2, panels)
    fine = Mesh(devices, ("y", "x", "core", "panel"))
    slab = ("y", "x", "core")
    in_specs = (P(slab, "panel"), P(), P(slab, None), P(slab), P(), P(), P())
    return jax.shard_map(body, mesh=fine, in_specs=in_specs, out_specs=P(slab, "panel"), check_vma=False)
```

```python
import functools

import jax
import jax.numpy as jnp
import numpy as np
from jax import lax
from jax.experimental import pallas as pl
from jax.experimental.pallas import tpu as pltpu
from jax.sharding import Mesh, PartitionSpec as P

HIGHEST = lax.Precision.HIGHEST
F32 = jnp.float32
BF16 = jnp.bfloat16
BLK = 256
WIDE = 128
HALF = 64
META = 16
MISSING = 8
STEPS = (
    [(0, 1), (3, 4), (1, 2), (6, 7)],
    [(0, 7), (3, 2), (1, 0), (6, 5)],
    [(0, 6), (3, 5), (1, 3), (6, 4)],
)
HELD = ((0, 1, 2, 0, 1, 3, 3, 2), (2, 0, 1, 3, 3, 2, 0, 1))
VM = pltpu.VMEM
SM = pltpu.SMEM


def lane_sign(first):
    lane = lax.broadcasted_iota(jnp.int32, (1, WIDE), 1)
    return jnp.where(lane < HALF, first, -first).astype(F32)


def times_i(packed):
    return lane_sign(-1.0) * pltpu.roll(packed, HALF, 1)


def dot(a, b, **kw):
    return lax.dot_general(a, b, (((1,), (0,)), ((), ())), preferred_element_type=F32, **kw)


def dot_t(a, b, **kw):
    return lax.dot_general(a, b, (((0,), (0,)), ((), ())), preferred_element_type=F32, **kw)


def split(x):
    hi = x.astype(BF16)
    return hi, (x - hi.astype(F32)).astype(BF16)


def pack_kernel(v, kinds, phase, up, down, tile):
    half = v.shape[0] // 2
    down[:half, :] = v[:half, :].astype(BF16)
    up[:half, :] = v[half:, :].astype(BF16)
    tile[...] = jnp.zeros(tile.shape, F32)
    tile[0:2, 0:4] = (kinds[...] - MISSING).astype(F32)
    tile[2:3, 0:4] = phase[...].astype(F32)
    tile[3:4, :] = jnp.ones((1, WIDE), F32)
    info = tile[...].astype(BF16)
    down[half:, :] = info
    up[half:, :] = info


def pack(v, kinds, phase):
    spec = pl.BlockSpec(memory_space=VM)
    shape = jax.ShapeDtypeStruct((v.shape[0] // 2 + META, WIDE), BF16)
    return pl.pallas_call(
        pack_kernel,
        out_shape=(shape, shape),
        in_specs=[spec] * 3,
        out_specs=(spec, spec),
        scratch_shapes=[VM((META, WIDE), F32)],
        name="pack",
    )(v, kinds, phase)


def filter_kernel(
    kinds, phase, shift, width, base, sides, hop, hop_t, sym, cos_t, sin_t,
    w, w_hi, vb, cosb, sinb, z, y1, y1b,
):
    half = base.shape[0] // 2
    left, right = sides.at[0 : half + META], sides.at[half + META :]
    centre = shift[0]
    h = jnp.broadcast_to(width[0], (1, WIDE))
    inv_h = 1.0 / h
    pick = lax.broadcasted_iota(jnp.int32, (cos_t.shape[1], WIDE), 0) % 16
    tile_l = left[half : half + META, :].astype(F32)
    tile_r = right[half : half + META, :].astype(F32)
    row = lax.broadcasted_iota(jnp.int32, (META, WIDE), 0)
    lane = lax.broadcasted_iota(jnp.int32, (META, WIDE), 1)

    def item(tile, i, j):
        return jnp.sum(jnp.where((row == i) & (lane == j), tile, 0.0)).astype(jnp.int32)

    own = {-1: item(tile_l, 0, 3) + MISSING, 4: item(tile_r, 0, 0) + MISSING}
    ahead_of = {r: item(tile_l, 1, 4 + r) + MISSING for r in (-2, -1)}
    ahead_of[4] = item(tile_r, 1, 0) + MISSING
    own.update({r: kinds[0, r] for r in range(4)})
    ahead_of.update({r: kinds[1, r] for r in range(4)})
    pattern = {r: tile_l[2:3, 4 + r : 5 + r].astype(jnp.int32) for r in (-2, -1)}
    pattern[4] = tile_r[2:3, 0:1].astype(jnp.int32)
    pattern.update({r: phase[0, r] for r in range(4)})
    has_left, has_right = tile_l[3:4, :], tile_r[3:4, :]

    def own_kind(r):
        return own[r]

    def next_kind(r):
        return ahead_of[r]

    def flag(kind):
        return jnp.where(kind < MISSING, 1.0, 0.0).astype(F32)

    for r in range(-2, 5):
        hot = jnp.where(pick == pattern[r], 1.0, 0.0).astype(BF16)
        cosb[r + 2] = dot(cos_t[...], hot)
        sinb[r + 2] = dot(sin_t[...], hot)

    def v_row(r):
        if r < 0:
            return left[(r + 2) * BLK : (r + 3) * BLK, :]
        if r > 3:
            return right[(r - 4) * BLK : (r - 3) * BLK, :]
        return vb[r * BLK : (r + 1) * BLK, :]

    def y_row(r):
        return y1b[r + 1]

    def back_phase(x, r):
        x = x.astype(F32)
        return (cosb[r + 2] * x - sinb[r + 2] * times_i(x)).astype(BF16)

    def hop_row(r, row):
        ko, kn, kb = own_kind(r), next_kind(r), next_kind(r - 1)
        total = flag(ko) * dot(sym[jnp.minimum(ko, 7)], row(r))
        ahead = flag(kn) * dot(hop[jnp.minimum(kn, 7)], row(r + 1))
        total += cosb[r + 2] * ahead + sinb[r + 2] * times_i(ahead)
        return total + flag(kb) * dot(hop_t[jnp.minimum(kb, 7)], z[r + 1])

    vb[...] = (h * base[...]).astype(BF16)
    for r in range(-2, 4):
        z[r + 2] = back_phase(v_row(r), r)
    for r in range(-1, 5):
        scaled = base[r * BLK : (r + 1) * BLK, :] if 0 <= r < 4 else v_row(r).astype(F32) * inv_h
        y = hop_row(r, v_row) * inv_h - centre * scaled
        if r == -1:
            y = y * has_left
        if r == 4:
            y = y * has_right
        if 0 <= r < 4:
            y1[r] = y
        y1b[r + 1] = y.astype(BF16)
    for r in range(-1, 4):
        z[r + 2] = back_phase(y_row(r), r)
    for r in range(4):
        y = (2.0 * inv_h) * (hop_row(r, y_row) - centre * y1[r]) - h * base[r * BLK : (r + 1) * BLK, :]
        w[r * BLK : (r + 1) * BLK, :] = y
        w_hi[r * BLK : (r + 1) * BLK, :] = y.astype(BF16)


def chebyshev(*args):
    spec = pl.BlockSpec(memory_space=VM)
    smem = pl.BlockSpec(memory_space=SM)
    return pl.pallas_call(
        filter_kernel,
        out_shape=(jax.ShapeDtypeStruct(args[4].shape, F32), jax.ShapeDtypeStruct(args[4].shape, BF16)),
        in_specs=[smem] * 4 + [spec] * 7,
        out_specs=(spec, spec),
        scratch_shapes=[
            VM(args[4].shape, BF16),
            VM((7, BLK, WIDE), F32),
            VM((7, BLK, WIDE), F32),
            VM((6, BLK, WIDE), BF16),
            VM((4, BLK, WIDE), F32),
            VM((6, BLK, WIDE), BF16),
        ],
        compiler_params=pltpu.CompilerParams(vmem_limit_bytes=16 << 20),
        name="chebyshev",
    )(*args)


def gram_kernel(pos, w, own, first, second, third, p01, out):
    which = pos[0]
    for src, ref in enumerate((own, first, second, third)):
        for panel in range(2):
            here = [z for z in range(8) if HELD[panel][z] == src]
            hit = functools.reduce(jnp.logical_or, [which == z for z in here])

            @pl.when(hit)
            def _(ref=ref, panel=panel):
                p01[:, panel * WIDE : (panel + 1) * WIDE] = ref[...]

    both = p01[...]
    w_hi, w_lo = split(w[...])
    prod = dot_t(both, jnp.concatenate([both, w_hi, w_lo], 1))

    def inner(a, b):
        d = prod[a * WIDE : (a + 1) * WIDE, b * WIDE : (b + 1) * WIDE]
        return d[:HALF] + lane_sign(1.0) * pltpu.roll(d[HALF:], HALF, 1)

    row = lax.broadcasted_iota(jnp.int32, (HALF, WIDE), 0)
    lane = lax.broadcasted_iota(jnp.int32, (HALF, WIDE), 1)
    col = jnp.where(lane < HALF, lane, lane - HALF)
    g00, g11 = inner(0, 0), inner(1, 1)
    diag = jnp.where(lane < HALF, g00, pltpu.roll(g11, HALF, 1))
    out[0:HALF, :] = jnp.where(col > row, g00, jnp.where(col < row, g11, diag)).astype(BF16)
    out[HALF : 2 * HALF, :] = inner(0, 1).astype(BF16)
    out[2 * HALF : 3 * HALF, :] = (inner(0, 2) + inner(0, 3)).astype(BF16)
    out[3 * HALF : 4 * HALF, :] = (inner(1, 2) + inner(1, 3)).astype(BF16)


def gram(pos, w, parts):
    spec = pl.BlockSpec(memory_space=VM)
    return pl.pallas_call(
        gram_kernel,
        out_shape=(
            jax.ShapeDtypeStruct((w.shape[0], 2 * WIDE), BF16),
            jax.ShapeDtypeStruct((4 * HALF, WIDE), BF16),
        ),
        in_specs=[pl.BlockSpec(memory_space=SM)] + [spec] * 5,
        out_specs=(spec, spec),
        compiler_params=pltpu.CompilerParams(vmem_limit_bytes=16 << 20),
        name="gram",
    )(pos, w, *parts)


def inverse_factor(tr, ti):
    tiles = WIDE // 8
    re = [tr[8 * t : 8 * t + 8] for t in range(tiles)]
    im = [ti[8 * t : 8 * t + 8] for t in range(tiles)]
    lane = lax.broadcasted_iota(jnp.int32, (8, WIDE), 1)
    sub = lax.broadcasted_iota(jnp.int32, (8, WIDE), 0)
    for k in range(WIDE):
        g, j = divmod(k, 8)
        at_k = lane == k
        row_r = re[g][j : j + 1]
        row_i = im[g][j : j + 1]
        inv = 1.0 / jnp.broadcast_to(row_r[:, k : k + 1], (1, WIDE))
        row_r = jnp.where(at_k[:1], 1.0, row_r) * inv
        row_i = jnp.where(at_k[:1], 0.0, row_i) * inv
        row_r = jnp.broadcast_to(row_r, (8, WIDE))
        row_i = jnp.broadcast_to(row_i, (8, WIDE))
        for t in range(g, tiles):
            if t == g and j == 7:
                continue
            cr = jnp.broadcast_to(re[t][:, k : k + 1], (8, WIDE))
            ci = jnp.broadcast_to(im[t][:, k : k + 1], (8, WIDE))
            keep_r = jnp.where(at_k, 0.0, re[t])
            keep_i = jnp.where(at_k, 0.0, im[t])
            new_r = keep_r - (cr * row_r - ci * row_i)
            new_i = keep_i - (cr * row_i + ci * row_r)
            if t == g:
                new_r = jnp.where(sub > j, new_r, re[t])
                new_i = jnp.where(sub > j, new_i, im[t])
            re[t], im[t] = new_r, new_i
    out_r, out_i = [], []
    for t in range(tiles):
        diag = lane == sub + 8 * t
        below = lane < sub + 8 * t
        pivot = jnp.sum(jnp.where(diag, re[t], 0.0), axis=1, keepdims=True)
        scale = lax.rsqrt(pivot)
        out_r.append(jnp.where(diag, 1.0, jnp.where(below, re[t], 0.0)) * scale)
        out_i.append(jnp.where(below, im[t], 0.0) * scale)
    return jnp.concatenate(out_r, 0), jnp.concatenate(out_i, 0)


def wide_dot(x, y):
    return split_dot(split(x), split(y))


def split_dot(x, y):
    (xh, xl), (yh, yl) = x, y
    return dot(xh, yh) + (dot(xh, yl) + dot(xl, yh))


def pair(re, im):
    return jnp.concatenate([jnp.concatenate([re, im], 1), jnp.concatenate([-im, re], 1)], 0)


def refine(tr, ti, root):
    row = lax.broadcasted_iota(jnp.int32, (WIDE, WIDE), 0)
    col = lax.broadcasted_iota(jnp.int32, (WIDE, WIDE), 1)
    one = jnp.where(row == col, 1.0, 0.0)
    weight = jnp.where(col < row, 1.0, 0.5 * one)
    down = lax.rsqrt(jnp.sum(one * tr, axis=1, keepdims=True))
    across = lax.rsqrt(jnp.sum(one * tr, axis=0, keepdims=True))
    ar, ai = tr * down * across, ti * down * across
    unit = split(pair(ar, ai))
    root[:, :WIDE] = one - jnp.where(col < row, ar, 0.0)
    root[:, WIDE:] = -jnp.where(col < row, ai, 0.0)

    def cond(carry):
        step, size = carry
        return (step < 8) & (size > 1e-5) & (size < 1.0)

    def step(carry):
        count, _ = carry
        r = root[...]
        half = split_dot(split(r), unit)
        rt, it = jnp.transpose(r[:, :WIDE]), jnp.transpose(r[:, WIDE:])
        e = wide_dot(half, pair(rt, -it))
        er, ei = e[:, :WIDE] - one, e[:, WIDE:]
        size = jnp.sum(er * er + ei * ei)
        fix = jnp.concatenate([weight * er, weight * ei], 1)
        root[...] = r - wide_dot(fix, pair(r[:, :WIDE], r[:, WIDE:]))
        return count + 1, size

    count, size = lax.while_loop(cond, step, (jnp.int32(0), jnp.float32(0.5)))
    good = size <= 1e-5

    @pl.when(good)
    def _():
        root[:, :WIDE] = root[:, :WIDE] * across
        root[:, WIDE:] = root[:, WIDE:] * across

    @pl.when(jnp.logical_not(good))
    def _():
        re, im = inverse_factor(tr, ti)
        root[:, :WIDE] = re
        root[:, WIDE:] = im


def embed(block):
    return jnp.concatenate([block, times_i(block)], 0)


def finish_kernel(pos, g, w, p01, out, root):
    row = lax.broadcasted_iota(jnp.int32, (HALF, WIDE), 0)
    lane = lax.broadcasted_iota(jnp.int32, (HALF, WIDE), 1)
    left = lane < HALF
    col = jnp.where(left, lane, lane - HALF)
    c, g01 = g[0:HALF, :], g[HALF : 2 * HALF, :]
    c_turn, g01_turn = pltpu.roll(c, HALF, 1), pltpu.roll(g01, HALF, 1)
    above, below, diag = col > row, col < row, col == row

    def stack(top_left, top_right, low_right):
        return jnp.concatenate([jnp.where(left, top_left, top_right), jnp.where(left, 0.0, low_right)], 0)

    once_r = stack(jnp.where(above, c, 0.0), g01_turn, jnp.where(below, c_turn, 0.0))
    once_i = stack(jnp.where(above, c_turn, 0.0), g01, jnp.where(below, c, 0.0))
    pivots = jnp.where(diag, c, 0.0)
    tr = once_r + jnp.transpose(once_r) + stack(pivots, 0.0, pivots)
    ti = once_i - jnp.transpose(once_i)
    refine(tr, ti, root)
    rr, ri = root[:, :WIDE], root[:, WIDE:]
    which = pos[0]

    @pl.when(which >= 2)
    def _():
        m = g[2 * HALF : 4 * HALF, :]
        n = wide_dot(root[...], embed(m))
        k = wide_dot(jnp.concatenate([jnp.transpose(rr), -jnp.transpose(ri)], 1), embed(n))
        e_hi, e_lo = split(jnp.concatenate([embed(k[:HALF]), embed(k[HALF:])], 0))
        out[...] = w[...] - (dot(p01[...], e_hi) + dot(p01[...], e_lo))

    @pl.when(which < 2)
    def _():
        rt, it = jnp.transpose(rr), jnp.transpose(ri)
        full = lax.broadcasted_iota(jnp.int32, (WIDE, WIDE), 1) < HALF
        first = jnp.where(full, rt, -pltpu.roll(it, HALF, 1))
        second = jnp.where(full, pltpu.roll(rt, HALF, 1), -it)
        is_first = which == 0
        own = jnp.where(is_first, first[:HALF], second[HALF:])
        other = jnp.where(is_first, 0.0, second[:HALF])
        o_hi, o_lo = split(embed(other))
        p0 = p01[:, :WIDE]
        out[...] = dot(w[...], embed(own), precision=HIGHEST) + dot(p0, o_hi) + dot(p0, o_lo)


def finish(pos, g, w, p01):
    spec = pl.BlockSpec(memory_space=VM)
    return pl.pallas_call(
        finish_kernel,
        out_shape=jax.ShapeDtypeStruct(w.shape, F32),
        in_specs=[pl.BlockSpec(memory_space=SM), spec, spec, spec],
        out_specs=spec,
        scratch_shapes=[VM((WIDE, 2 * WIDE), F32)],
        compiler_params=pltpu.CompilerParams(vmem_limit_bytes=16 << 20),
        name="finish",
    )(pos, g, w, p01)


def swap(x, axes):
    return lax.all_to_all(x, axes, 0, 0, tiled=True)


def copies(x, count):
    return jnp.broadcast_to(x[None], (count,) + x.shape).reshape((count * x.shape[0],) + x.shape[1:])


def sum_pieces(x, count):
    return jnp.sum(x.reshape((count, -1) + x.shape[1:]).astype(F32), axis=0)


def slab_sum(x, inner, outer):
    near, far = lax.axis_size(inner), lax.axis_size(outer)
    piece = sum_pieces(swap(x, inner), near)
    piece = sum_pieces(swap(copies(piece, far), outer), far)
    return swap(copies(piece, near), inner)


def spread(w_hi, pos):
    far = lax.ppermute(w_hi, "panel", [(0, 3), (1, 6)])
    own = jnp.where((pos == 3) | (pos == 6), far, w_hi)
    return (own,) + tuple(lax.ppermute(own, "panel", pairs) for pairs in STEPS)


def thirds(x):
    a = lax.reduce_precision(x, 8, 7)
    b = lax.reduce_precision(x - a, 8, 7)
    return jnp.concatenate([a, b, x - a - b], axis=0).astype(BF16).T


def body(vectors, hop_table, block_kind, block_phase, phase_angles, centre, half_width):
    slab = ("y", "x", "core")
    count = lax.axis_size(slab)
    kinds, phase = block_kind.T, block_phase[None, :]
    up, down = pack(vectors, kinds, phase)
    left = lax.ppermute(up, slab, [(i, i + 1) for i in range(count - 1)])
    right = lax.ppermute(down, slab, [(i + 1, i) for i in range(count - 1)])
    base = vectors / half_width[0]
    sides = jnp.concatenate([left, right], axis=0)
    wide = hop_table.astype(F32)
    turned = jnp.transpose(hop_table, (0, 2, 1))
    sym = ((wide + turned.astype(F32)) * 0.5).astype(BF16)
    cos_t = thirds(jnp.cos(phase_angles))
    sin_t = thirds(jnp.sin(phase_angles))
    w, w_hi = chebyshev(
        kinds, phase, centre, half_width, base, sides, hop_table, turned, sym, cos_t, sin_t
    )
    pos = lax.axis_index("panel").astype(jnp.int32)
    spot = pos.reshape(1)
    p01, part = gram(spot, w, spread(w_hi, pos))
    return finish(spot, slab_sum(part, ("x", "core"), "y"), w, p01)


def solution(mesh):
    panels = mesh.shape["panel"]
    devices = np.asarray(mesh.devices).reshape(8, 4, 2, panels)
    fine = Mesh(devices, ("y", "x", "core", "panel"))
    slab = ("y", "x", "core")
    in_specs = (P(slab, "panel"), P(), P(slab, None), P(slab), P(), P(), P())
    return jax.shard_map(body, mesh=fine, in_specs=in_specs, out_specs=P(slab, "panel"), check_vma=False)
```

```python
import functools

import jax
import jax.numpy as jnp
import numpy as np
from jax import lax
from jax.experimental import pallas as pl
from jax.experimental.pallas import tpu as pltpu
from jax.sharding import Mesh, PartitionSpec as P

HIGHEST = lax.Precision.HIGHEST
F32 = jnp.float32
BF16 = jnp.bfloat16
BLK = 256
WIDE = 128
HALF = 64
META = 16
MISSING = 8
STEPS = (
    [(0, 6), (3, 5), (1, 3), (6, 4)],
    [(0, 1), (3, 4), (1, 2), (6, 7)],
    [(0, 7), (3, 2), (1, 0), (6, 5)],
)
HELD = ((0, 2, 3, 0, 2, 1, 1, 3), (3, 0, 2, 1, 1, 3, 0, 2))
VM = pltpu.VMEM
SM = pltpu.SMEM


def lane_sign(first):
    lane = lax.broadcasted_iota(jnp.int32, (1, WIDE), 1)
    return jnp.where(lane < HALF, first, -first).astype(F32)


def times_i(packed):
    return lane_sign(-1.0) * pltpu.roll(packed, HALF, 1)


def dot(a, b, **kw):
    return lax.dot_general(a, b, (((1,), (0,)), ((), ())), preferred_element_type=F32, **kw)


def dot_t(a, b, **kw):
    return lax.dot_general(a, b, (((0,), (0,)), ((), ())), preferred_element_type=F32, **kw)


def split(x):
    hi = x.astype(BF16)
    return hi, (x - hi.astype(F32)).astype(BF16)


def pack_kernel(v, kinds, phase, up, down, tile):
    half = v.shape[0] // 2
    down[:half, :] = v[:half, :].astype(BF16)
    up[:half, :] = v[half:, :].astype(BF16)
    tile[...] = jnp.zeros(tile.shape, F32)
    tile[0:2, 0:4] = (kinds[...] - MISSING).astype(F32)
    tile[2:3, 0:4] = phase[...].astype(F32)
    tile[3:4, :] = jnp.ones((1, WIDE), F32)
    info = tile[...].astype(BF16)
    down[half:, :] = info
    up[half:, :] = info


def pack(v, kinds, phase):
    spec = pl.BlockSpec(memory_space=VM)
    shape = jax.ShapeDtypeStruct((v.shape[0] // 2 + META, WIDE), BF16)
    return pl.pallas_call(
        pack_kernel,
        out_shape=(shape, shape),
        in_specs=[spec] * 3,
        out_specs=(spec, spec),
        scratch_shapes=[VM((META, WIDE), F32)],
        name="pack",
    )(v, kinds, phase)


def filter_kernel(
    kinds, phase, shift, width, base, sides, hop, hop_t, sym, cos_t, sin_t,
    w, w_hi, vb, cosb, sinb, z, y1, y1b,
):
    half = base.shape[0] // 2
    left, right = sides.at[0 : half + META], sides.at[half + META :]
    centre = shift[0]
    h = jnp.broadcast_to(width[0], (1, WIDE))
    inv_h = 1.0 / h
    pick = lax.broadcasted_iota(jnp.int32, (cos_t.shape[1], WIDE), 0) % 16
    tile_l = left[half : half + META, :].astype(F32)
    tile_r = right[half : half + META, :].astype(F32)
    row = lax.broadcasted_iota(jnp.int32, (META, WIDE), 0)
    lane = lax.broadcasted_iota(jnp.int32, (META, WIDE), 1)

    def item(tile, i, j):
        return jnp.sum(jnp.where((row == i) & (lane == j), tile, 0.0)).astype(jnp.int32)

    own = {-1: item(tile_l, 0, 3) + MISSING, 4: item(tile_r, 0, 0) + MISSING}
    ahead_of = {r: item(tile_l, 1, 4 + r) + MISSING for r in (-2, -1)}
    ahead_of[4] = item(tile_r, 1, 0) + MISSING
    own.update({r: kinds[0, r] for r in range(4)})
    ahead_of.update({r: kinds[1, r] for r in range(4)})
    pattern = {r: tile_l[2:3, 4 + r : 5 + r].astype(jnp.int32) for r in (-2, -1)}
    pattern[4] = tile_r[2:3, 0:1].astype(jnp.int32)
    pattern.update({r: phase[0, r] for r in range(4)})
    has_left, has_right = tile_l[3:4, :], tile_r[3:4, :]

    def own_kind(r):
        return own[r]

    def next_kind(r):
        return ahead_of[r]

    def flag(kind):
        return jnp.where(kind < MISSING, 1.0, 0.0).astype(F32)

    for r in range(-2, 5):
        hot = jnp.where(pick == pattern[r], 1.0, 0.0).astype(BF16)
        cosb[r + 2] = dot(cos_t[...], hot)
        sinb[r + 2] = dot(sin_t[...], hot)

    def v_row(r):
        if r < 0:
            return left[(r + 2) * BLK : (r + 3) * BLK, :]
        if r > 3:
            return right[(r - 4) * BLK : (r - 3) * BLK, :]
        return vb[r * BLK : (r + 1) * BLK, :]

    def y_row(r):
        return y1b[r + 1]

    def back_phase(x, r):
        x = x.astype(F32)
        return (cosb[r + 2] * x - sinb[r + 2] * times_i(x)).astype(BF16)

    def hop_row(r, row):
        ko, kn, kb = own_kind(r), next_kind(r), next_kind(r - 1)
        total = flag(ko) * dot(sym[jnp.minimum(ko, 7)], row(r))
        ahead = flag(kn) * dot(hop[jnp.minimum(kn, 7)], row(r + 1))
        total += cosb[r + 2] * ahead + sinb[r + 2] * times_i(ahead)
        return total + flag(kb) * dot(hop_t[jnp.minimum(kb, 7)], z[r + 1])

    vb[...] = (h * base[...]).astype(BF16)
    for r in range(-2, 4):
        z[r + 2] = back_phase(v_row(r), r)
    for r in range(-1, 5):
        scaled = base[r * BLK : (r + 1) * BLK, :] if 0 <= r < 4 else v_row(r).astype(F32) * inv_h
        y = hop_row(r, v_row) * inv_h - centre * scaled
        if r == -1:
            y = y * has_left
        if r == 4:
            y = y * has_right
        if 0 <= r < 4:
            y1[r] = y
        y1b[r + 1] = y.astype(BF16)
    for r in range(-1, 4):
        z[r + 2] = back_phase(y_row(r), r)
    for r in range(4):
        y = (2.0 * inv_h) * (hop_row(r, y_row) - centre * y1[r]) - h * base[r * BLK : (r + 1) * BLK, :]
        w[r * BLK : (r + 1) * BLK, :] = y
        w_hi[r * BLK : (r + 1) * BLK, :] = y.astype(BF16)


def chebyshev(*args):
    spec = pl.BlockSpec(memory_space=VM)
    smem = pl.BlockSpec(memory_space=SM)
    return pl.pallas_call(
        filter_kernel,
        out_shape=(jax.ShapeDtypeStruct(args[4].shape, F32), jax.ShapeDtypeStruct(args[4].shape, BF16)),
        in_specs=[smem] * 4 + [spec] * 7,
        out_specs=(spec, spec),
        scratch_shapes=[
            VM(args[4].shape, BF16),
            VM((7, BLK, WIDE), F32),
            VM((7, BLK, WIDE), F32),
            VM((6, BLK, WIDE), BF16),
            VM((4, BLK, WIDE), F32),
            VM((6, BLK, WIDE), BF16),
        ],
        compiler_params=pltpu.CompilerParams(vmem_limit_bytes=16 << 20),
        name="chebyshev",
    )(*args)


def gram_kernel(pos, w, own, first, second, third, p01, out):
    which = pos[0]
    for src, ref in enumerate((own, first, second, third)):
        for panel in range(2):
            here = [z for z in range(8) if HELD[panel][z] == src]
            hit = functools.reduce(jnp.logical_or, [which == z for z in here])

            @pl.when(hit)
            def _(ref=ref, panel=panel):
                p01[:, panel * WIDE : (panel + 1) * WIDE] = ref[...]

    both = p01[...]
    w_hi, w_lo = split(w[...])
    prod = dot_t(both, jnp.concatenate([both, w_hi, w_lo], 1))

    def inner(a, b):
        d = prod[a * WIDE : (a + 1) * WIDE, b * WIDE : (b + 1) * WIDE]
        return d[:HALF] + lane_sign(1.0) * pltpu.roll(d[HALF:], HALF, 1)

    row = lax.broadcasted_iota(jnp.int32, (HALF, WIDE), 0)
    lane = lax.broadcasted_iota(jnp.int32, (HALF, WIDE), 1)
    col = jnp.where(lane < HALF, lane, lane - HALF)
    g00, g11 = inner(0, 0), inner(1, 1)
    diag = jnp.where(lane < HALF, g00, pltpu.roll(g11, HALF, 1))
    out[0:HALF, :] = jnp.where(col > row, g00, jnp.where(col < row, g11, diag))
    out[HALF : 2 * HALF, :] = inner(0, 1)
    out[2 * HALF : 3 * HALF, :] = inner(0, 2) + inner(0, 3)
    out[3 * HALF : 4 * HALF, :] = inner(1, 2) + inner(1, 3)


def gram(pos, w, parts):
    spec = pl.BlockSpec(memory_space=VM)
    return pl.pallas_call(
        gram_kernel,
        out_shape=(
            jax.ShapeDtypeStruct((w.shape[0], 2 * WIDE), BF16),
            jax.ShapeDtypeStruct((4 * HALF, WIDE), F32),
        ),
        in_specs=[pl.BlockSpec(memory_space=SM)] + [spec] * 5,
        out_specs=(spec, spec),
        compiler_params=pltpu.CompilerParams(vmem_limit_bytes=16 << 20),
        name="gram",
    )(pos, w, *parts)


def inverse_factor(tr, ti):
    tiles = WIDE // 8
    re = [tr[8 * t : 8 * t + 8] for t in range(tiles)]
    im = [ti[8 * t : 8 * t + 8] for t in range(tiles)]
    lane = lax.broadcasted_iota(jnp.int32, (8, WIDE), 1)
    sub = lax.broadcasted_iota(jnp.int32, (8, WIDE), 0)
    for k in range(WIDE):
        g, j = divmod(k, 8)
        at_k = lane == k
        row_r = re[g][j : j + 1]
        row_i = im[g][j : j + 1]
        inv = 1.0 / jnp.broadcast_to(row_r[:, k : k + 1], (1, WIDE))
        row_r = jnp.where(at_k[:1], 1.0, row_r) * inv
        row_i = jnp.where(at_k[:1], 0.0, row_i) * inv
        row_r = jnp.broadcast_to(row_r, (8, WIDE))
        row_i = jnp.broadcast_to(row_i, (8, WIDE))
        for t in range(g, tiles):
            if t == g and j == 7:
                continue
            cr = jnp.broadcast_to(re[t][:, k : k + 1], (8, WIDE))
            ci = jnp.broadcast_to(im[t][:, k : k + 1], (8, WIDE))
            keep_r = jnp.where(at_k, 0.0, re[t])
            keep_i = jnp.where(at_k, 0.0, im[t])
            new_r = keep_r - (cr * row_r - ci * row_i)
            new_i = keep_i - (cr * row_i + ci * row_r)
            if t == g:
                new_r = jnp.where(sub > j, new_r, re[t])
                new_i = jnp.where(sub > j, new_i, im[t])
            re[t], im[t] = new_r, new_i
    out_r, out_i = [], []
    for t in range(tiles):
        diag = lane == sub + 8 * t
        below = lane < sub + 8 * t
        pivot = jnp.sum(jnp.where(diag, re[t], 0.0), axis=1, keepdims=True)
        scale = lax.rsqrt(pivot)
        out_r.append(jnp.where(diag, 1.0, jnp.where(below, re[t], 0.0)) * scale)
        out_i.append(jnp.where(below, im[t], 0.0) * scale)
    return jnp.concatenate(out_r, 0), jnp.concatenate(out_i, 0)


def wide_dot(x, y):
    return split_dot(split(x), split(y))


def split_dot(x, y):
    (xh, xl), (yh, yl) = x, y
    return dot(xh, yh) + (dot(xh, yl) + dot(xl, yh))


def pair(re, im):
    return jnp.concatenate([jnp.concatenate([re, im], 1), jnp.concatenate([-im, re], 1)], 0)


def refine(tr, ti, root):
    row = lax.broadcasted_iota(jnp.int32, (WIDE, WIDE), 0)
    col = lax.broadcasted_iota(jnp.int32, (WIDE, WIDE), 1)
    one = jnp.where(row == col, 1.0, 0.0)
    weight = jnp.where(col < row, 1.0, 0.5 * one)
    down = lax.rsqrt(jnp.sum(one * tr, axis=1, keepdims=True))
    across = lax.rsqrt(jnp.sum(one * tr, axis=0, keepdims=True))
    ar, ai = tr * down * across, ti * down * across
    unit = split(pair(ar, ai))
    root[:, :WIDE] = one - jnp.where(col < row, ar, 0.0)
    root[:, WIDE:] = -jnp.where(col < row, ai, 0.0)

    def cond(carry):
        step, size = carry
        return (step < 8) & (size > 1e-5) & (size < 1.0)

    def step(carry):
        count, _ = carry
        r = root[...]
        half = split_dot(split(r), unit)
        rt, it = jnp.transpose(r[:, :WIDE]), jnp.transpose(r[:, WIDE:])
        e = wide_dot(half, pair(rt, -it))
        er, ei = e[:, :WIDE] - one, e[:, WIDE:]
        size = jnp.sum(er * er + ei * ei)
        fix = jnp.concatenate([weight * er, weight * ei], 1)
        root[...] = r - wide_dot(fix, pair(r[:, :WIDE], r[:, WIDE:]))
        return count + 1, size

    count, size = lax.while_loop(cond, step, (jnp.int32(0), jnp.float32(0.5)))
    good = size <= 1e-5

    @pl.when(good)
    def _():
        root[:, :WIDE] = root[:, :WIDE] * across
        root[:, WIDE:] = root[:, WIDE:] * across

    @pl.when(jnp.logical_not(good))
    def _():
        re, im = inverse_factor(tr, ti)
        root[:, :WIDE] = re
        root[:, WIDE:] = im


def embed(block):
    return jnp.concatenate([block, times_i(block)], 0)


def finish_kernel(pos, g, w, p01, out, root):
    row = lax.broadcasted_iota(jnp.int32, (HALF, WIDE), 0)
    lane = lax.broadcasted_iota(jnp.int32, (HALF, WIDE), 1)
    left = lane < HALF
    col = jnp.where(left, lane, lane - HALF)
    c, g01 = g[0:HALF, :], g[HALF : 2 * HALF, :]
    c_turn, g01_turn = pltpu.roll(c, HALF, 1), pltpu.roll(g01, HALF, 1)
    above, below, diag = col > row, col < row, col == row

    def stack(top_left, top_right, low_right):
        return jnp.concatenate([jnp.where(left, top_left, top_right), jnp.where(left, 0.0, low_right)], 0)

    once_r = stack(jnp.where(above, c, 0.0), g01_turn, jnp.where(below, c_turn, 0.0))
    once_i = stack(jnp.where(above, c_turn, 0.0), g01, jnp.where(below, c, 0.0))
    pivots = jnp.where(diag, c, 0.0)
    tr = once_r + jnp.transpose(once_r) + stack(pivots, 0.0, pivots)
    ti = once_i - jnp.transpose(once_i)
    refine(tr, ti, root)
    rr, ri = root[:, :WIDE], root[:, WIDE:]
    which = pos[0]

    @pl.when(which >= 2)
    def _():
        m = g[2 * HALF : 4 * HALF, :]
        n = wide_dot(root[...], embed(m))
        k = wide_dot(jnp.concatenate([jnp.transpose(rr), -jnp.transpose(ri)], 1), embed(n))
        e_hi, e_lo = split(jnp.concatenate([embed(k[:HALF]), embed(k[HALF:])], 0))
        out[...] = w[...] - (dot(p01[...], e_hi) + dot(p01[...], e_lo))

    @pl.when(which < 2)
    def _():
        rt, it = jnp.transpose(rr), jnp.transpose(ri)
        full = lax.broadcasted_iota(jnp.int32, (WIDE, WIDE), 1) < HALF
        first = jnp.where(full, rt, -pltpu.roll(it, HALF, 1))
        second = jnp.where(full, pltpu.roll(rt, HALF, 1), -it)
        is_first = which == 0
        own = jnp.where(is_first, first[:HALF], second[HALF:])
        other = jnp.where(is_first, 0.0, second[:HALF])
        o_hi, o_lo = split(embed(other))
        p0 = p01[:, :WIDE]
        out[...] = dot(w[...], embed(own), precision=HIGHEST) + dot(p0, o_hi) + dot(p0, o_lo)


def finish(pos, g, w, p01):
    spec = pl.BlockSpec(memory_space=VM)
    return pl.pallas_call(
        finish_kernel,
        out_shape=jax.ShapeDtypeStruct(w.shape, F32),
        in_specs=[pl.BlockSpec(memory_space=SM), spec, spec, spec],
        out_specs=spec,
        scratch_shapes=[VM((WIDE, 2 * WIDE), F32)],
        compiler_params=pltpu.CompilerParams(vmem_limit_bytes=16 << 20),
        name="finish",
    )(pos, g, w, p01)


def swap(x, axes):
    return lax.all_to_all(x, axes, 0, 0, tiled=True)


def copies(x, count):
    return jnp.broadcast_to(x[None], (count,) + x.shape).reshape((count * x.shape[0],) + x.shape[1:])


def sum_pieces(x, count):
    return jnp.sum(x.reshape((count, -1) + x.shape[1:]), axis=0)


def slab_sum(x, inner, outer):
    near, far = lax.axis_size(inner), lax.axis_size(outer)
    piece = sum_pieces(swap(x, inner), near)
    piece = sum_pieces(swap(copies(piece, far), outer), far)
    return swap(copies(piece, near), inner)


def spread(w_hi, pos):
    far = lax.ppermute(w_hi, "panel", [(0, 3), (1, 6)])
    own = jnp.where((pos == 3) | (pos == 6), far, w_hi)
    return (own,) + tuple(lax.ppermute(own, "panel", pairs) for pairs in STEPS)


def thirds(x):
    a = lax.reduce_precision(x, 8, 7)
    b = lax.reduce_precision(x - a, 8, 7)
    return jnp.concatenate([a, b, x - a - b], axis=0).astype(BF16).T


def body(vectors, hop_table, block_kind, block_phase, phase_angles, centre, half_width):
    slab = ("y", "x", "core")
    count = lax.axis_size(slab)
    kinds, phase = block_kind.T, block_phase[None, :]
    up, down = pack(vectors, kinds, phase)
    left = lax.ppermute(up, slab, [(i, i + 1) for i in range(count - 1)])
    right = lax.ppermute(down, slab, [(i + 1, i) for i in range(count - 1)])
    base = vectors / half_width[0]
    sides = jnp.concatenate([left, right], axis=0)
    wide = hop_table.astype(F32)
    turned = jnp.transpose(hop_table, (0, 2, 1))
    sym = ((wide + turned.astype(F32)) * 0.5).astype(BF16)
    cos_t = thirds(jnp.cos(phase_angles))
    sin_t = thirds(jnp.sin(phase_angles))
    w, w_hi = chebyshev(
        kinds, phase, centre, half_width, base, sides, hop_table, turned, sym, cos_t, sin_t
    )
    pos = lax.axis_index("panel").astype(jnp.int32)
    spot = pos.reshape(1)
    p01, part = gram(spot, w, spread(w_hi, pos))
    return finish(spot, slab_sum(part, ("x", "core"), "y"), w, p01)


def solution(mesh):
    panels = mesh.shape["panel"]
    devices = np.asarray(mesh.devices).reshape(8, 4, 2, panels)
    fine = Mesh(devices, ("y", "x", "core", "panel"))
    slab = ("y", "x", "core")
    in_specs = (P(slab, "panel"), P(), P(slab, None), P(slab), P(), P(), P())
    return jax.shard_map(body, mesh=fine, in_specs=in_specs, out_specs=P(slab, "panel"), check_vma=False)
```

```python
import functools

import jax
import jax.numpy as jnp
import numpy as np
from jax import lax
from jax.experimental import pallas as pl
from jax.experimental.pallas import tpu as pltpu
from jax.sharding import Mesh, PartitionSpec as P

HIGHEST = lax.Precision.HIGHEST
F32 = jnp.float32
BF16 = jnp.bfloat16
BLK = 256
WIDE = 128
HALF = 64
META = 16
MISSING = 8
STEPS = (
    [(0, 7), (3, 4), (1, 2), (6, 5)],
    [(0, 1), (3, 2), (1, 0), (6, 7)],
    [(0, 6), (3, 5), (1, 3), (6, 4)],
)
HELD = ((0, 2, 2, 0, 1, 3, 3, 1), (2, 0, 1, 3, 3, 1, 0, 2))
VM = pltpu.VMEM
SM = pltpu.SMEM


def lane_sign(first):
    lane = lax.broadcasted_iota(jnp.int32, (1, WIDE), 1)
    return jnp.where(lane < HALF, first, -first).astype(F32)


def times_i(packed):
    return lane_sign(-1.0) * pltpu.roll(packed, HALF, 1)


def dot(a, b, **kw):
    return lax.dot_general(a, b, (((1,), (0,)), ((), ())), preferred_element_type=F32, **kw)


def dot_t(a, b, **kw):
    return lax.dot_general(a, b, (((0,), (0,)), ((), ())), preferred_element_type=F32, **kw)


def split(x):
    hi = x.astype(BF16)
    return hi, (x - hi.astype(F32)).astype(BF16)


def pack_kernel(v, kinds, phase, up, down, tile):
    half = v.shape[0] // 2
    down[:half, :] = v[:half, :].astype(BF16)
    up[:half, :] = v[half:, :].astype(BF16)
    tile[...] = jnp.zeros(tile.shape, F32)
    tile[0:2, 0:4] = (kinds[...] - MISSING).astype(F32)
    tile[2:3, 0:4] = phase[...].astype(F32)
    tile[3:4, :] = jnp.ones((1, WIDE), F32)
    info = tile[...].astype(BF16)
    down[half:, :] = info
    up[half:, :] = info


def pack(v, kinds, phase):
    spec = pl.BlockSpec(memory_space=VM)
    shape = jax.ShapeDtypeStruct((v.shape[0] // 2 + META, WIDE), BF16)
    return pl.pallas_call(
        pack_kernel,
        out_shape=(shape, shape),
        in_specs=[spec] * 3,
        out_specs=(spec, spec),
        scratch_shapes=[VM((META, WIDE), F32)],
        name="pack",
    )(v, kinds, phase)


def filter_kernel(
    kinds, phase, shift, width, base, sides, hop, hop_t, sym, cos_t, sin_t,
    w, w_hi, vb, cosb, sinb, z, y1, y1b,
):
    half = base.shape[0] // 2
    left, right = sides.at[0 : half + META], sides.at[half + META :]
    centre = shift[0]
    h = jnp.broadcast_to(width[0], (1, WIDE))
    inv_h = 1.0 / h
    pick = lax.broadcasted_iota(jnp.int32, (cos_t.shape[1], WIDE), 0) % 16
    tile_l = left[half : half + META, :].astype(F32)
    tile_r = right[half : half + META, :].astype(F32)
    row = lax.broadcasted_iota(jnp.int32, (META, WIDE), 0)
    lane = lax.broadcasted_iota(jnp.int32, (META, WIDE), 1)

    def item(tile, i, j):
        return jnp.sum(jnp.where((row == i) & (lane == j), tile, 0.0)).astype(jnp.int32)

    own = {-1: item(tile_l, 0, 3) + MISSING, 4: item(tile_r, 0, 0) + MISSING}
    ahead_of = {r: item(tile_l, 1, 4 + r) + MISSING for r in (-2, -1)}
    ahead_of[4] = item(tile_r, 1, 0) + MISSING
    own.update({r: kinds[0, r] for r in range(4)})
    ahead_of.update({r: kinds[1, r] for r in range(4)})
    pattern = {r: tile_l[2:3, 4 + r : 5 + r].astype(jnp.int32) for r in (-2, -1)}
    pattern[4] = tile_r[2:3, 0:1].astype(jnp.int32)
    pattern.update({r: phase[0, r] for r in range(4)})
    has_left, has_right = tile_l[3:4, :], tile_r[3:4, :]

    def own_kind(r):
        return own[r]

    def next_kind(r):
        return ahead_of[r]

    def flag(kind):
        return jnp.where(kind < MISSING, 1.0, 0.0).astype(F32)

    for r in range(-2, 5):
        hot = jnp.where(pick == pattern[r], 1.0, 0.0).astype(BF16)
        cosb[r + 2] = dot(cos_t[...], hot)
        sinb[r + 2] = dot(sin_t[...], hot)

    def v_row(r):
        if r < 0:
            return left[(r + 2) * BLK : (r + 3) * BLK, :]
        if r > 3:
            return right[(r - 4) * BLK : (r - 3) * BLK, :]
        return vb[r * BLK : (r + 1) * BLK, :]

    def y_row(r):
        return y1b[r + 1]

    def back_phase(x, r):
        x = x.astype(F32)
        return (cosb[r + 2] * x - sinb[r + 2] * times_i(x)).astype(BF16)

    def hop_row(r, row):
        ko, kn, kb = own_kind(r), next_kind(r), next_kind(r - 1)
        total = flag(ko) * dot(sym[jnp.minimum(ko, 7)], row(r))
        ahead = flag(kn) * dot(hop[jnp.minimum(kn, 7)], row(r + 1))
        total += cosb[r + 2] * ahead + sinb[r + 2] * times_i(ahead)
        return total + flag(kb) * dot(hop_t[jnp.minimum(kb, 7)], z[r + 1])

    vb[...] = (h * base[...]).astype(BF16)
    for r in range(-2, 4):
        z[r + 2] = back_phase(v_row(r), r)
    for r in range(-1, 5):
        scaled = base[r * BLK : (r + 1) * BLK, :] if 0 <= r < 4 else v_row(r).astype(F32) * inv_h
        y = hop_row(r, v_row) * inv_h - centre * scaled
        if r == -1:
            y = y * has_left
        if r == 4:
            y = y * has_right
        if 0 <= r < 4:
            y1[r] = y
        y1b[r + 1] = y.astype(BF16)
    for r in range(-1, 4):
        z[r + 2] = back_phase(y_row(r), r)
    for r in range(4):
        y = (2.0 * inv_h) * (hop_row(r, y_row) - centre * y1[r]) - h * base[r * BLK : (r + 1) * BLK, :]
        w[r * BLK : (r + 1) * BLK, :] = y
        w_hi[r * BLK : (r + 1) * BLK, :] = y.astype(BF16)


def chebyshev(*args):
    spec = pl.BlockSpec(memory_space=VM)
    smem = pl.BlockSpec(memory_space=SM)
    return pl.pallas_call(
        filter_kernel,
        out_shape=(jax.ShapeDtypeStruct(args[4].shape, F32), jax.ShapeDtypeStruct(args[4].shape, BF16)),
        in_specs=[smem] * 4 + [spec] * 7,
        out_specs=(spec, spec),
        scratch_shapes=[
            VM(args[4].shape, BF16),
            VM((7, BLK, WIDE), F32),
            VM((7, BLK, WIDE), F32),
            VM((6, BLK, WIDE), BF16),
            VM((4, BLK, WIDE), F32),
            VM((6, BLK, WIDE), BF16),
        ],
        compiler_params=pltpu.CompilerParams(vmem_limit_bytes=16 << 20),
        name="chebyshev",
    )(*args)


def gram_kernel(pos, w, own, first, second, third, p01, out):
    which = pos[0]
    for src, ref in enumerate((own, first, second, third)):
        for panel in range(2):
            here = [z for z in range(8) if HELD[panel][z] == src]
            hit = functools.reduce(jnp.logical_or, [which == z for z in here])

            @pl.when(hit)
            def _(ref=ref, panel=panel):
                p01[:, panel * WIDE : (panel + 1) * WIDE] = ref[...]

    both = p01[...]
    w_hi, w_lo = split(w[...])
    prod = dot_t(both, jnp.concatenate([both, w_hi, w_lo], 1))

    def inner(a, b):
        d = prod[a * WIDE : (a + 1) * WIDE, b * WIDE : (b + 1) * WIDE]
        return d[:HALF] + lane_sign(1.0) * pltpu.roll(d[HALF:], HALF, 1)

    row = lax.broadcasted_iota(jnp.int32, (HALF, WIDE), 0)
    lane = lax.broadcasted_iota(jnp.int32, (HALF, WIDE), 1)
    col = jnp.where(lane < HALF, lane, lane - HALF)
    g00, g11 = inner(0, 0), inner(1, 1)
    diag = jnp.where(lane < HALF, g00, pltpu.roll(g11, HALF, 1))
    out[0:HALF, :] = jnp.where(col > row, g00, jnp.where(col < row, g11, diag))
    out[HALF : 2 * HALF, :] = inner(0, 1)
    out[2 * HALF : 3 * HALF, :] = inner(0, 2) + inner(0, 3)
    out[3 * HALF : 4 * HALF, :] = inner(1, 2) + inner(1, 3)


def gram(pos, w, parts):
    spec = pl.BlockSpec(memory_space=VM)
    return pl.pallas_call(
        gram_kernel,
        out_shape=(
            jax.ShapeDtypeStruct((w.shape[0], 2 * WIDE), BF16),
            jax.ShapeDtypeStruct((4 * HALF, WIDE), F32),
        ),
        in_specs=[pl.BlockSpec(memory_space=SM)] + [spec] * 5,
        out_specs=(spec, spec),
        compiler_params=pltpu.CompilerParams(vmem_limit_bytes=16 << 20),
        name="gram",
    )(pos, w, *parts)


def inverse_factor(tr, ti):
    tiles = WIDE // 8
    re = [tr[8 * t : 8 * t + 8] for t in range(tiles)]
    im = [ti[8 * t : 8 * t + 8] for t in range(tiles)]
    lane = lax.broadcasted_iota(jnp.int32, (8, WIDE), 1)
    sub = lax.broadcasted_iota(jnp.int32, (8, WIDE), 0)
    for k in range(WIDE):
        g, j = divmod(k, 8)
        at_k = lane == k
        row_r = re[g][j : j + 1]
        row_i = im[g][j : j + 1]
        inv = 1.0 / jnp.broadcast_to(row_r[:, k : k + 1], (1, WIDE))
        row_r = jnp.where(at_k[:1], 1.0, row_r) * inv
        row_i = jnp.where(at_k[:1], 0.0, row_i) * inv
        row_r = jnp.broadcast_to(row_r, (8, WIDE))
        row_i = jnp.broadcast_to(row_i, (8, WIDE))
        for t in range(g, tiles):
            if t == g and j == 7:
                continue
            cr = jnp.broadcast_to(re[t][:, k : k + 1], (8, WIDE))
            ci = jnp.broadcast_to(im[t][:, k : k + 1], (8, WIDE))
            keep_r = jnp.where(at_k, 0.0, re[t])
            keep_i = jnp.where(at_k, 0.0, im[t])
            new_r = keep_r - (cr * row_r - ci * row_i)
            new_i = keep_i - (cr * row_i + ci * row_r)
            if t == g:
                new_r = jnp.where(sub > j, new_r, re[t])
                new_i = jnp.where(sub > j, new_i, im[t])
            re[t], im[t] = new_r, new_i
    out_r, out_i = [], []
    for t in range(tiles):
        diag = lane == sub + 8 * t
        below = lane < sub + 8 * t
        pivot = jnp.sum(jnp.where(diag, re[t], 0.0), axis=1, keepdims=True)
        scale = lax.rsqrt(pivot)
        out_r.append(jnp.where(diag, 1.0, jnp.where(below, re[t], 0.0)) * scale)
        out_i.append(jnp.where(below, im[t], 0.0) * scale)
    return jnp.concatenate(out_r, 0), jnp.concatenate(out_i, 0)


def wide_dot(x, y):
    return split_dot(split(x), split(y))


def split_dot(x, y):
    (xh, xl), (yh, yl) = x, y
    return dot(xh, yh) + (dot(xh, yl) + dot(xl, yh))


def pair(re, im):
    return jnp.concatenate([jnp.concatenate([re, im], 1), jnp.concatenate([-im, re], 1)], 0)


def refine(tr, ti, root):
    row = lax.broadcasted_iota(jnp.int32, (WIDE, WIDE), 0)
    col = lax.broadcasted_iota(jnp.int32, (WIDE, WIDE), 1)
    one = jnp.where(row == col, 1.0, 0.0)
    weight = jnp.where(col < row, 1.0, 0.5 * one)
    down = lax.rsqrt(jnp.sum(one * tr, axis=1, keepdims=True))
    across = lax.rsqrt(jnp.sum(one * tr, axis=0, keepdims=True))
    ar, ai = tr * down * across, ti * down * across
    unit = split(pair(ar, ai))
    root[:, :WIDE] = one - jnp.where(col < row, ar, 0.0)
    root[:, WIDE:] = -jnp.where(col < row, ai, 0.0)

    def cond(carry):
        step, size = carry
        return (step < 8) & (size > 1e-5) & (size < 1.0)

    def step(carry):
        count, _ = carry
        r = root[...]
        half = split_dot(split(r), unit)
        rt, it = jnp.transpose(r[:, :WIDE]), jnp.transpose(r[:, WIDE:])
        e = wide_dot(half, pair(rt, -it))
        er, ei = e[:, :WIDE] - one, e[:, WIDE:]
        size = jnp.sum(er * er + ei * ei)
        fix = jnp.concatenate([weight * er, weight * ei], 1)
        root[...] = r - wide_dot(fix, pair(r[:, :WIDE], r[:, WIDE:]))
        return count + 1, size

    count, size = lax.while_loop(cond, step, (jnp.int32(0), jnp.float32(0.5)))
    good = size <= 1e-5

    @pl.when(good)
    def _():
        root[:, :WIDE] = root[:, :WIDE] * across
        root[:, WIDE:] = root[:, WIDE:] * across

    @pl.when(jnp.logical_not(good))
    def _():
        re, im = inverse_factor(tr, ti)
        root[:, :WIDE] = re
        root[:, WIDE:] = im


def embed(block):
    return jnp.concatenate([block, times_i(block)], 0)


def finish_kernel(pos, g, w, p01, out, root):
    row = lax.broadcasted_iota(jnp.int32, (HALF, WIDE), 0)
    lane = lax.broadcasted_iota(jnp.int32, (HALF, WIDE), 1)
    left = lane < HALF
    col = jnp.where(left, lane, lane - HALF)
    c, g01 = g[0:HALF, :], g[HALF : 2 * HALF, :]
    c_turn, g01_turn = pltpu.roll(c, HALF, 1), pltpu.roll(g01, HALF, 1)
    above, below, diag = col > row, col < row, col == row

    def stack(top_left, top_right, low_right):
        return jnp.concatenate([jnp.where(left, top_left, top_right), jnp.where(left, 0.0, low_right)], 0)

    once_r = stack(jnp.where(above, c, 0.0), g01_turn, jnp.where(below, c_turn, 0.0))
    once_i = stack(jnp.where(above, c_turn, 0.0), g01, jnp.where(below, c, 0.0))
    pivots = jnp.where(diag, c, 0.0)
    tr = once_r + jnp.transpose(once_r) + stack(pivots, 0.0, pivots)
    ti = once_i - jnp.transpose(once_i)
    refine(tr, ti, root)
    rr, ri = root[:, :WIDE], root[:, WIDE:]
    which = pos[0]

    @pl.when(which >= 2)
    def _():
        m = g[2 * HALF : 4 * HALF, :]
        n = wide_dot(root[...], embed(m))
        k = wide_dot(jnp.concatenate([jnp.transpose(rr), -jnp.transpose(ri)], 1), embed(n))
        e_hi, e_lo = split(jnp.concatenate([embed(k[:HALF]), embed(k[HALF:])], 0))
        out[...] = w[...] - (dot(p01[...], e_hi) + dot(p01[...], e_lo))

    @pl.when(which < 2)
    def _():
        rt, it = jnp.transpose(rr), jnp.transpose(ri)
        full = lax.broadcasted_iota(jnp.int32, (WIDE, WIDE), 1) < HALF
        first = jnp.where(full, rt, -pltpu.roll(it, HALF, 1))
        second = jnp.where(full, pltpu.roll(rt, HALF, 1), -it)
        is_first = which == 0
        own = jnp.where(is_first, first[:HALF], second[HALF:])
        other = jnp.where(is_first, 0.0, second[:HALF])
        o_hi, o_lo = split(embed(other))
        p0 = p01[:, :WIDE]
        out[...] = dot(w[...], embed(own), precision=HIGHEST) + dot(p0, o_hi) + dot(p0, o_lo)


def finish(pos, g, w, p01):
    spec = pl.BlockSpec(memory_space=VM)
    return pl.pallas_call(
        finish_kernel,
        out_shape=jax.ShapeDtypeStruct(w.shape, F32),
        in_specs=[pl.BlockSpec(memory_space=SM), spec, spec, spec],
        out_specs=spec,
        scratch_shapes=[VM((WIDE, 2 * WIDE), F32)],
        compiler_params=pltpu.CompilerParams(vmem_limit_bytes=16 << 20),
        name="finish",
    )(pos, g, w, p01)


def swap(x, axes):
    return lax.all_to_all(x, axes, 0, 0, tiled=True)


def copies(x, count):
    return jnp.broadcast_to(x[None], (count,) + x.shape).reshape((count * x.shape[0],) + x.shape[1:])


def sum_pieces(x, count):
    return jnp.sum(x.reshape((count, -1) + x.shape[1:]), axis=0)


def slab_sum(x, inner, outer):
    near, far = lax.axis_size(inner), lax.axis_size(outer)
    piece = sum_pieces(swap(x, inner), near)
    piece = sum_pieces(swap(copies(piece, far), outer), far)
    return swap(copies(piece, near), inner)


def spread(w_hi, pos):
    far = lax.ppermute(w_hi, "panel", [(0, 3), (1, 6)])
    own = jnp.where((pos == 3) | (pos == 6), far, w_hi)
    return (own,) + tuple(lax.ppermute(own, "panel", pairs) for pairs in STEPS)


def thirds(x):
    a = lax.reduce_precision(x, 8, 7)
    b = lax.reduce_precision(x - a, 8, 7)
    return jnp.concatenate([a, b, x - a - b], axis=0).astype(BF16).T


def body(vectors, hop_table, block_kind, block_phase, phase_angles, centre, half_width):
    slab = ("y", "x", "core")
    count = lax.axis_size(slab)
    kinds, phase = block_kind.T, block_phase[None, :]
    up, down = pack(vectors, kinds, phase)
    left = lax.ppermute(up, slab, [(i, i + 1) for i in range(count - 1)])
    right = lax.ppermute(down, slab, [(i + 1, i) for i in range(count - 1)])
    base = vectors / half_width[0]
    sides = jnp.concatenate([left, right], axis=0)
    wide = hop_table.astype(F32)
    turned = jnp.transpose(hop_table, (0, 2, 1))
    sym = ((wide + turned.astype(F32)) * 0.5).astype(BF16)
    cos_t = thirds(jnp.cos(phase_angles))
    sin_t = thirds(jnp.sin(phase_angles))
    w, w_hi = chebyshev(
        kinds, phase, centre, half_width, base, sides, hop_table, turned, sym, cos_t, sin_t
    )
    pos = lax.axis_index("panel").astype(jnp.int32)
    spot = pos.reshape(1)
    p01, part = gram(spot, w, spread(w_hi, pos))
    return finish(spot, slab_sum(part, ("x", "core"), "y"), w, p01)


def solution(mesh):
    panels = mesh.shape["panel"]
    devices = np.asarray(mesh.devices).reshape(8, 4, 2, panels)
    fine = Mesh(devices, ("y", "x", "core", "panel"))
    slab = ("y", "x", "core")
    in_specs = (P(slab, "panel"), P(), P(slab, None), P(slab), P(), P(), P())
    return jax.shard_map(body, mesh=fine, in_specs=in_specs, out_specs=P(slab, "panel"), check_vma=False)
```

```python
import functools

import jax
import jax.numpy as jnp
import numpy as np
from jax import lax
from jax.experimental import pallas as pl
from jax.experimental.pallas import tpu as pltpu
from jax.sharding import Mesh, PartitionSpec as P

HIGHEST = lax.Precision.HIGHEST
F32 = jnp.float32
BF16 = jnp.bfloat16
BLK = 256
WIDE = 128
HALF = 64
META = 16
MISSING = 8
STEPS = (
    [(0, 7), (3, 4), (1, 2), (6, 5)],
    [(0, 1), (3, 5), (1, 0), (6, 4)],
    [(0, 6), (3, 2), (1, 3), (6, 7)],
)
HELD = ((0, 2, 3, 0, 1, 2, 3, 1), (2, 0, 1, 3, 2, 1, 0, 3))
VM = pltpu.VMEM
SM = pltpu.SMEM


def lane_sign(first):
    lane = lax.broadcasted_iota(jnp.int32, (1, WIDE), 1)
    return jnp.where(lane < HALF, first, -first).astype(F32)


def times_i(packed):
    return lane_sign(-1.0) * pltpu.roll(packed, HALF, 1)


def dot(a, b, **kw):
    return lax.dot_general(a, b, (((1,), (0,)), ((), ())), preferred_element_type=F32, **kw)


def dot_t(a, b, **kw):
    return lax.dot_general(a, b, (((0,), (0,)), ((), ())), preferred_element_type=F32, **kw)


def split(x):
    hi = x.astype(BF16)
    return hi, (x - hi.astype(F32)).astype(BF16)


def pack_kernel(v, kinds, phase, up, down, tile):
    half = v.shape[0] // 2
    down[:half, :] = v[:half, :].astype(BF16)
    up[:half, :] = v[half:, :].astype(BF16)
    tile[...] = jnp.zeros(tile.shape, F32)
    tile[0:2, 0:4] = (kinds[...] - MISSING).astype(F32)
    tile[2:3, 0:4] = phase[...].astype(F32)
    tile[3:4, :] = jnp.ones((1, WIDE), F32)
    info = tile[...].astype(BF16)
    down[half:, :] = info
    up[half:, :] = info


def pack(v, kinds, phase):
    spec = pl.BlockSpec(memory_space=VM)
    shape = jax.ShapeDtypeStruct((v.shape[0] // 2 + META, WIDE), BF16)
    return pl.pallas_call(
        pack_kernel,
        out_shape=(shape, shape),
        in_specs=[spec] * 3,
        out_specs=(spec, spec),
        scratch_shapes=[VM((META, WIDE), F32)],
        name="pack",
    )(v, kinds, phase)


def filter_kernel(
    kinds, phase, shift, width, base, sides, hop, hop_t, sym, cos_t, sin_t,
    w, w_hi, vb, cosb, sinb, z, y1, y1b,
):
    half = base.shape[0] // 2
    left, right = sides.at[0 : half + META], sides.at[half + META :]
    centre = shift[0]
    h = jnp.broadcast_to(width[0], (1, WIDE))
    inv_h = 1.0 / h
    pick = lax.broadcasted_iota(jnp.int32, (cos_t.shape[1], WIDE), 0) % 16
    tile_l = left[half : half + META, :].astype(F32)
    tile_r = right[half : half + META, :].astype(F32)
    row = lax.broadcasted_iota(jnp.int32, (META, WIDE), 0)
    lane = lax.broadcasted_iota(jnp.int32, (META, WIDE), 1)

    def item(tile, i, j):
        return jnp.sum(jnp.where((row == i) & (lane == j), tile, 0.0)).astype(jnp.int32)

    own = {-1: item(tile_l, 0, 3) + MISSING, 4: item(tile_r, 0, 0) + MISSING}
    ahead_of = {r: item(tile_l, 1, 4 + r) + MISSING for r in (-2, -1)}
    ahead_of[4] = item(tile_r, 1, 0) + MISSING
    own.update({r: kinds[0, r] for r in range(4)})
    ahead_of.update({r: kinds[1, r] for r in range(4)})
    pattern = {r: tile_l[2:3, 4 + r : 5 + r].astype(jnp.int32) for r in (-2, -1)}
    pattern[4] = tile_r[2:3, 0:1].astype(jnp.int32)
    pattern.update({r: phase[0, r] for r in range(4)})
    has_left, has_right = tile_l[3:4, :], tile_r[3:4, :]

    def own_kind(r):
        return own[r]

    def next_kind(r):
        return ahead_of[r]

    def flag(kind):
        return jnp.where(kind < MISSING, 1.0, 0.0).astype(F32)

    for r in range(-2, 5):
        hot = jnp.where(pick == pattern[r], 1.0, 0.0).astype(BF16)
        cosb[r + 2] = dot(cos_t[...], hot)
        sinb[r + 2] = dot(sin_t[...], hot)

    def v_row(r):
        if r < 0:
            return left[(r + 2) * BLK : (r + 3) * BLK, :]
        if r > 3:
            return right[(r - 4) * BLK : (r - 3) * BLK, :]
        return vb[r * BLK : (r + 1) * BLK, :]

    def y_row(r):
        return y1b[r + 1]

    def back_phase(x, r):
        x = x.astype(F32)
        return (cosb[r + 2] * x - sinb[r + 2] * times_i(x)).astype(BF16)

    def hop_row(r, row):
        ko, kn, kb = own_kind(r), next_kind(r), next_kind(r - 1)
        total = flag(ko) * dot(sym[jnp.minimum(ko, 7)], row(r))
        ahead = flag(kn) * dot(hop[jnp.minimum(kn, 7)], row(r + 1))
        total += cosb[r + 2] * ahead + sinb[r + 2] * times_i(ahead)
        return total + flag(kb) * dot(hop_t[jnp.minimum(kb, 7)], z[r + 1])

    vb[...] = (h * base[...]).astype(BF16)
    for r in range(-2, 4):
        z[r + 2] = back_phase(v_row(r), r)
    for r in range(-1, 5):
        scaled = base[r * BLK : (r + 1) * BLK, :] if 0 <= r < 4 else v_row(r).astype(F32) * inv_h
        y = hop_row(r, v_row) * inv_h - centre * scaled
        if r == -1:
            y = y * has_left
        if r == 4:
            y = y * has_right
        if 0 <= r < 4:
            y1[r] = y
        y1b[r + 1] = y.astype(BF16)
    for r in range(-1, 4):
        z[r + 2] = back_phase(y_row(r), r)
    for r in range(4):
        y = (2.0 * inv_h) * (hop_row(r, y_row) - centre * y1[r]) - h * base[r * BLK : (r + 1) * BLK, :]
        w[r * BLK : (r + 1) * BLK, :] = y
        w_hi[r * BLK : (r + 1) * BLK, :] = y.astype(BF16)


def chebyshev(*args):
    spec = pl.BlockSpec(memory_space=VM)
    smem = pl.BlockSpec(memory_space=SM)
    return pl.pallas_call(
        filter_kernel,
        out_shape=(jax.ShapeDtypeStruct(args[4].shape, F32), jax.ShapeDtypeStruct(args[4].shape, BF16)),
        in_specs=[smem] * 4 + [spec] * 7,
        out_specs=(spec, spec),
        scratch_shapes=[
            VM(args[4].shape, BF16),
            VM((7, BLK, WIDE), F32),
            VM((7, BLK, WIDE), F32),
            VM((6, BLK, WIDE), BF16),
            VM((4, BLK, WIDE), F32),
            VM((6, BLK, WIDE), BF16),
        ],
        compiler_params=pltpu.CompilerParams(vmem_limit_bytes=16 << 20),
        name="chebyshev",
    )(*args)


def gram_kernel(pos, w, own, first, second, third, p01, out):
    which = pos[0]
    for src, ref in enumerate((own, first, second, third)):
        for panel in range(2):
            here = [z for z in range(8) if HELD[panel][z] == src]
            hit = functools.reduce(jnp.logical_or, [which == z for z in here])

            @pl.when(hit)
            def _(ref=ref, panel=panel):
                p01[:, panel * WIDE : (panel + 1) * WIDE] = ref[...]

    both = p01[...]
    w_hi, w_lo = split(w[...])
    prod = dot_t(both, jnp.concatenate([both, w_hi, w_lo], 1))

    def inner(a, b):
        d = prod[a * WIDE : (a + 1) * WIDE, b * WIDE : (b + 1) * WIDE]
        return d[:HALF] + lane_sign(1.0) * pltpu.roll(d[HALF:], HALF, 1)

    row = lax.broadcasted_iota(jnp.int32, (HALF, WIDE), 0)
    lane = lax.broadcasted_iota(jnp.int32, (HALF, WIDE), 1)
    col = jnp.where(lane < HALF, lane, lane - HALF)
    g00, g11 = inner(0, 0), inner(1, 1)
    diag = jnp.where(lane < HALF, g00, pltpu.roll(g11, HALF, 1))
    out[0:HALF, :] = jnp.where(col > row, g00, jnp.where(col < row, g11, diag))
    out[HALF : 2 * HALF, :] = inner(0, 1)
    out[2 * HALF : 3 * HALF, :] = inner(0, 2) + inner(0, 3)
    out[3 * HALF : 4 * HALF, :] = inner(1, 2) + inner(1, 3)


def gram(pos, w, parts):
    spec = pl.BlockSpec(memory_space=VM)
    return pl.pallas_call(
        gram_kernel,
        out_shape=(
            jax.ShapeDtypeStruct((w.shape[0], 2 * WIDE), BF16),
            jax.ShapeDtypeStruct((4 * HALF, WIDE), F32),
        ),
        in_specs=[pl.BlockSpec(memory_space=SM)] + [spec] * 5,
        out_specs=(spec, spec),
        compiler_params=pltpu.CompilerParams(vmem_limit_bytes=16 << 20),
        name="gram",
    )(pos, w, *parts)


def inverse_factor(tr, ti):
    tiles = WIDE // 8
    re = [tr[8 * t : 8 * t + 8] for t in range(tiles)]
    im = [ti[8 * t : 8 * t + 8] for t in range(tiles)]
    lane = lax.broadcasted_iota(jnp.int32, (8, WIDE), 1)
    sub = lax.broadcasted_iota(jnp.int32, (8, WIDE), 0)
    for k in range(WIDE):
        g, j = divmod(k, 8)
        at_k = lane == k
        row_r = re[g][j : j + 1]
        row_i = im[g][j : j + 1]
        inv = 1.0 / jnp.broadcast_to(row_r[:, k : k + 1], (1, WIDE))
        row_r = jnp.where(at_k[:1], 1.0, row_r) * inv
        row_i = jnp.where(at_k[:1], 0.0, row_i) * inv
        row_r = jnp.broadcast_to(row_r, (8, WIDE))
        row_i = jnp.broadcast_to(row_i, (8, WIDE))
        for t in range(g, tiles):
            if t == g and j == 7:
                continue
            cr = jnp.broadcast_to(re[t][:, k : k + 1], (8, WIDE))
            ci = jnp.broadcast_to(im[t][:, k : k + 1], (8, WIDE))
            keep_r = jnp.where(at_k, 0.0, re[t])
            keep_i = jnp.where(at_k, 0.0, im[t])
            new_r = keep_r - (cr * row_r - ci * row_i)
            new_i = keep_i - (cr * row_i + ci * row_r)
            if t == g:
                new_r = jnp.where(sub > j, new_r, re[t])
                new_i = jnp.where(sub > j, new_i, im[t])
            re[t], im[t] = new_r, new_i
    out_r, out_i = [], []
    for t in range(tiles):
        diag = lane == sub + 8 * t
        below = lane < sub + 8 * t
        pivot = jnp.sum(jnp.where(diag, re[t], 0.0), axis=1, keepdims=True)
        scale = lax.rsqrt(pivot)
        out_r.append(jnp.where(diag, 1.0, jnp.where(below, re[t], 0.0)) * scale)
        out_i.append(jnp.where(below, im[t], 0.0) * scale)
    return jnp.concatenate(out_r, 0), jnp.concatenate(out_i, 0)


def wide_dot(x, y):
    return split_dot(split(x), split(y))


def split_dot(x, y):
    (xh, xl), (yh, yl) = x, y
    return dot(xh, yh) + (dot(xh, yl) + dot(xl, yh))


def pair(re, im):
    return jnp.concatenate([jnp.concatenate([re, im], 1), jnp.concatenate([-im, re], 1)], 0)


def refine(tr, ti, root):
    row = lax.broadcasted_iota(jnp.int32, (WIDE, WIDE), 0)
    col = lax.broadcasted_iota(jnp.int32, (WIDE, WIDE), 1)
    one = jnp.where(row == col, 1.0, 0.0)
    weight = jnp.where(col < row, 1.0, 0.5 * one)
    down = lax.rsqrt(jnp.sum(one * tr, axis=1, keepdims=True))
    across = lax.rsqrt(jnp.sum(one * tr, axis=0, keepdims=True))
    ar, ai = tr * down * across, ti * down * across
    unit = split(pair(ar, ai))
    root[:, :WIDE] = one - jnp.where(col < row, ar, 0.0)
    root[:, WIDE:] = -jnp.where(col < row, ai, 0.0)

    def cond(carry):
        step, size = carry
        return (step < 8) & (size > 1e-5) & (size < 1.0)

    def step(carry):
        count, _ = carry
        r = root[...]
        half = split_dot(split(r), unit)
        rt, it = jnp.transpose(r[:, :WIDE]), jnp.transpose(r[:, WIDE:])
        e = wide_dot(half, pair(rt, -it))
        er, ei = e[:, :WIDE] - one, e[:, WIDE:]
        size = jnp.sum(er * er + ei * ei)
        fix = jnp.concatenate([weight * er, weight * ei], 1)
        root[...] = r - wide_dot(fix, pair(r[:, :WIDE], r[:, WIDE:]))
        return count + 1, size

    count, size = lax.while_loop(cond, step, (jnp.int32(0), jnp.float32(0.5)))
    good = size <= 1e-5

    @pl.when(good)
    def _():
        root[:, :WIDE] = root[:, :WIDE] * across
        root[:, WIDE:] = root[:, WIDE:] * across

    @pl.when(jnp.logical_not(good))
    def _():
        re, im = inverse_factor(tr, ti)
        root[:, :WIDE] = re
        root[:, WIDE:] = im


def embed(block):
    return jnp.concatenate([block, times_i(block)], 0)


def finish_kernel(pos, g, w, p01, out, root):
    row = lax.broadcasted_iota(jnp.int32, (HALF, WIDE), 0)
    lane = lax.broadcasted_iota(jnp.int32, (HALF, WIDE), 1)
    left = lane < HALF
    col = jnp.where(left, lane, lane - HALF)
    c, g01 = g[0:HALF, :], g[HALF : 2 * HALF, :]
    c_turn, g01_turn = pltpu.roll(c, HALF, 1), pltpu.roll(g01, HALF, 1)
    above, below, diag = col > row, col < row, col == row

    def stack(top_left, top_right, low_right):
        return jnp.concatenate([jnp.where(left, top_left, top_right), jnp.where(left, 0.0, low_right)], 0)

    once_r = stack(jnp.where(above, c, 0.0), g01_turn, jnp.where(below, c_turn, 0.0))
    once_i = stack(jnp.where(above, c_turn, 0.0), g01, jnp.where(below, c, 0.0))
    pivots = jnp.where(diag, c, 0.0)
    tr = once_r + jnp.transpose(once_r) + stack(pivots, 0.0, pivots)
    ti = once_i - jnp.transpose(once_i)
    refine(tr, ti, root)
    rr, ri = root[:, :WIDE], root[:, WIDE:]
    which = pos[0]

    @pl.when(which >= 2)
    def _():
        m = g[2 * HALF : 4 * HALF, :]
        n = wide_dot(root[...], embed(m))
        k = wide_dot(jnp.concatenate([jnp.transpose(rr), -jnp.transpose(ri)], 1), embed(n))
        e_hi, e_lo = split(jnp.concatenate([embed(k[:HALF]), embed(k[HALF:])], 0))
        out[...] = w[...] - (dot(p01[...], e_hi) + dot(p01[...], e_lo))

    @pl.when(which < 2)
    def _():
        rt, it = jnp.transpose(rr), jnp.transpose(ri)
        full = lax.broadcasted_iota(jnp.int32, (WIDE, WIDE), 1) < HALF
        first = jnp.where(full, rt, -pltpu.roll(it, HALF, 1))
        second = jnp.where(full, pltpu.roll(rt, HALF, 1), -it)
        is_first = which == 0
        own = jnp.where(is_first, first[:HALF], second[HALF:])
        other = jnp.where(is_first, 0.0, second[:HALF])
        o_hi, o_lo = split(embed(other))
        p0 = p01[:, :WIDE]
        out[...] = dot(w[...], embed(own), precision=HIGHEST) + dot(p0, o_hi) + dot(p0, o_lo)


def finish(pos, g, w, p01):
    spec = pl.BlockSpec(memory_space=VM)
    return pl.pallas_call(
        finish_kernel,
        out_shape=jax.ShapeDtypeStruct(w.shape, F32),
        in_specs=[pl.BlockSpec(memory_space=SM), spec, spec, spec],
        out_specs=spec,
        scratch_shapes=[VM((WIDE, 2 * WIDE), F32)],
        compiler_params=pltpu.CompilerParams(vmem_limit_bytes=16 << 20),
        name="finish",
    )(pos, g, w, p01)


def swap(x, axes):
    return lax.all_to_all(x, axes, 0, 0, tiled=True)


def copies(x, count):
    return jnp.broadcast_to(x[None], (count,) + x.shape).reshape((count * x.shape[0],) + x.shape[1:])


def sum_pieces(x, count):
    return jnp.sum(x.reshape((count, -1) + x.shape[1:]), axis=0)


def slab_sum(x, inner, outer):
    near, far = lax.axis_size(inner), lax.axis_size(outer)
    piece = sum_pieces(swap(x, inner), near)
    piece = sum_pieces(swap(copies(piece, far), outer), far)
    return swap(copies(piece, near), inner)


def spread(w_hi, pos):
    far = lax.ppermute(w_hi, "panel", [(0, 3), (1, 6)])
    own = jnp.where((pos == 3) | (pos == 6), far, w_hi)
    return (own,) + tuple(lax.ppermute(own, "panel", pairs) for pairs in STEPS)


def thirds(x):
    a = lax.reduce_precision(x, 8, 7)
    b = lax.reduce_precision(x - a, 8, 7)
    return jnp.concatenate([a, b, x - a - b], axis=0).astype(BF16).T


def body(vectors, hop_table, block_kind, block_phase, phase_angles, centre, half_width):
    slab = ("y", "x", "core")
    count = lax.axis_size(slab)
    kinds, phase = block_kind.T, block_phase[None, :]
    up, down = pack(vectors, kinds, phase)
    left = lax.ppermute(up, slab, [(i, i + 1) for i in range(count - 1)])
    right = lax.ppermute(down, slab, [(i + 1, i) for i in range(count - 1)])
    base = vectors / half_width[0]
    sides = jnp.concatenate([left, right], axis=0)
    wide = hop_table.astype(F32)
    turned = jnp.transpose(hop_table, (0, 2, 1))
    sym = ((wide + turned.astype(F32)) * 0.5).astype(BF16)
    cos_t = thirds(jnp.cos(phase_angles))
    sin_t = thirds(jnp.sin(phase_angles))
    w, w_hi = chebyshev(
        kinds, phase, centre, half_width, base, sides, hop_table, turned, sym, cos_t, sin_t
    )
    pos = lax.axis_index("panel").astype(jnp.int32)
    spot = pos.reshape(1)
    p01, part = gram(spot, w, spread(w_hi, pos))
    return finish(spot, slab_sum(part, ("x", "core"), "y"), w, p01)


def solution(mesh):
    panels = mesh.shape["panel"]
    devices = np.asarray(mesh.devices).reshape(8, 4, 2, panels)
    fine = Mesh(devices, ("y", "x", "core", "panel"))
    slab = ("y", "x", "core")
    in_specs = (P(slab, "panel"), P(), P(slab, None), P(slab), P(), P(), P())
    return jax.shard_map(body, mesh=fine, in_specs=in_specs, out_specs=P(slab, "panel"), check_vma=False)
```

```python
import functools

import jax
import jax.numpy as jnp
import numpy as np
from jax import lax
from jax.experimental import pallas as pl
from jax.experimental.pallas import tpu as pltpu
from jax.sharding import Mesh, PartitionSpec as P

HIGHEST = lax.Precision.HIGHEST
F32 = jnp.float32
BF16 = jnp.bfloat16
BLK = 256
WIDE = 128
HALF = 64
META = 16
MISSING = 8
STEPS = (
    [(0, 7), (3, 4), (1, 2), (6, 5)],
    [(0, 1), (3, 5), (1, 0), (6, 4)],
    [(0, 6), (3, 2), (1, 3), (6, 7)],
)
HELD = ((0, 2, 3, 0, 1, 2, 3, 1), (2, 0, 1, 3, 2, 1, 0, 3))
VM = pltpu.VMEM
SM = pltpu.SMEM


def lane_sign(first):
    lane = lax.broadcasted_iota(jnp.int32, (1, WIDE), 1)
    return jnp.where(lane < HALF, first, -first).astype(F32)


def times_i(packed):
    return lane_sign(-1.0) * pltpu.roll(packed, HALF, 1)


def dot(a, b, **kw):
    return lax.dot_general(a, b, (((1,), (0,)), ((), ())), preferred_element_type=F32, **kw)


def dot_t(a, b, **kw):
    return lax.dot_general(a, b, (((0,), (0,)), ((), ())), preferred_element_type=F32, **kw)


def split(x):
    hi = x.astype(BF16)
    return hi, (x - hi.astype(F32)).astype(BF16)


def pack_kernel(v, kinds, phase, up, down, tile):
    half = v.shape[0] // 2
    down[:half, :] = v[:half, :].astype(BF16)
    up[:half, :] = v[half:, :].astype(BF16)
    tile[...] = jnp.zeros(tile.shape, F32)
    tile[0:2, 0:4] = (kinds[...] - MISSING).astype(F32)
    tile[2:3, 0:4] = phase[...].astype(F32)
    tile[3:4, :] = jnp.ones((1, WIDE), F32)
    info = tile[...].astype(BF16)
    down[half:, :] = info
    up[half:, :] = info


def pack(v, kinds, phase):
    spec = pl.BlockSpec(memory_space=VM)
    shape = jax.ShapeDtypeStruct((v.shape[0] // 2 + META, WIDE), BF16)
    return pl.pallas_call(
        pack_kernel,
        out_shape=(shape, shape),
        in_specs=[spec] * 3,
        out_specs=(spec, spec),
        scratch_shapes=[VM((META, WIDE), F32)],
        name="pack",
    )(v, kinds, phase)


def filter_kernel(
    kinds, phase, shift, width, base, sides, hop, hop_t, sym, waves,
    w, w_hi, vb, cosb, sinb, z, y1, y1b,
):
    half = base.shape[0] // 2
    left, right = sides.at[0 : half + META], sides.at[half + META :]
    centre = shift[0]
    h = jnp.broadcast_to(width[0], (1, WIDE))
    inv_h = 1.0 / h
    pick = lax.broadcasted_iota(jnp.int32, (waves.shape[1], 2 * WIDE), 0)
    side = lax.broadcasted_iota(jnp.int32, (waves.shape[1], 2 * WIDE), 1)
    same = (pick < waves.shape[1] // 2) == (side < WIDE)
    pick = pick % 16
    tile_l = left[half : half + META, :].astype(F32)
    tile_r = right[half : half + META, :].astype(F32)
    row = lax.broadcasted_iota(jnp.int32, (META, WIDE), 0)
    lane = lax.broadcasted_iota(jnp.int32, (META, WIDE), 1)

    def item(tile, i, j):
        return jnp.sum(jnp.where((row == i) & (lane == j), tile, 0.0)).astype(jnp.int32)

    own = {-1: item(tile_l, 0, 3) + MISSING, 4: item(tile_r, 0, 0) + MISSING}
    ahead_of = {r: item(tile_l, 1, 4 + r) + MISSING for r in (-2, -1)}
    ahead_of[4] = item(tile_r, 1, 0) + MISSING
    own.update({r: kinds[0, r] for r in range(4)})
    ahead_of.update({r: kinds[1, r] for r in range(4)})
    pattern = {r: tile_l[2:3, 4 + r : 5 + r].astype(jnp.int32) for r in (-2, -1)}
    pattern[4] = tile_r[2:3, 0:1].astype(jnp.int32)
    pattern.update({r: phase[0, r] for r in range(4)})
    has_left, has_right = tile_l[3:4, :], tile_r[3:4, :]

    def own_kind(r):
        return own[r]

    def next_kind(r):
        return ahead_of[r]

    def flag(kind):
        return jnp.where(kind < MISSING, 1.0, 0.0).astype(F32)

    for r in range(-2, 5):
        hot = jnp.where(same & (pick == pattern[r]), 1.0, 0.0).astype(BF16)
        both = dot(waves[...], hot)
        cosb[r + 2] = both[:, :WIDE]
        sinb[r + 2] = both[:, WIDE:]

    def v_row(r):
        if r < 0:
            return left[(r + 2) * BLK : (r + 3) * BLK, :]
        if r > 3:
            return right[(r - 4) * BLK : (r - 3) * BLK, :]
        return vb[r * BLK : (r + 1) * BLK, :]

    def y_row(r):
        return y1b[r + 1]

    def back_phase(x, r):
        x = x.astype(F32)
        return (cosb[r + 2] * x - sinb[r + 2] * times_i(x)).astype(BF16)

    def hop_row(r, row):
        ko, kn, kb = own_kind(r), next_kind(r), next_kind(r - 1)
        total = flag(ko) * dot(sym[jnp.minimum(ko, 7)], row(r))
        ahead = flag(kn) * dot(hop[jnp.minimum(kn, 7)], row(r + 1))
        total += cosb[r + 2] * ahead + sinb[r + 2] * times_i(ahead)
        return total + flag(kb) * dot(hop_t[jnp.minimum(kb, 7)], z[r + 1])

    vb[...] = (h * base[...]).astype(BF16)
    for r in range(-2, 4):
        z[r + 2] = back_phase(v_row(r), r)
    for r in range(-1, 5):
        scaled = base[r * BLK : (r + 1) * BLK, :] if 0 <= r < 4 else v_row(r).astype(F32) * inv_h
        y = hop_row(r, v_row) * inv_h - centre * scaled
        if r == -1:
            y = y * has_left
        if r == 4:
            y = y * has_right
        if 0 <= r < 4:
            y1[r] = y
        y1b[r + 1] = y.astype(BF16)
    for r in range(-1, 4):
        z[r + 2] = back_phase(y_row(r), r)
    for r in range(4):
        y = (2.0 * inv_h) * (hop_row(r, y_row) - centre * y1[r]) - h * base[r * BLK : (r + 1) * BLK, :]
        w[r * BLK : (r + 1) * BLK, :] = y
        w_hi[r * BLK : (r + 1) * BLK, :] = y.astype(BF16)


def chebyshev(*args):
    spec = pl.BlockSpec(memory_space=VM)
    smem = pl.BlockSpec(memory_space=SM)
    return pl.pallas_call(
        filter_kernel,
        out_shape=(jax.ShapeDtypeStruct(args[4].shape, F32), jax.ShapeDtypeStruct(args[4].shape, BF16)),
        in_specs=[smem] * 4 + [spec] * 6,
        out_specs=(spec, spec),
        scratch_shapes=[
            VM(args[4].shape, BF16),
            VM((7, BLK, WIDE), F32),
            VM((7, BLK, WIDE), F32),
            VM((6, BLK, WIDE), BF16),
            VM((4, BLK, WIDE), F32),
            VM((6, BLK, WIDE), BF16),
        ],
        compiler_params=pltpu.CompilerParams(vmem_limit_bytes=16 << 20),
        name="chebyshev",
    )(*args)


def gram_kernel(pos, w, own, first, second, third, p01, out):
    which = pos[0]
    for src, ref in enumerate((own, first, second, third)):
        for panel in range(2):
            here = [z for z in range(8) if HELD[panel][z] == src]
            hit = functools.reduce(jnp.logical_or, [which == z for z in here])

            @pl.when(hit)
            def _(ref=ref, panel=panel):
                p01[:, panel * WIDE : (panel + 1) * WIDE] = ref[...]

    both = p01[...]
    w_hi, w_lo = split(w[...])
    prod = dot_t(both, jnp.concatenate([both, w_hi, w_lo], 1))

    def inner(a, b):
        d = prod[a * WIDE : (a + 1) * WIDE, b * WIDE : (b + 1) * WIDE]
        return d[:HALF] + lane_sign(1.0) * pltpu.roll(d[HALF:], HALF, 1)

    row = lax.broadcasted_iota(jnp.int32, (HALF, WIDE), 0)
    lane = lax.broadcasted_iota(jnp.int32, (HALF, WIDE), 1)
    col = jnp.where(lane < HALF, lane, lane - HALF)
    g00, g11 = inner(0, 0), inner(1, 1)
    diag = jnp.where(lane < HALF, g00, pltpu.roll(g11, HALF, 1))
    out[0:HALF, :] = jnp.where(col > row, g00, jnp.where(col < row, g11, diag))
    out[HALF : 2 * HALF, :] = inner(0, 1)
    out[2 * HALF : 3 * HALF, :] = inner(0, 2) + inner(0, 3)
    out[3 * HALF : 4 * HALF, :] = inner(1, 2) + inner(1, 3)


def gram(pos, w, parts):
    spec = pl.BlockSpec(memory_space=VM)
    return pl.pallas_call(
        gram_kernel,
        out_shape=(
            jax.ShapeDtypeStruct((w.shape[0], 2 * WIDE), BF16),
            jax.ShapeDtypeStruct((4 * HALF, WIDE), F32),
        ),
        in_specs=[pl.BlockSpec(memory_space=SM)] + [spec] * 5,
        out_specs=(spec, spec),
        compiler_params=pltpu.CompilerParams(vmem_limit_bytes=16 << 20),
        name="gram",
    )(pos, w, *parts)


def inverse_factor(tr, ti):
    tiles = WIDE // 8
    re = [tr[8 * t : 8 * t + 8] for t in range(tiles)]
    im = [ti[8 * t : 8 * t + 8] for t in range(tiles)]
    lane = lax.broadcasted_iota(jnp.int32, (8, WIDE), 1)
    sub = lax.broadcasted_iota(jnp.int32, (8, WIDE), 0)
    for k in range(WIDE):
        g, j = divmod(k, 8)
        at_k = lane == k
        row_r = re[g][j : j + 1]
        row_i = im[g][j : j + 1]
        inv = 1.0 / jnp.broadcast_to(row_r[:, k : k + 1], (1, WIDE))
        row_r = jnp.where(at_k[:1], 1.0, row_r) * inv
        row_i = jnp.where(at_k[:1], 0.0, row_i) * inv
        row_r = jnp.broadcast_to(row_r, (8, WIDE))
        row_i = jnp.broadcast_to(row_i, (8, WIDE))
        for t in range(g, tiles):
            if t == g and j == 7:
                continue
            cr = jnp.broadcast_to(re[t][:, k : k + 1], (8, WIDE))
            ci = jnp.broadcast_to(im[t][:, k : k + 1], (8, WIDE))
            keep_r = jnp.where(at_k, 0.0, re[t])
            keep_i = jnp.where(at_k, 0.0, im[t])
            new_r = keep_r - (cr * row_r - ci * row_i)
            new_i = keep_i - (cr * row_i + ci * row_r)
            if t == g:
                new_r = jnp.where(sub > j, new_r, re[t])
                new_i = jnp.where(sub > j, new_i, im[t])
            re[t], im[t] = new_r, new_i
    out_r, out_i = [], []
    for t in range(tiles):
        diag = lane == sub + 8 * t
        below = lane < sub + 8 * t
        pivot = jnp.sum(jnp.where(diag, re[t], 0.0), axis=1, keepdims=True)
        scale = lax.rsqrt(pivot)
        out_r.append(jnp.where(diag, 1.0, jnp.where(below, re[t], 0.0)) * scale)
        out_i.append(jnp.where(below, im[t], 0.0) * scale)
    return jnp.concatenate(out_r, 0), jnp.concatenate(out_i, 0)


def wide_dot(x, y):
    return split_dot(split(x), split(y))


def split_dot(x, y):
    (xh, xl), (yh, yl) = x, y
    return dot(xh, yh) + (dot(xh, yl) + dot(xl, yh))


def pair(re, im):
    return jnp.concatenate([jnp.concatenate([re, im], 1), jnp.concatenate([-im, re], 1)], 0)


def refine(tr, ti, root):
    row = lax.broadcasted_iota(jnp.int32, (WIDE, WIDE), 0)
    col = lax.broadcasted_iota(jnp.int32, (WIDE, WIDE), 1)
    one = jnp.where(row == col, 1.0, 0.0)
    weight = jnp.where(col < row, 1.0, 0.5 * one)
    down = lax.rsqrt(jnp.sum(one * tr, axis=1, keepdims=True))
    across = lax.rsqrt(jnp.sum(one * tr, axis=0, keepdims=True))
    ar, ai = tr * down * across, ti * down * across
    unit = split(pair(ar, ai))
    root[:, :WIDE] = one - jnp.where(col < row, ar, 0.0)
    root[:, WIDE:] = -jnp.where(col < row, ai, 0.0)

    def cond(carry):
        step, size = carry
        return (step < 8) & (size > 1e-5) & (size < 1.0)

    def step(carry):
        count, _ = carry
        r = root[...]
        half = split_dot(split(r), unit)
        rt, it = jnp.transpose(r[:, :WIDE]), jnp.transpose(r[:, WIDE:])
        e = wide_dot(half, pair(rt, -it))
        er, ei = e[:, :WIDE] - one, e[:, WIDE:]
        size = jnp.sum(er * er + ei * ei)
        fix = jnp.concatenate([weight * er, weight * ei], 1)
        root[...] = r - wide_dot(fix, pair(r[:, :WIDE], r[:, WIDE:]))
        return count + 1, size

    count, size = lax.while_loop(cond, step, (jnp.int32(0), jnp.float32(0.5)))
    good = size <= 1e-5

    @pl.when(good)
    def _():
        root[:, :WIDE] = root[:, :WIDE] * across
        root[:, WIDE:] = root[:, WIDE:] * across

    @pl.when(jnp.logical_not(good))
    def _():
        re, im = inverse_factor(tr, ti)
        root[:, :WIDE] = re
        root[:, WIDE:] = im


def embed(block):
    return jnp.concatenate([block, times_i(block)], 0)


def finish_kernel(pos, g, w, p01, out, root):
    row = lax.broadcasted_iota(jnp.int32, (HALF, WIDE), 0)
    lane = lax.broadcasted_iota(jnp.int32, (HALF, WIDE), 1)
    left = lane < HALF
    col = jnp.where(left, lane, lane - HALF)
    c, g01 = g[0:HALF, :], g[HALF : 2 * HALF, :]
    c_turn, g01_turn = pltpu.roll(c, HALF, 1), pltpu.roll(g01, HALF, 1)
    above, below, diag = col > row, col < row, col == row

    def stack(top_left, top_right, low_right):
        return jnp.concatenate([jnp.where(left, top_left, top_right), jnp.where(left, 0.0, low_right)], 0)

    once_r = stack(jnp.where(above, c, 0.0), g01_turn, jnp.where(below, c_turn, 0.0))
    once_i = stack(jnp.where(above, c_turn, 0.0), g01, jnp.where(below, c, 0.0))
    pivots = jnp.where(diag, c, 0.0)
    tr = once_r + jnp.transpose(once_r) + stack(pivots, 0.0, pivots)
    ti = once_i - jnp.transpose(once_i)
    refine(tr, ti, root)
    rr, ri = root[:, :WIDE], root[:, WIDE:]
    which = pos[0]

    @pl.when(which >= 2)
    def _():
        m = g[2 * HALF : 4 * HALF, :]
        n = wide_dot(root[...], embed(m))
        k = wide_dot(jnp.concatenate([jnp.transpose(rr), -jnp.transpose(ri)], 1), embed(n))
        e_hi, e_lo = split(jnp.concatenate([embed(k[:HALF]), embed(k[HALF:])], 0))
        out[...] = w[...] - (dot(p01[...], e_hi) + dot(p01[...], e_lo))

    @pl.when(which < 2)
    def _():
        rt, it = jnp.transpose(rr), jnp.transpose(ri)
        full = lax.broadcasted_iota(jnp.int32, (WIDE, WIDE), 1) < HALF
        first = jnp.where(full, rt, -pltpu.roll(it, HALF, 1))
        second = jnp.where(full, pltpu.roll(rt, HALF, 1), -it)
        is_first = which == 0
        own = jnp.where(is_first, first[:HALF], second[HALF:])
        other = jnp.where(is_first, 0.0, second[:HALF])
        o_hi, o_lo = split(embed(other))
        p0 = p01[:, :WIDE]
        out[...] = dot(w[...], embed(own), precision=HIGHEST) + dot(p0, o_hi) + dot(p0, o_lo)


def finish(pos, g, w, p01):
    spec = pl.BlockSpec(memory_space=VM)
    return pl.pallas_call(
        finish_kernel,
        out_shape=jax.ShapeDtypeStruct(w.shape, F32),
        in_specs=[pl.BlockSpec(memory_space=SM), spec, spec, spec],
        out_specs=spec,
        scratch_shapes=[VM((WIDE, 2 * WIDE), F32)],
        compiler_params=pltpu.CompilerParams(vmem_limit_bytes=16 << 20),
        name="finish",
    )(pos, g, w, p01)


def swap(x, axes):
    return lax.all_to_all(x, axes, 0, 0, tiled=True)


def copies(x, count):
    return jnp.broadcast_to(x[None], (count,) + x.shape).reshape((count * x.shape[0],) + x.shape[1:])


def sum_pieces(x, count):
    return jnp.sum(x.reshape((count, -1) + x.shape[1:]), axis=0)


def slab_sum(x, inner, outer):
    near, far = lax.axis_size(inner), lax.axis_size(outer)
    piece = sum_pieces(swap(x, inner), near)
    piece = sum_pieces(swap(copies(piece, far), outer), far)
    return swap(copies(piece, near), inner)


def spread(w_hi, pos):
    far = lax.ppermute(w_hi, "panel", [(0, 3), (1, 6)])
    own = jnp.where((pos == 3) | (pos == 6), far, w_hi)
    return (own,) + tuple(lax.ppermute(own, "panel", pairs) for pairs in STEPS)


def thirds(x):
    a = lax.reduce_precision(x, 8, 7)
    b = lax.reduce_precision(x - a, 8, 7)
    return [a, b, x - a - b]


def body(vectors, hop_table, block_kind, block_phase, phase_angles, centre, half_width):
    slab = ("y", "x", "core")
    count = lax.axis_size(slab)
    kinds, phase = block_kind.T, block_phase[None, :]
    up, down = pack(vectors, kinds, phase)
    left = lax.ppermute(up, slab, [(i, i + 1) for i in range(count - 1)])
    right = lax.ppermute(down, slab, [(i + 1, i) for i in range(count - 1)])
    base = vectors / half_width[0]
    sides = jnp.concatenate([left, right], axis=0)
    wide = hop_table.astype(F32)
    turned = jnp.transpose(hop_table, (0, 2, 1))
    sym = ((wide + turned.astype(F32)) * 0.5).astype(BF16)
    parts = thirds(jnp.cos(phase_angles)) + thirds(jnp.sin(phase_angles))
    waves = jnp.concatenate(parts, axis=0).astype(BF16).T
    w, w_hi = chebyshev(
        kinds, phase, centre, half_width, base, sides, hop_table, turned, sym, waves
    )
    pos = lax.axis_index("panel").astype(jnp.int32)
    spot = pos.reshape(1)
    p01, part = gram(spot, w, spread(w_hi, pos))
    return finish(spot, slab_sum(part, ("x", "core"), "y"), w, p01)


def solution(mesh):
    panels = mesh.shape["panel"]
    devices = np.asarray(mesh.devices).reshape(8, 4, 2, panels)
    fine = Mesh(devices, ("y", "x", "core", "panel"))
    slab = ("y", "x", "core")
    in_specs = (P(slab, "panel"), P(), P(slab, None), P(slab), P(), P(), P())
    return jax.shard_map(body, mesh=fine, in_specs=in_specs, out_specs=P(slab, "panel"), check_vma=False)
```

```python
import functools

import jax
import jax.numpy as jnp
import numpy as np
from jax import lax
from jax.experimental import pallas as pl
from jax.experimental.pallas import tpu as pltpu
from jax.sharding import Mesh, PartitionSpec as P

HIGHEST = lax.Precision.HIGHEST
F32 = jnp.float32
BF16 = jnp.bfloat16
BLK = 256
WIDE = 128
HALF = 64
META = 16
MISSING = 8
STEPS = (
    [(0, 7), (1, 2), (5, 6), (4, 3)],
    [(0, 1), (1, 0), (5, 3), (4, 6)],
    [(0, 2), (1, 7), (5, 4), (4, 5)],
)
HELD = ((0, 2, 3, 2, 3, 0, 1, 1), (2, 0, 1, 1, 0, 3, 2, 3))
VM = pltpu.VMEM
SM = pltpu.SMEM


def lane_sign(first):
    lane = lax.broadcasted_iota(jnp.int32, (1, WIDE), 1)
    return jnp.where(lane < HALF, first, -first).astype(F32)


def times_i(packed):
    return lane_sign(-1.0) * pltpu.roll(packed, HALF, 1)


def dot(a, b, **kw):
    return lax.dot_general(a, b, (((1,), (0,)), ((), ())), preferred_element_type=F32, **kw)


def dot_t(a, b, **kw):
    return lax.dot_general(a, b, (((0,), (0,)), ((), ())), preferred_element_type=F32, **kw)


def split(x):
    hi = x.astype(BF16)
    return hi, (x - hi.astype(F32)).astype(BF16)


def pack_kernel(v, kinds, phase, up, down, tile):
    half = v.shape[0] // 2
    down[:half, :] = v[:half, :].astype(BF16)
    up[:half, :] = v[half:, :].astype(BF16)
    tile[...] = jnp.zeros(tile.shape, F32)
    tile[0:2, 0:4] = (kinds[...] - MISSING).astype(F32)
    tile[2:3, 0:4] = phase[...].astype(F32)
    tile[3:4, :] = jnp.ones((1, WIDE), F32)
    info = tile[...].astype(BF16)
    down[half:, :] = info
    up[half:, :] = info


def pack(v, kinds, phase):
    spec = pl.BlockSpec(memory_space=VM)
    shape = jax.ShapeDtypeStruct((v.shape[0] // 2 + META, WIDE), BF16)
    return pl.pallas_call(
        pack_kernel,
        out_shape=(shape, shape),
        in_specs=[spec] * 3,
        out_specs=(spec, spec),
        scratch_shapes=[VM((META, WIDE), F32)],
        name="pack",
    )(v, kinds, phase)


def filter_kernel(
    kinds, phase, shift, width, base, sides, hop, hop_t, sym, cos_t, sin_t,
    w, w_hi, vb, cosb, sinb, z, y1, y1b,
):
    half = base.shape[0] // 2
    left, right = sides.at[0 : half + META], sides.at[half + META :]
    centre = shift[0]
    h = jnp.broadcast_to(width[0], (1, WIDE))
    inv_h = 1.0 / h
    pick = lax.broadcasted_iota(jnp.int32, (cos_t.shape[1], WIDE), 0) % 16
    tile_l = left[half : half + META, :].astype(F32)
    tile_r = right[half : half + META, :].astype(F32)
    row = lax.broadcasted_iota(jnp.int32, (META, WIDE), 0)
    lane = lax.broadcasted_iota(jnp.int32, (META, WIDE), 1)

    def item(tile, i, j):
        return jnp.sum(jnp.where((row == i) & (lane == j), tile, 0.0)).astype(jnp.int32)

    own = {-1: item(tile_l, 0, 3) + MISSING, 4: item(tile_r, 0, 0) + MISSING}
    ahead_of = {r: item(tile_l, 1, 4 + r) + MISSING for r in (-2, -1)}
    ahead_of[4] = item(tile_r, 1, 0) + MISSING
    own.update({r: kinds[0, r] for r in range(4)})
    ahead_of.update({r: kinds[1, r] for r in range(4)})
    pattern = {r: tile_l[2:3, 4 + r : 5 + r].astype(jnp.int32) for r in (-2, -1)}
    pattern[4] = tile_r[2:3, 0:1].astype(jnp.int32)
    pattern.update({r: phase[0, r] for r in range(4)})
    has_left, has_right = tile_l[3:4, :], tile_r[3:4, :]

    def own_kind(r):
        return own[r]

    def next_kind(r):
        return ahead_of[r]

    def flag(kind):
        return jnp.where(kind < MISSING, 1.0, 0.0).astype(F32)

    for r in range(-2, 5):
        hot = jnp.where(pick == pattern[r], 1.0, 0.0).astype(BF16)
        cosb[r + 2] = dot(cos_t[...], hot)
        sinb[r + 2] = dot(sin_t[...], hot)

    def v_row(r):
        if r < 0:
            return left[(r + 2) * BLK : (r + 3) * BLK, :]
        if r > 3:
            return right[(r - 4) * BLK : (r - 3) * BLK, :]
        return vb[r * BLK : (r + 1) * BLK, :]

    def y_row(r):
        return y1b[r + 1]

    def back_phase(x, r):
        x = x.astype(F32)
        return (cosb[r + 2] * x - sinb[r + 2] * times_i(x)).astype(BF16)

    def hop_row(r, row):
        ko, kn, kb = own_kind(r), next_kind(r), next_kind(r - 1)
        total = flag(ko) * dot(sym[jnp.minimum(ko, 7)], row(r))
        ahead = flag(kn) * dot(hop[jnp.minimum(kn, 7)], row(r + 1))
        total += cosb[r + 2] * ahead + sinb[r + 2] * times_i(ahead)
        return total + flag(kb) * dot(hop_t[jnp.minimum(kb, 7)], z[r + 1])

    vb[...] = (h * base[...]).astype(BF16)
    for r in range(-2, 4):
        z[r + 2] = back_phase(v_row(r), r)
    for r in range(-1, 5):
        scaled = base[r * BLK : (r + 1) * BLK, :] if 0 <= r < 4 else v_row(r).astype(F32) * inv_h
        y = hop_row(r, v_row) * inv_h - centre * scaled
        if r == -1:
            y = y * has_left
        if r == 4:
            y = y * has_right
        if 0 <= r < 4:
            y1[r] = y
        y1b[r + 1] = y.astype(BF16)
    for r in range(-1, 4):
        z[r + 2] = back_phase(y_row(r), r)
    for r in range(4):
        y = (2.0 * inv_h) * (hop_row(r, y_row) - centre * y1[r]) - h * base[r * BLK : (r + 1) * BLK, :]
        w[r * BLK : (r + 1) * BLK, :] = y
        w_hi[r * BLK : (r + 1) * BLK, :] = y.astype(BF16)


def chebyshev(*args):
    spec = pl.BlockSpec(memory_space=VM)
    smem = pl.BlockSpec(memory_space=SM)
    return pl.pallas_call(
        filter_kernel,
        out_shape=(jax.ShapeDtypeStruct(args[4].shape, F32), jax.ShapeDtypeStruct(args[4].shape, BF16)),
        in_specs=[smem] * 4 + [spec] * 7,
        out_specs=(spec, spec),
        scratch_shapes=[
            VM(args[4].shape, BF16),
            VM((7, BLK, WIDE), F32),
            VM((7, BLK, WIDE), F32),
            VM((6, BLK, WIDE), BF16),
            VM((4, BLK, WIDE), F32),
            VM((6, BLK, WIDE), BF16),
        ],
        compiler_params=pltpu.CompilerParams(vmem_limit_bytes=16 << 20),
        name="chebyshev",
    )(*args)


def gram_kernel(pos, w, own, first, second, third, p01, out):
    which = pos[0]
    for src, ref in enumerate((own, first, second, third)):
        for panel in range(2):
            here = [z for z in range(8) if HELD[panel][z] == src]
            hit = functools.reduce(jnp.logical_or, [which == z for z in here])

            @pl.when(hit)
            def _(ref=ref, panel=panel):
                p01[:, panel * WIDE : (panel + 1) * WIDE] = ref[...]

    both = p01[...]
    w_hi, w_lo = split(w[...])
    prod = dot_t(both, jnp.concatenate([both, w_hi, w_lo], 1))

    def inner(a, b):
        d = prod[a * WIDE : (a + 1) * WIDE, b * WIDE : (b + 1) * WIDE]
        return d[:HALF] + lane_sign(1.0) * pltpu.roll(d[HALF:], HALF, 1)

    row = lax.broadcasted_iota(jnp.int32, (HALF, WIDE), 0)
    lane = lax.broadcasted_iota(jnp.int32, (HALF, WIDE), 1)
    col = jnp.where(lane < HALF, lane, lane - HALF)
    g00, g11 = inner(0, 0), inner(1, 1)
    diag = jnp.where(lane < HALF, g00, pltpu.roll(g11, HALF, 1))
    out[0:HALF, :] = jnp.where(col > row, g00, jnp.where(col < row, g11, diag))
    out[HALF : 2 * HALF, :] = inner(0, 1)
    out[2 * HALF : 3 * HALF, :] = inner(0, 2) + inner(0, 3)
    out[3 * HALF : 4 * HALF, :] = inner(1, 2) + inner(1, 3)


def gram(pos, w, parts):
    spec = pl.BlockSpec(memory_space=VM)
    return pl.pallas_call(
        gram_kernel,
        out_shape=(
            jax.ShapeDtypeStruct((w.shape[0], 2 * WIDE), BF16),
            jax.ShapeDtypeStruct((4 * HALF, WIDE), F32),
        ),
        in_specs=[pl.BlockSpec(memory_space=SM)] + [spec] * 5,
        out_specs=(spec, spec),
        compiler_params=pltpu.CompilerParams(vmem_limit_bytes=16 << 20),
        name="gram",
    )(pos, w, *parts)


def inverse_factor(tr, ti):
    tiles = WIDE // 8
    re = [tr[8 * t : 8 * t + 8] for t in range(tiles)]
    im = [ti[8 * t : 8 * t + 8] for t in range(tiles)]
    lane = lax.broadcasted_iota(jnp.int32, (8, WIDE), 1)
    sub = lax.broadcasted_iota(jnp.int32, (8, WIDE), 0)
    for k in range(WIDE):
        g, j = divmod(k, 8)
        at_k = lane == k
        row_r = re[g][j : j + 1]
        row_i = im[g][j : j + 1]
        inv = 1.0 / jnp.broadcast_to(row_r[:, k : k + 1], (1, WIDE))
        row_r = jnp.where(at_k[:1], 1.0, row_r) * inv
        row_i = jnp.where(at_k[:1], 0.0, row_i) * inv
        row_r = jnp.broadcast_to(row_r, (8, WIDE))
        row_i = jnp.broadcast_to(row_i, (8, WIDE))
        for t in range(g, tiles):
            if t == g and j == 7:
                continue
            cr = jnp.broadcast_to(re[t][:, k : k + 1], (8, WIDE))
            ci = jnp.broadcast_to(im[t][:, k : k + 1], (8, WIDE))
            keep_r = jnp.where(at_k, 0.0, re[t])
            keep_i = jnp.where(at_k, 0.0, im[t])
            new_r = keep_r - (cr * row_r - ci * row_i)
            new_i = keep_i - (cr * row_i + ci * row_r)
            if t == g:
                new_r = jnp.where(sub > j, new_r, re[t])
                new_i = jnp.where(sub > j, new_i, im[t])
            re[t], im[t] = new_r, new_i
    out_r, out_i = [], []
    for t in range(tiles):
        diag = lane == sub + 8 * t
        below = lane < sub + 8 * t
        pivot = jnp.sum(jnp.where(diag, re[t], 0.0), axis=1, keepdims=True)
        scale = lax.rsqrt(pivot)
        out_r.append(jnp.where(diag, 1.0, jnp.where(below, re[t], 0.0)) * scale)
        out_i.append(jnp.where(below, im[t], 0.0) * scale)
    return jnp.concatenate(out_r, 0), jnp.concatenate(out_i, 0)


def wide_dot(x, y):
    return split_dot(split(x), split(y))


def split_dot(x, y):
    (xh, xl), (yh, yl) = x, y
    return dot(xh, yh) + (dot(xh, yl) + dot(xl, yh))


def pair(re, im):
    return jnp.concatenate([jnp.concatenate([re, im], 1), jnp.concatenate([-im, re], 1)], 0)


def refine(tr, ti, root):
    row = lax.broadcasted_iota(jnp.int32, (WIDE, WIDE), 0)
    col = lax.broadcasted_iota(jnp.int32, (WIDE, WIDE), 1)
    one = jnp.where(row == col, 1.0, 0.0)
    weight = jnp.where(col < row, 1.0, 0.5 * one)
    down = lax.rsqrt(jnp.sum(one * tr, axis=1, keepdims=True))
    across = lax.rsqrt(jnp.sum(one * tr, axis=0, keepdims=True))
    ar, ai = tr * down * across, ti * down * across
    unit = split(pair(ar, ai))
    root[:, :WIDE] = one - jnp.where(col < row, ar, 0.0)
    root[:, WIDE:] = -jnp.where(col < row, ai, 0.0)

    def cond(carry):
        step, size = carry
        return (step < 8) & (size > 1e-5) & (size < 1.0)

    def step(carry):
        count, _ = carry
        r = root[...]
        half = split_dot(split(r), unit)
        rt, it = jnp.transpose(r[:, :WIDE]), jnp.transpose(r[:, WIDE:])
        e = wide_dot(half, pair(rt, -it))
        er, ei = e[:, :WIDE] - one, e[:, WIDE:]
        size = jnp.sum(er * er + ei * ei)
        fix = jnp.concatenate([weight * er, weight * ei], 1)
        root[...] = r - wide_dot(fix, pair(r[:, :WIDE], r[:, WIDE:]))
        return count + 1, size

    count, size = lax.while_loop(cond, step, (jnp.int32(0), jnp.float32(0.5)))
    good = size <= 1e-5

    @pl.when(good)
    def _():
        root[:, :WIDE] = root[:, :WIDE] * across
        root[:, WIDE:] = root[:, WIDE:] * across

    @pl.when(jnp.logical_not(good))
    def _():
        re, im = inverse_factor(tr, ti)
        root[:, :WIDE] = re
        root[:, WIDE:] = im


def embed(block):
    return jnp.concatenate([block, times_i(block)], 0)


def finish_kernel(pos, g, w, p01, out, root):
    row = lax.broadcasted_iota(jnp.int32, (HALF, WIDE), 0)
    lane = lax.broadcasted_iota(jnp.int32, (HALF, WIDE), 1)
    left = lane < HALF
    col = jnp.where(left, lane, lane - HALF)
    c, g01 = g[0:HALF, :], g[HALF : 2 * HALF, :]
    c_turn, g01_turn = pltpu.roll(c, HALF, 1), pltpu.roll(g01, HALF, 1)
    above, below, diag = col > row, col < row, col == row

    def stack(top_left, top_right, low_right):
        return jnp.concatenate([jnp.where(left, top_left, top_right), jnp.where(left, 0.0, low_right)], 0)

    once_r = stack(jnp.where(above, c, 0.0), g01_turn, jnp.where(below, c_turn, 0.0))
    once_i = stack(jnp.where(above, c_turn, 0.0), g01, jnp.where(below, c, 0.0))
    pivots = jnp.where(diag, c, 0.0)
    tr = once_r + jnp.transpose(once_r) + stack(pivots, 0.0, pivots)
    ti = once_i - jnp.transpose(once_i)
    refine(tr, ti, root)
    rr, ri = root[:, :WIDE], root[:, WIDE:]
    which = pos[0]

    @pl.when(which >= 2)
    def _():
        m = g[2 * HALF : 4 * HALF, :]
        n = wide_dot(root[...], embed(m))
        k = wide_dot(jnp.concatenate([jnp.transpose(rr), -jnp.transpose(ri)], 1), embed(n))
        e_hi, e_lo = split(jnp.concatenate([embed(k[:HALF]), embed(k[HALF:])], 0))
        out[...] = w[...] - (dot(p01[...], e_hi) + dot(p01[...], e_lo))

    @pl.when(which < 2)
    def _():
        rt, it = jnp.transpose(rr), jnp.transpose(ri)
        full = lax.broadcasted_iota(jnp.int32, (WIDE, WIDE), 1) < HALF
        first = jnp.where(full, rt, -pltpu.roll(it, HALF, 1))
        second = jnp.where(full, pltpu.roll(rt, HALF, 1), -it)
        is_first = which == 0
        own = jnp.where(is_first, first[:HALF], second[HALF:])
        other = jnp.where(is_first, 0.0, second[:HALF])
        o_hi, o_lo = split(embed(other))
        p0 = p01[:, :WIDE]
        out[...] = dot(w[...], embed(own), precision=HIGHEST) + dot(p0, o_hi) + dot(p0, o_lo)


def finish(pos, g, w, p01):
    spec = pl.BlockSpec(memory_space=VM)
    return pl.pallas_call(
        finish_kernel,
        out_shape=jax.ShapeDtypeStruct(w.shape, F32),
        in_specs=[pl.BlockSpec(memory_space=SM), spec, spec, spec],
        out_specs=spec,
        scratch_shapes=[VM((WIDE, 2 * WIDE), F32)],
        compiler_params=pltpu.CompilerParams(vmem_limit_bytes=16 << 20),
        name="finish",
    )(pos, g, w, p01)


def swap(x, axes):
    return lax.all_to_all(x, axes, 0, 0, tiled=True)


def copies(x, count):
    return jnp.broadcast_to(x[None], (count,) + x.shape).reshape((count * x.shape[0],) + x.shape[1:])


def sum_pieces(x, count):
    return jnp.sum(x.reshape((count, -1) + x.shape[1:]), axis=0)


def slab_sum(x, inner, outer):
    near, far = lax.axis_size(inner), lax.axis_size(outer)
    piece = sum_pieces(swap(x, inner), near)
    piece = sum_pieces(swap(copies(piece, far), outer), far)
    return swap(copies(piece, near), inner)


def spread(w_hi, pos):
    far = lax.ppermute(w_hi, "panel", [(0, 5), (1, 4)])
    own = jnp.where((pos == 5) | (pos == 4), far, w_hi)
    return (own,) + tuple(lax.ppermute(own, "panel", pairs) for pairs in STEPS)


def thirds(x):
    a = lax.reduce_precision(x, 8, 7)
    b = lax.reduce_precision(x - a, 8, 7)
    return jnp.concatenate([a, b, x - a - b], axis=0).astype(BF16).T


def body(vectors, hop_table, block_kind, block_phase, phase_angles, centre, half_width):
    slab = ("y", "x", "core")
    count = lax.axis_size(slab)
    kinds, phase = block_kind.T, block_phase[None, :]
    up, down = pack(vectors, kinds, phase)
    left = lax.ppermute(up, slab, [(i, i + 1) for i in range(count - 1)])
    right = lax.ppermute(down, slab, [(i + 1, i) for i in range(count - 1)])
    base = vectors / half_width[0]
    sides = jnp.concatenate([left, right], axis=0)
    wide = hop_table.astype(F32)
    turned = jnp.transpose(hop_table, (0, 2, 1))
    sym = ((wide + turned.astype(F32)) * 0.5).astype(BF16)
    cos_t = thirds(jnp.cos(phase_angles))
    sin_t = thirds(jnp.sin(phase_angles))
    w, w_hi = chebyshev(
        kinds, phase, centre, half_width, base, sides, hop_table, turned, sym, cos_t, sin_t
    )
    pos = lax.axis_index("panel").astype(jnp.int32)
    spot = pos.reshape(1)
    p01, part = gram(spot, w, spread(w_hi, pos))
    return finish(spot, slab_sum(part, ("x", "core"), "y"), w, p01)


def solution(mesh):
    panels = mesh.shape["panel"]
    devices = np.asarray(mesh.devices).reshape(8, 4, 2, panels)
    fine = Mesh(devices, ("y", "x", "core", "panel"))
    slab = ("y", "x", "core")
    in_specs = (P(slab, "panel"), P(), P(slab, None), P(slab), P(), P(), P())
    return jax.shard_map(body, mesh=fine, in_specs=in_specs, out_specs=P(slab, "panel"), check_vma=False)
```

```python
import functools

import jax
import jax.numpy as jnp
import numpy as np
from jax import lax
from jax.experimental import pallas as pl
from jax.experimental.pallas import tpu as pltpu
from jax.sharding import Mesh, PartitionSpec as P

HIGHEST = lax.Precision.HIGHEST
F32 = jnp.float32
BF16 = jnp.bfloat16
BLK = 256
WIDE = 128
HALF = 64
META = 16
MISSING = 8
STEPS = (
    [(0, 7), (1, 2), (5, 6), (4, 3)],
    [(0, 2), (1, 7), (5, 4), (4, 5)],
    [(0, 1), (1, 0), (5, 3), (4, 6)],
)
HELD = ((0, 3, 2, 3, 2, 0, 1, 1), (3, 0, 1, 1, 0, 2, 3, 2))
VM = pltpu.VMEM
SM = pltpu.SMEM


def lane_sign(first):
    lane = lax.broadcasted_iota(jnp.int32, (1, WIDE), 1)
    return jnp.where(lane < HALF, first, -first).astype(F32)


def times_i(packed):
    return lane_sign(-1.0) * pltpu.roll(packed, HALF, 1)


def dot(a, b, **kw):
    return lax.dot_general(a, b, (((1,), (0,)), ((), ())), preferred_element_type=F32, **kw)


def dot_t(a, b, **kw):
    return lax.dot_general(a, b, (((0,), (0,)), ((), ())), preferred_element_type=F32, **kw)


def split(x):
    hi = x.astype(BF16)
    return hi, (x - hi.astype(F32)).astype(BF16)


def pack_kernel(v, kinds, phase, up, down, tile):
    half = v.shape[0] // 2
    down[:half, :] = v[:half, :].astype(BF16)
    up[:half, :] = v[half:, :].astype(BF16)
    tile[...] = jnp.zeros(tile.shape, F32)
    tile[0:2, 0:4] = (kinds[...] - MISSING).astype(F32)
    tile[2:3, 0:4] = phase[...].astype(F32)
    tile[3:4, :] = jnp.ones((1, WIDE), F32)
    info = tile[...].astype(BF16)
    down[half:, :] = info
    up[half:, :] = info


def pack(v, kinds, phase):
    spec = pl.BlockSpec(memory_space=VM)
    shape = jax.ShapeDtypeStruct((v.shape[0] // 2 + META, WIDE), BF16)
    return pl.pallas_call(
        pack_kernel,
        out_shape=(shape, shape),
        in_specs=[spec] * 3,
        out_specs=(spec, spec),
        scratch_shapes=[VM((META, WIDE), F32)],
        name="pack",
    )(v, kinds, phase)


def filter_kernel(
    kinds, phase, shift, width, base, sides, hop, hop_t, sym, cos_t, sin_t,
    w, w_hi, vb, cosb, sinb, z, y1, y1b,
):
    half = base.shape[0] // 2
    left, right = sides.at[0 : half + META], sides.at[half + META :]
    centre = shift[0]
    h = jnp.broadcast_to(width[0], (1, WIDE))
    inv_h = 1.0 / h
    pick = lax.broadcasted_iota(jnp.int32, (cos_t.shape[1], WIDE), 0) % 16
    tile_l = left[half : half + META, :].astype(F32)
    tile_r = right[half : half + META, :].astype(F32)
    row = lax.broadcasted_iota(jnp.int32, (META, WIDE), 0)
    lane = lax.broadcasted_iota(jnp.int32, (META, WIDE), 1)

    def item(tile, i, j):
        return jnp.sum(jnp.where((row == i) & (lane == j), tile, 0.0)).astype(jnp.int32)

    own = {-1: item(tile_l, 0, 3) + MISSING, 4: item(tile_r, 0, 0) + MISSING}
    ahead_of = {r: item(tile_l, 1, 4 + r) + MISSING for r in (-2, -1)}
    ahead_of[4] = item(tile_r, 1, 0) + MISSING
    own.update({r: kinds[0, r] for r in range(4)})
    ahead_of.update({r: kinds[1, r] for r in range(4)})
    pattern = {r: tile_l[2:3, 4 + r : 5 + r].astype(jnp.int32) for r in (-2, -1)}
    pattern[4] = tile_r[2:3, 0:1].astype(jnp.int32)
    pattern.update({r: phase[0, r] for r in range(4)})
    has_left, has_right = tile_l[3:4, :], tile_r[3:4, :]

    def own_kind(r):
        return own[r]

    def next_kind(r):
        return ahead_of[r]

    def flag(kind):
        return jnp.where(kind < MISSING, 1.0, 0.0).astype(F32)

    for r in range(-2, 5):
        hot = jnp.where(pick == pattern[r], 1.0, 0.0).astype(BF16)
        cosb[r + 2] = dot(cos_t[...], hot)
        sinb[r + 2] = dot(sin_t[...], hot)

    def v_row(r):
        if r < 0:
            return left[(r + 2) * BLK : (r + 3) * BLK, :]
        if r > 3:
            return right[(r - 4) * BLK : (r - 3) * BLK, :]
        return vb[r * BLK : (r + 1) * BLK, :]

    def y_row(r):
        return y1b[r + 1]

    def back_phase(x, r):
        x = x.astype(F32)
        return (cosb[r + 2] * x - sinb[r + 2] * times_i(x)).astype(BF16)

    def hop_row(r, row):
        ko, kn, kb = own_kind(r), next_kind(r), next_kind(r - 1)
        total = flag(ko) * dot(sym[jnp.minimum(ko, 7)], row(r))
        ahead = flag(kn) * dot(hop[jnp.minimum(kn, 7)], row(r + 1))
        total += cosb[r + 2] * ahead + sinb[r + 2] * times_i(ahead)
        return total + flag(kb) * dot(hop_t[jnp.minimum(kb, 7)], z[r + 1])

    vb[...] = (h * base[...]).astype(BF16)
    for r in range(-2, 4):
        z[r + 2] = back_phase(v_row(r), r)
    for r in range(-1, 5):
        scaled = base[r * BLK : (r + 1) * BLK, :] if 0 <= r < 4 else v_row(r).astype(F32) * inv_h
        y = hop_row(r, v_row) * inv_h - centre * scaled
        if r == -1:
            y = y * has_left
        if r == 4:
            y = y * has_right
        if 0 <= r < 4:
            y1[r] = y
        y1b[r + 1] = y.astype(BF16)
    for r in range(-1, 4):
        z[r + 2] = back_phase(y_row(r), r)
    for r in range(4):
        y = (2.0 * inv_h) * (hop_row(r, y_row) - centre * y1[r]) - h * base[r * BLK : (r + 1) * BLK, :]
        w[r * BLK : (r + 1) * BLK, :] = y
        w_hi[r * BLK : (r + 1) * BLK, :] = y.astype(BF16)


def chebyshev(*args):
    spec = pl.BlockSpec(memory_space=VM)
    smem = pl.BlockSpec(memory_space=SM)
    return pl.pallas_call(
        filter_kernel,
        out_shape=(jax.ShapeDtypeStruct(args[4].shape, F32), jax.ShapeDtypeStruct(args[4].shape, BF16)),
        in_specs=[smem] * 4 + [spec] * 7,
        out_specs=(spec, spec),
        scratch_shapes=[
            VM(args[4].shape, BF16),
            VM((7, BLK, WIDE), F32),
            VM((7, BLK, WIDE), F32),
            VM((6, BLK, WIDE), BF16),
            VM((4, BLK, WIDE), F32),
            VM((6, BLK, WIDE), BF16),
        ],
        compiler_params=pltpu.CompilerParams(vmem_limit_bytes=16 << 20),
        name="chebyshev",
    )(*args)


def gram_kernel(pos, w, own, first, second, third, p01, out):
    which = pos[0]
    for src, ref in enumerate((own, first, second, third)):
        for panel in range(2):
            here = [z for z in range(8) if HELD[panel][z] == src]
            hit = functools.reduce(jnp.logical_or, [which == z for z in here])

            @pl.when(hit)
            def _(ref=ref, panel=panel):
                p01[:, panel * WIDE : (panel + 1) * WIDE] = ref[...]

    both = p01[...]
    w_hi, w_lo = split(w[...])
    prod = dot_t(both, jnp.concatenate([both, w_hi, w_lo], 1))

    def inner(a, b):
        d = prod[a * WIDE : (a + 1) * WIDE, b * WIDE : (b + 1) * WIDE]
        return d[:HALF] + lane_sign(1.0) * pltpu.roll(d[HALF:], HALF, 1)

    row = lax.broadcasted_iota(jnp.int32, (HALF, WIDE), 0)
    lane = lax.broadcasted_iota(jnp.int32, (HALF, WIDE), 1)
    col = jnp.where(lane < HALF, lane, lane - HALF)
    g00, g11 = inner(0, 0), inner(1, 1)
    diag = jnp.where(lane < HALF, g00, pltpu.roll(g11, HALF, 1))
    out[0:HALF, :] = jnp.where(col > row, g00, jnp.where(col < row, g11, diag))
    out[HALF : 2 * HALF, :] = inner(0, 1)
    out[2 * HALF : 3 * HALF, :] = inner(0, 2) + inner(0, 3)
    out[3 * HALF : 4 * HALF, :] = inner(1, 2) + inner(1, 3)


def gram(pos, w, parts):
    spec = pl.BlockSpec(memory_space=VM)
    return pl.pallas_call(
        gram_kernel,
        out_shape=(
            jax.ShapeDtypeStruct((w.shape[0], 2 * WIDE), BF16),
            jax.ShapeDtypeStruct((4 * HALF, WIDE), F32),
        ),
        in_specs=[pl.BlockSpec(memory_space=SM)] + [spec] * 5,
        out_specs=(spec, spec),
        compiler_params=pltpu.CompilerParams(vmem_limit_bytes=16 << 20),
        name="gram",
    )(pos, w, *parts)


def inverse_factor(tr, ti):
    tiles = WIDE // 8
    re = [tr[8 * t : 8 * t + 8] for t in range(tiles)]
    im = [ti[8 * t : 8 * t + 8] for t in range(tiles)]
    lane = lax.broadcasted_iota(jnp.int32, (8, WIDE), 1)
    sub = lax.broadcasted_iota(jnp.int32, (8, WIDE), 0)
    for k in range(WIDE):
        g, j = divmod(k, 8)
        at_k = lane == k
        row_r = re[g][j : j + 1]
        row_i = im[g][j : j + 1]
        inv = 1.0 / jnp.broadcast_to(row_r[:, k : k + 1], (1, WIDE))
        row_r = jnp.where(at_k[:1], 1.0, row_r) * inv
        row_i = jnp.where(at_k[:1], 0.0, row_i) * inv
        row_r = jnp.broadcast_to(row_r, (8, WIDE))
        row_i = jnp.broadcast_to(row_i, (8, WIDE))
        for t in range(g, tiles):
            if t == g and j == 7:
                continue
            cr = jnp.broadcast_to(re[t][:, k : k + 1], (8, WIDE))
            ci = jnp.broadcast_to(im[t][:, k : k + 1], (8, WIDE))
            keep_r = jnp.where(at_k, 0.0, re[t])
            keep_i = jnp.where(at_k, 0.0, im[t])
            new_r = keep_r - (cr * row_r - ci * row_i)
            new_i = keep_i - (cr * row_i + ci * row_r)
            if t == g:
                new_r = jnp.where(sub > j, new_r, re[t])
                new_i = jnp.where(sub > j, new_i, im[t])
            re[t], im[t] = new_r, new_i
    out_r, out_i = [], []
    for t in range(tiles):
        diag = lane == sub + 8 * t
        below = lane < sub + 8 * t
        pivot = jnp.sum(jnp.where(diag, re[t], 0.0), axis=1, keepdims=True)
        scale = lax.rsqrt(pivot)
        out_r.append(jnp.where(diag, 1.0, jnp.where(below, re[t], 0.0)) * scale)
        out_i.append(jnp.where(below, im[t], 0.0) * scale)
    return jnp.concatenate(out_r, 0), jnp.concatenate(out_i, 0)


def wide_dot(x, y):
    return split_dot(split(x), split(y))


def split_dot(x, y):
    (xh, xl), (yh, yl) = x, y
    return dot(xh, yh) + (dot(xh, yl) + dot(xl, yh))


def pair(re, im):
    return jnp.concatenate([jnp.concatenate([re, im], 1), jnp.concatenate([-im, re], 1)], 0)


def refine(tr, ti, root):
    row = lax.broadcasted_iota(jnp.int32, (WIDE, WIDE), 0)
    col = lax.broadcasted_iota(jnp.int32, (WIDE, WIDE), 1)
    one = jnp.where(row == col, 1.0, 0.0)
    weight = jnp.where(col < row, 1.0, 0.5 * one)
    down = lax.rsqrt(jnp.sum(one * tr, axis=1, keepdims=True))
    across = lax.rsqrt(jnp.sum(one * tr, axis=0, keepdims=True))
    ar, ai = tr * down * across, ti * down * across
    unit = split(pair(ar, ai))
    root[:, :WIDE] = one - jnp.where(col < row, ar, 0.0)
    root[:, WIDE:] = -jnp.where(col < row, ai, 0.0)

    def cond(carry):
        step, size = carry
        return (step < 8) & (size > 1e-5) & (size < 1.0)

    def step(carry):
        count, _ = carry
        r = root[...]
        half = split_dot(split(r), unit)
        rt, it = jnp.transpose(r[:, :WIDE]), jnp.transpose(r[:, WIDE:])
        e = wide_dot(half, pair(rt, -it))
        er, ei = e[:, :WIDE] - one, e[:, WIDE:]
        size = jnp.sum(er * er + ei * ei)
        fix = jnp.concatenate([weight * er, weight * ei], 1)
        root[...] = r - wide_dot(fix, pair(r[:, :WIDE], r[:, WIDE:]))
        return count + 1, size

    count, size = lax.while_loop(cond, step, (jnp.int32(0), jnp.float32(0.5)))
    good = size <= 1e-5

    @pl.when(good)
    def _():
        root[:, :WIDE] = root[:, :WIDE] * across
        root[:, WIDE:] = root[:, WIDE:] * across

    @pl.when(jnp.logical_not(good))
    def _():
        re, im = inverse_factor(tr, ti)
        root[:, :WIDE] = re
        root[:, WIDE:] = im


def embed(block):
    return jnp.concatenate([block, times_i(block)], 0)


def finish_kernel(pos, g, w, p01, out, root):
    row = lax.broadcasted_iota(jnp.int32, (HALF, WIDE), 0)
    lane = lax.broadcasted_iota(jnp.int32, (HALF, WIDE), 1)
    left = lane < HALF
    col = jnp.where(left, lane, lane - HALF)
    c, g01 = g[0:HALF, :], g[HALF : 2 * HALF, :]
    c_turn, g01_turn = pltpu.roll(c, HALF, 1), pltpu.roll(g01, HALF, 1)
    above, below, diag = col > row, col < row, col == row

    def stack(top_left, top_right, low_right):
        return jnp.concatenate([jnp.where(left, top_left, top_right), jnp.where(left, 0.0, low_right)], 0)

    once_r = stack(jnp.where(above, c, 0.0), g01_turn, jnp.where(below, c_turn, 0.0))
    once_i = stack(jnp.where(above, c_turn, 0.0), g01, jnp.where(below, c, 0.0))
    pivots = jnp.where(diag, c, 0.0)
    tr = once_r + jnp.transpose(once_r) + stack(pivots, 0.0, pivots)
    ti = once_i - jnp.transpose(once_i)
    refine(tr, ti, root)
    rr, ri = root[:, :WIDE], root[:, WIDE:]
    which = pos[0]

    @pl.when(which >= 2)
    def _():
        m = g[2 * HALF : 4 * HALF, :]
        n = wide_dot(root[...], embed(m))
        k = wide_dot(jnp.concatenate([jnp.transpose(rr), -jnp.transpose(ri)], 1), embed(n))
        e_hi, e_lo = split(jnp.concatenate([embed(k[:HALF]), embed(k[HALF:])], 0))
        out[...] = w[...] - (dot(p01[...], e_hi) + dot(p01[...], e_lo))

    @pl.when(which < 2)
    def _():
        rt, it = jnp.transpose(rr), jnp.transpose(ri)
        full = lax.broadcasted_iota(jnp.int32, (WIDE, WIDE), 1) < HALF
        first = jnp.where(full, rt, -pltpu.roll(it, HALF, 1))
        second = jnp.where(full, pltpu.roll(rt, HALF, 1), -it)
        is_first = which == 0
        own = jnp.where(is_first, first[:HALF], second[HALF:])
        other = jnp.where(is_first, 0.0, second[:HALF])
        o_hi, o_lo = split(embed(other))
        p0 = p01[:, :WIDE]
        out[...] = dot(w[...], embed(own), precision=HIGHEST) + dot(p0, o_hi) + dot(p0, o_lo)


def finish(pos, g, w, p01):
    spec = pl.BlockSpec(memory_space=VM)
    return pl.pallas_call(
        finish_kernel,
        out_shape=jax.ShapeDtypeStruct(w.shape, F32),
        in_specs=[pl.BlockSpec(memory_space=SM), spec, spec, spec],
        out_specs=spec,
        scratch_shapes=[VM((WIDE, 2 * WIDE), F32)],
        compiler_params=pltpu.CompilerParams(vmem_limit_bytes=16 << 20),
        name="finish",
    )(pos, g, w, p01)


def swap(x, axes):
    return lax.all_to_all(x, axes, 0, 0, tiled=True)


def copies(x, count):
    return jnp.broadcast_to(x[None], (count,) + x.shape).reshape((count * x.shape[0],) + x.shape[1:])


def sum_pieces(x, count):
    return jnp.sum(x.reshape((count, -1) + x.shape[1:]), axis=0)


def slab_sum(x, inner, outer):
    near, far = lax.axis_size(inner), lax.axis_size(outer)
    piece = sum_pieces(swap(x, inner), near)
    piece = sum_pieces(swap(copies(piece, far), outer), far)
    return swap(copies(piece, near), inner)


def spread(w_hi, pos):
    far = lax.ppermute(w_hi, "panel", [(0, 5), (1, 4)])
    own = jnp.where((pos == 5) | (pos == 4), far, w_hi)
    return (own,) + tuple(lax.ppermute(own, "panel", pairs) for pairs in STEPS)


def thirds(x):
    a = lax.reduce_precision(x, 8, 7)
    b = lax.reduce_precision(x - a, 8, 7)
    return jnp.concatenate([a, b, x - a - b], axis=0).astype(BF16).T


def body(vectors, hop_table, block_kind, block_phase, phase_angles, centre, half_width):
    slab = ("y", "x", "core")
    count = lax.axis_size(slab)
    kinds, phase = block_kind.T, block_phase[None, :]
    up, down = pack(vectors, kinds, phase)
    left = lax.ppermute(up, slab, [(i, i + 1) for i in range(count - 1)])
    right = lax.ppermute(down, slab, [(i + 1, i) for i in range(count - 1)])
    base = vectors / half_width[0]
    sides = jnp.concatenate([left, right], axis=0)
    wide = hop_table.astype(F32)
    turned = jnp.transpose(hop_table, (0, 2, 1))
    sym = ((wide + turned.astype(F32)) * 0.5).astype(BF16)
    cos_t = thirds(jnp.cos(phase_angles))
    sin_t = thirds(jnp.sin(phase_angles))
    w, w_hi = chebyshev(
        kinds, phase, centre, half_width, base, sides, hop_table, turned, sym, cos_t, sin_t
    )
    pos = lax.axis_index("panel").astype(jnp.int32)
    spot = pos.reshape(1)
    p01, part = gram(spot, w, spread(w_hi, pos))
    return finish(spot, slab_sum(part, ("x", "core"), "y"), w, p01)


def solution(mesh):
    panels = mesh.shape["panel"]
    devices = np.asarray(mesh.devices).reshape(8, 4, 2, panels)
    fine = Mesh(devices, ("y", "x", "core", "panel"))
    slab = ("y", "x", "core")
    in_specs = (P(slab, "panel"), P(), P(slab, None), P(slab), P(), P(), P())
    return jax.shard_map(body, mesh=fine, in_specs=in_specs, out_specs=P(slab, "panel"), check_vma=False)
```
